32 devices in a mesh: rows: 8 (over y, x, core), cols: 4 (over z).
Axes of the slice: x: 2, y: 2, z: 4, core: 2. Of those that a mesh axis runs over, the one named last changes fastest.
Arguments:
- features: bfloat16 [64, 256, 256], P('rows', 'cols'), may hold values from -6 to 6
- crop_ids: int32 [64, 256], P(None, 'cols'), may hold values from 0 to 1023, as said below
- conditioning: bfloat16 [2, 768], replicated, may hold values from -6 to 6
- qkv_weight: bfloat16 [256, 768], P(('rows', 'cols')), may hold values from -0.375 to 0.375
- out_weight: bfloat16 [256, 256], P(('rows', 'cols')), may hold values from -1.5 to 1.5
- up_weight: bfloat16 [256, 1536], P(('rows', 'cols')), may hold values from -0.375 to 0.375
- down_weight: bfloat16 [768, 256], P(('rows', 'cols')), may hold values from -0.21875 to 0.21875
- attn_cond_weight: bfloat16 [768, 256], P(('rows', 'cols')), may hold values from -0.109375 to 0.109375
- feed_cond_weight: bfloat16 [768, 256], P(('rows', 'cols')), may hold values from -0.109375 to 0.109375
- attention_scale: float32 [4], replicated, may hold values from 6 to 20
- cotangent: bfloat16 [64, 256, 256], P('rows', 'cols'), may hold values from -6 to 6
Outputs:
- output: bfloat16 [64, 256, 256], P('rows', 'cols')
- grad_features: float32 [64, 256, 256], P('rows', 'cols')
- grad_qkv: float32 [256, 768], P(('rows', 'cols'))
- grad_out: float32 [256, 256], P(('rows', 'cols'))
- grad_up: float32 [256, 1536], P(('rows', 'cols'))
- grad_down: float32 [768, 256], P(('rows', 'cols'))
- grad_attn_cond: float32 [768, 256], P(('rows', 'cols'))
- grad_feed_cond: float32 [768, 256], P(('rows', 'cols'))
- grad_scale: float32 [4], replicated
The draws below stay inside these ranges and needn't reach their ends.
Inputs may be any that keep to these rules, and one draw needn't show every extreme that they name: `crop_ids`: every crop is a run of whole rows inside one band of 16 columns (columns 16 * b to 16 * b + 15 of the array); different crops have different ids, ids of band b lie in b * 64 to b * 64 + 63 and its last crop has b * 64 + 63, and within a band the ids do not fall from row to row.
All inputs are finite; a program needn't handle non-finite values.
Results may differ from the reference program's by a relative error of at most 0.02.
Values may be sent and summed in bfloat16 or wider, within the bound.
No kernel may reach another device: no remote copies, remote signals or barrier semaphores. Data moves between devices by JAX's collectives and lax.ppermute only.
A program may use at most 256 MiB of HBM per device.

```python
import math
import jax
import jax.numpy as jnp
from jax import lax

D = 256
HEADS = 4
HEAD = 64
FF = 768
COND = 768
BAND = 16
CANVASES = 2
W = 128
ROWS_DEV = 8
H = 64
CW = 256
N_ROWS = 8


def draw_crop_ids(key, part):
    key = jax.random.fold_in(key, 17)
    cut_key, band_key = jax.random.split(key)
    band_count = CW // BAND
    boundary = (jax.random.randint(cut_key, (H, band_count), 0, 16) == 0).astype(jnp.int32)
    chosen = jax.random.randint(band_key, (), 0, band_count)
    row_index = jnp.arange(H)[:, None]
    band_index = jnp.arange(band_count)[None, :]
    boundary = jnp.where((row_index == 0) | (band_index == chosen), 0, boundary)
    segment = jnp.cumsum(boundary, axis=0)
    lifted = segment + (H - 1) - segment[H - 1:H, :]
    labels = band_index * H + lifted
    return jnp.repeat(labels, BAND, axis=1).astype(jnp.int32)


def levels(key, dims, cuts, smallest, high):
    level, own = 1.0, jax.random.fold_in(key, 6)
    for dim, parts in cuts:
        heights = jnp.exp(jax.random.uniform(jax.random.fold_in(own, dim), (parts,), jnp.float32, smallest / len(cuts), high / len(cuts)))
        level = level * jnp.repeat(heights, dims[dim] // parts).reshape([-1 if axis == dim else 1 for axis in range(len(dims))])
    return level


def scatter_about(key, dims, spread, limit, cuts=(), held_as=jnp.bfloat16):
    values = spread * jax.random.normal(key, dims, jnp.float32)
    if cuts:
        values = values * levels(key, dims, cuts, -0.22, 0.18)
    return jnp.clip(values, -limit, limit).astype(held_as)


def setup_inputs(seed: int = 0) -> dict:
    keys = jax.random.split(jax.random.key(seed), 12)
    return {
        "features": scatter_about(keys[0], (H, CW, D), 1.0, 6.0, ((0, 8), (1, 4))),
        "crop_ids": draw_crop_ids(jax.random.fold_in(keys[11], 71), 0),
        "conditioning": scatter_about(keys[2], (CANVASES, COND), 1.0, 6.0),
        "qkv_weight": scatter_about(keys[3], (D, 3 * D), D ** -0.5, 0.375, ((0, 32),)),
        "out_weight": scatter_about(keys[4], (D, D), (D // 16) ** -0.5, 1.5, ((0, 32),)),
        "up_weight": scatter_about(keys[5], (D, 2 * FF), D ** -0.5, 0.375, ((0, 32),)),
        "down_weight": scatter_about(keys[6], (FF, D), FF ** -0.5, 0.21875, ((0, 32),)),
        "attn_cond_weight": scatter_about(keys[7], (COND, D), (4 * COND) ** -0.5, 0.109375, ((0, 32),)),
        "feed_cond_weight": scatter_about(keys[8], (COND, D), (4 * COND) ** -0.5, 0.109375, ((0, 32),)),
        "attention_scale": jnp.clip(jnp.exp(jax.random.uniform(keys[9], (HEADS,), jnp.float32, math.log(6.0), math.log(20.0))), 6.0, 20.0),
        "cotangent": scatter_about(keys[10], (H, CW, D), 1.0, 6.0, ((0, 8), (1, 4))),
    }


HIGH = lax.Precision.HIGHEST

@jax.custom_vjp
def low(v):
    return lax.optimization_barrier(v.astype(jnp.bfloat16)).astype(jnp.float32)

@jax.custom_vjp
def low_back(v):
    return v

def low_keep(v):
    return (low(v), None)

def low_pass(kept, grad):
    return (grad,)

def back_keep(v):
    return (v, None)

def back_low(kept, grad):
    return (low(grad),)
low.defvjp(low_keep, low_pass)
low_back.defvjp(back_keep, back_low)

def ada_norm(values, gain):
    return values * lax.rsqrt(lax.optimization_barrier(jnp.mean(values * values, axis=-1, keepdims=True)) + 1e-06) * gain

def cosine_prep(vectors, scale):
    return vectors * jnp.sqrt(scale)[:, None] * lax.rsqrt(lax.optimization_barrier(jnp.sum(vectors * vectors, axis=-1, keepdims=True)) + 1e-06)

def rotate(vectors, row_place, col_place):
    quarter = vectors.shape[-1] // 8
    indices = jnp.arange(quarter).astype(jnp.float32)
    frequency = math.pi / 8.0 * jnp.exp(indices * (-math.log(10.0) / quarter))
    row_angle = row_place.astype(jnp.float32)[:, None] * frequency
    col_angle = col_place.astype(jnp.float32)[:, None] * frequency
    row_cos = jnp.cos(row_angle)[:, None, None, :]
    row_sin = jnp.sin(row_angle)[:, None, None, :]
    col_cos = jnp.cos(col_angle)[None, :, None, :]
    col_sin = jnp.sin(col_angle)[None, :, None, :]
    part_a = vectors[..., :quarter]
    part_b = vectors[..., quarter:2 * quarter]
    part_c = vectors[..., 2 * quarter:3 * quarter]
    part_d = vectors[..., 3 * quarter:4 * quarter]
    remainder = vectors[..., 4 * quarter:]
    return jnp.concatenate([part_a * row_cos - part_b * row_sin, part_a * row_sin + part_b * row_cos, part_c * col_cos - part_d * col_sin, part_c * col_sin + part_d * col_cos, remainder], axis=-1)

def windows(extended, offset, row_count, col_count):
    stripe = extended[offset:offset + row_count]
    return jnp.stack([stripe[:, column:column + col_count] for column in range(7)], axis=2)

def attend(query_block, key_block, value_block, id_block, own_ids):
    row_count, col_count = (query_block.shape[0], query_block.shape[1])
    score_parts = []
    allow_parts = []
    for offset in range(7):
        key_window = windows(key_block, offset, row_count, col_count)
        score_parts.append(jnp.einsum('rchd,rcxhd->rchx', query_block, key_window, precision=HIGH))
        allow_parts.append(windows(id_block, offset, row_count, col_count) == own_ids[:, :, None])
    scores = low_back(jnp.concatenate(score_parts, axis=-1))
    allowed = jnp.concatenate(allow_parts, axis=-1)[:, :, None, :]
    probs = low(jax.nn.softmax(jnp.where(allowed, scores, -1000000000.0), axis=-1))
    mixed = jnp.zeros(query_block.shape, jnp.float32)
    for offset in range(7):
        value_window = windows(value_block, offset, row_count, col_count)
        mixed = mixed + jnp.einsum('rchx,rcxhd->rchd', probs[..., 7 * offset:7 * offset + 7], value_window, precision=HIGH)
    return mixed

def window_attention(query_vectors, key_vectors, value_vectors, id_pad):
    key_pad = jnp.pad(key_vectors, ((3, 3), (3, 3), (0, 0), (0, 0)))
    value_pad = jnp.pad(value_vectors, ((3, 3), (3, 3), (0, 0), (0, 0)))

    def block(start):
        query_block = lax.dynamic_slice_in_dim(query_vectors, start, ROWS_DEV, 0)
        key_block = lax.dynamic_slice_in_dim(key_pad, start, ROWS_DEV + 6, 0)
        value_block = lax.dynamic_slice_in_dim(value_pad, start, ROWS_DEV + 6, 0)
        id_block = lax.dynamic_slice_in_dim(id_pad, start, ROWS_DEV + 6, 0)
        own_ids = id_block[3:3 + ROWS_DEV, 3:3 + CW]
        return attend(query_block, key_block, value_block, id_block, own_ids)
    starts = (jnp.arange(N_ROWS) * ROWS_DEV).astype(jnp.int32)
    blocks = lax.map(jax.checkpoint(block), starts)
    return blocks.reshape(query_vectors.shape)

def reference(features, crop_ids, conditioning, qkv_weight, out_weight, up_weight, down_weight, attn_cond_weight, feed_cond_weight, attention_scale, cotangent):
    cond_float = conditioning.astype(jnp.float32)
    row_place = jnp.arange(H).astype(jnp.int32)
    col_place = (jnp.arange(CW) % W).astype(jnp.int32)
    id_pad = jnp.pad(crop_ids, 3, constant_values=-1)

    def canvas_gain(weight):
        return jnp.repeat(1.0 + jnp.dot(cond_float, weight, precision=HIGH), W, axis=0)[None]

    def forward(inputs, full_qkv, full_out, full_up, full_down, full_attn_cond, full_feed_cond, scale):
        normed_attn = low(ada_norm(inputs, canvas_gain(full_attn_cond)))
        projected = low_back(jnp.dot(normed_attn.reshape(H * CW, D), full_qkv, precision=HIGH))
        projected = projected.reshape(H, CW, 3, HEADS, HEAD)
        query_vectors = low(rotate(cosine_prep(projected[:, :, 0], scale), row_place, col_place))
        key_vectors = low(rotate(cosine_prep(projected[:, :, 1], scale), row_place, col_place))
        value_vectors = low(projected[:, :, 2])
        attended = window_attention(query_vectors, key_vectors, value_vectors, id_pad)
        attended = low(low_back(attended)).reshape(H * CW, D)
        branch = low_back(jnp.dot(attended, full_out, precision=HIGH))
        middle = inputs + branch.reshape(H, CW, D)
        normed_feed = low(ada_norm(middle, canvas_gain(full_feed_cond))).reshape(H * CW, D)
        expanded = low_back(jnp.dot(normed_feed, full_up, precision=HIGH))
        gated = low(expanded[:, :FF] * jax.nn.gelu(expanded[:, FF:], approximate=False))
        return middle + jnp.dot(gated, full_down, precision=HIGH).reshape(H, CW, D)
    result, pullback = jax.vjp(forward, features.astype(jnp.float32), qkv_weight.astype(jnp.float32), out_weight.astype(jnp.float32), up_weight.astype(jnp.float32), down_weight.astype(jnp.float32), attn_cond_weight.astype(jnp.float32), feed_cond_weight.astype(jnp.float32), attention_scale)
    grads = pullback(cotangent.astype(jnp.float32))
    return (result.astype(jnp.bfloat16), grads[0], grads[1], grads[2], grads[3], grads[4], grads[5], grads[6], grads[7])
```

```python
import functools
import math

import jax
import jax.numpy as jnp
from jax import lax
from jax.experimental import pallas as pl
from jax.experimental.pallas import tpu as pltpu
from jax.sharding import PartitionSpec as P

CANVAS = 128
BAND = 16
REACH = 3
AXES = ("rows", "cols")
F32 = jnp.float32
BF16 = jnp.bfloat16
EPS = 1e-06
VMEM_LIMIT = 32 * 1024 * 1024


class Place:
    def __init__(self, direct, cols, n_cols):
        self.direct, self.cols, self.n_cols = direct, cols, n_cols

    def __getitem__(self, item):
        row, col = lax.axis_index("rows"), lax.axis_index("cols")
        if item == 0:
            return col * self.cols // CANVAS
        if item == 4:
            return row * self.n_cols + col
        if item == 5:
            return lax.rem(row, 2)
        if not self.direct:
            return (0, 0, 0, 0, 0, 0, 1)[item]
        return (None, row // 2, lax.rem(row, 2), col, None, None, 2 - lax.rem(row, 2))[item]


def mm(left, right):
    return lax.dot_general(left, right, (((1,), (0,)), ((), ())), preferred_element_type=F32)


def mm_rt(left, right):
    return lax.dot_general(left, right, (((1,), (1,)), ((), ())), preferred_element_type=F32)


def mm_lt(left, right):
    return lax.dot_general(left, right, (((0,), (0,)), ((), ())), preferred_element_type=F32)


def same_head(width, size):
    first = lax.broadcasted_iota(jnp.int32, (width, width), 0) // size
    second = lax.broadcasted_iota(jnp.int32, (width, width), 1) // size
    return jnp.where(first == second, 1.0, 0.0).astype(BF16)


def stack_heads(values, heads):
    lane = head_of(values.shape, heads)
    return jnp.concatenate(
        [jnp.where(lane == h, values, 0.0).astype(BF16) for h in range(heads)], axis=0
    )


def fold_heads(values, heads):
    count = values.shape[0] // heads
    lane = head_of((count, values.shape[1]), heads)
    total = values[:count]
    for h in range(1, heads):
        total = jnp.where(lane == h, values[h * count : (h + 1) * count], total)
    return total


def turned_order(width, heads):
    size = width // heads
    part = size // 8
    row = lax.broadcasted_iota(jnp.int32, (width, width), 0)
    col = lax.broadcasted_iota(jnp.int32, (width, width), 1)
    half, lane = col // (width // 2), col % (width // 2)
    head, j = lane // (size // 2), lane % (size // 2)
    rotated = j // part * 2 * part + j % part + half * part
    kept = 4 * part + j - 2 * part + half * 2 * part
    return jnp.where(row == head * size + jnp.where(j < 2 * part, rotated, kept), 1.0, 0.0).astype(BF16)


def halves(values):
    half = values.shape[1] // 2
    return values[:, :half], values[:, half:]


def head_of(shape, heads):
    half = shape[1] // 2
    return lax.broadcasted_iota(jnp.int32, shape, 1) % half // (half // heads)


def own_rows(values, count):
    edge = REACH * BAND
    return jnp.concatenate(
        [values[start + edge : start + edge + count] for start in range(0, values.shape[0], 2 * count)], axis=0
    )


def bands_of(ref, bands):
    parts = [
        ref[:, band * BAND : (band + 1) * BAND, :].astype(F32).reshape(-1, ref.shape[-1])
        for band in range(bands)
    ]
    return jnp.concatenate(parts, axis=0)


def pair_lanes(values, heads, pair):
    size = values.shape[1] // heads
    part = values[:, 128 * pair : 128 * pair + 128]
    lane = lax.broadcasted_iota(jnp.int32, part.shape, 1)
    return jnp.concatenate(
        [jnp.where(lane < size, part, 0.0), jnp.where(lane < size, 0.0, part)], axis=0
    ).astype(BF16)


def merge_pair(values, size):
    count = values.shape[0] // 2
    lane = lax.broadcasted_iota(jnp.int32, (count, 128), 1)
    return jnp.where(lane < size, values[:count], values[count:])


def close(shape, query_row, key_row):
    token = lax.broadcasted_iota(jnp.int32, shape, 0)
    place = lax.broadcasted_iota(jnp.int32, shape, 1)
    return (jnp.abs(token // BAND + query_row - place // BAND - key_row) <= REACH) & (
        jnp.abs(token % BAND - place % BAND) <= REACH
    )


def norm_scale(values):
    return lax.rsqrt(jnp.mean(values * values, axis=-1, keepdims=True) + EPS)


def place_parts(place, part_refs, wide_ref, last):
    lanes = wide_ref.shape[-1]
    for index, part in enumerate(part_refs):
        chip = place[1] ^ (index % 4)
        core = place[2] ^ (index // 4)
        group = part.shape[0]
        start = part.shape[-1] - lanes if last else 0
        for col in range(group):
            wide_ref[(chip * 2 + core) * group + col] = part[col, :, start : start + lanes].astype(F32)


def columns(wide_ref, start, width):
    chunks = wide_ref.shape[0]
    return wide_ref[:, :, start : start + width].reshape(chunks * 8, width).astype(BF16)


def split_parts(place, wide_ref, mine_ref, other_ref):
    group = mine_ref.shape[1]
    for chip in range(mine_ref.shape[0]):
        for col in range(group):
            mine_ref[chip, col] = wide_ref[(chip * 2 + place[2]) * group + col].astype(BF16)
            other_ref[chip, col] = wide_ref[(chip * 2 + 1 - place[2]) * group + col].astype(BF16)


def pack_kernel(
    per_canvas, place, cond_ref, qkv_ref, up_ref, out_ref, down_ref, attn_ref, feed_ref,
    near_ref, far_ref, cond_own_ref,
):
    own = attn_ref.shape[0]
    canvases, total = cond_ref.shape
    width = out_ref.shape[1]
    row = lax.broadcasted_iota(jnp.int32, (own, total), 0) + place[4] * own
    pick = jnp.where(row == lax.broadcasted_iota(jnp.int32, (own, total), 1), 1.0, 0.0).astype(BF16)
    cond = mm_rt(pick, cond_ref[...])
    cond_own_ref[...] = cond
    tails = []
    for canvas in range(canvases):
        lines = []
        for weight_ref in (attn_ref, feed_ref):
            line = jnp.sum(
                cond[:, canvas : canvas + 1] * weight_ref[...].astype(F32), axis=0, keepdims=True
            )
            high = line.astype(BF16).astype(F32)
            for part in (high, line - high):
                lines += [part[:, :128], part[:, 128:]]
        tails.append(jnp.concatenate(lines, axis=0))
    down = down_ref[...].astype(F32)
    parts = [up_ref[...], out_ref[...]] + [down[8 * i : 8 * i + 8].astype(BF16) for i in range(down.shape[0] // 8)]
    qkv = qkv_ref.shape[1]
    mine = place[0] == 0
    for ref, tail in (
        (near_ref, jnp.where(mine, tails[0], tails[1])),
        (far_ref, jnp.where(mine, tails[1], tails[0])),
    ):
        ref[:, :qkv] = qkv_ref[...]
        ref[:, qkv : qkv + 128] = tail.astype(BF16)
        at = qkv + 128
        for part in parts:
            ref[:, at : at + part.shape[1]] = part
            at += part.shape[1]


def line_kernel(place, p0, p1, p2, p3, line_ref):
    for index, part in enumerate((p0, p1, p2, p3)):
        line_ref[place[3] ^ index] = part[...]


def core_sum_kernel(place, mine_ref, got_ref, *refs):
    lanes = mine_ref.shape[-1]
    for index, out_ref in enumerate(refs[-4:]):
        chip = place[1] ^ (0, place[6], place[6] ^ 3, 3)[index]
        start = 0 if len(refs) == 4 else out_ref.shape[-1] - lanes
        out_ref[:, :, start : start + lanes] = (
            mine_ref[chip].astype(F32) + got_ref[chip].astype(F32)
        ).astype(BF16)


def pair_sum_kernel(one_ref, two_ref, out_ref):
    out_ref[...] = (one_ref[...].astype(F32) + two_ref[...].astype(F32)).astype(BF16)


def chip_sum_kernel(place, p0, p1, p2, o0, o1, o2, o3, keep_ref):
    keep_ref[...] = p0[...].astype(F32) + p1[...].astype(F32) + p2[...].astype(F32)
    for index, out_ref in enumerate((o0, o1, o2, o3)):
        out_ref[...] = keep_ref[place[3] ^ index].astype(out_ref.dtype)


def last_kernel(
    per_canvas, size, place, cond_ref, own_ref, one_ref, two_ref, three_ref,
    qkv_ref, out_ref, up_ref, down_ref, attn_ref, feed_ref, scale_ref,
):
    parts = [own_ref[...]] + [ref[...].astype(F32) for ref in (one_ref, two_ref, three_ref)]
    total = parts[0] + parts[1] + parts[2] + parts[3]
    width = out_ref.shape[1]
    at = up_ref.shape[1]
    up_ref[...] = total[:, :at]
    out_ref[...] = total[:, at : at + width]
    for i in range(down_ref.shape[0] // 8):
        at += width
        down_ref[8 * i : 8 * i + 8, :] = total[:, at : at + width]
    at += width
    qkv_ref[...] = total[:, at : at + qkv_ref.shape[1]]
    at += qkv_ref.shape[1]
    cond = cond_ref[...]
    attn, feed = 0.0, 0.0
    for canvas in range(cond.shape[1]):
        tail = jnp.zeros((8, 128), F32)
        for index, part in enumerate(parts):
            same = (place[3] ^ index) // per_canvas == canvas
            tail = tail + jnp.where(same, part[:, at:], 0.0)
        weight = cond[:, canvas : canvas + 1]
        attn = attn + weight * jnp.concatenate([tail[0:1], tail[1:2]], axis=1)
        feed = feed + weight * jnp.concatenate([tail[2:3], tail[3:4]], axis=1)
    attn_ref[...] = attn
    feed_ref[...] = feed
    tail = total[:, at:]
    scale = tail[4:5] + tail[5:6]
    for h in range(scale_ref.shape[0]):
        scale_ref[h] = scale[0, h * size]


def ready_kernel(
    heads, place, scale_ref, feat_ref, cot_ref, swap_ref, beside_ref, row_ref, col_ref, id_query_ref, id_key_ref,
    unit_ref, unit_turned_ref, own_turned_ref, cos_ref, sine_ref, mask_ref, inputs_ref, cot_out_ref, root_ref,
):
    rows, cols, width = feat_ref.shape
    count = rows * BAND
    bands = cols // BAND
    odd = place[5] == 1
    near = close((count, 2 * count), REACH, 0)
    lane = lax.broadcasted_iota(jnp.int32, (1, width // 2), 1) // (width // 2 // heads)
    root = jnp.zeros((1, width // 2), F32)
    for h in range(heads):
        root = jnp.where(lane == h, scale_ref[h], root)
    root_ref[...] = jnp.sqrt(root)
    inputs_ref[...] = bands_of(feat_ref, bands)
    cot_out_ref[...] = bands_of(cot_ref, bands).astype(BF16)
    for band in range(bands):
        part = slice(band * BAND, (band + 1) * BAND)
        swapped = swap_ref[:, part, :].astype(F32)
        beside = beside_ref[:, part, :].astype(F32)
        full = jnp.concatenate(
            [
                jnp.where(odd, swapped, beside),
                feat_ref[:, part, :].astype(F32),
                jnp.where(odd, beside, swapped),
                jnp.zeros((2, BAND, width), F32),
            ],
            axis=0,
        ).reshape(2 * count, width)
        span = slice(2 * band * count, 2 * (band + 1) * count)
        unit = full * norm_scale(full)
        unit_ref[span] = unit
        turned = jnp.transpose(unit).astype(BF16)
        unit_turned_ref[:, span] = turned
        own = slice(REACH * BAND, REACH * BAND + count)
        own_turned_ref[:, band * count : (band + 1) * count] = jnp.transpose(unit[own]).astype(BF16)
        for i, ref in enumerate((cos_ref, sine_ref)):
            ref[span] = (row_ref[i][:, None, :] + col_ref[i, part, :][None]).reshape(2 * count, width // 2)
        alike = id_query_ref[REACH * BAND : REACH * BAND + count, band : band + 1] == id_key_ref[
            band : band + 1, :
        ]
        mask_ref[band] = jnp.where(near & alike, 1.0, 0.0).astype(BF16)


def attend_kernel(
    heads, place, root_ref, unit_ref, cos_ref, sine_ref, mask_ref, p0, p1, p2, p3, p4, p5, p6, p7,
    query_ref, key_ref, value_ref, raised_ref, mixed_ref, inverse_ref, along_q_ref, length_q_ref, along_k_ref, length_k_ref,
    gain_ref, gain_col_ref, w_ref,
    wide_ref,
):
    bands, count = mask_ref.shape[:2]
    width = unit_ref.shape[1]
    size = width // heads
    edge = REACH * BAND
    place_parts(place, (p0, p1, p2, p3, p4, p5, p6, p7), wide_ref, False)
    weight = columns(wide_ref, 0, 3 * width)
    order = turned_order(width, heads)
    turned = mm(
        jnp.concatenate([weight[:, :width], weight[:, width : 2 * width]], axis=0), order
    ).astype(BF16)
    w_ref[:, :width], w_ref[:, width : 2 * width] = turned[:width], turned[width:]
    w_ref[:, 2 * width :] = weight[:, 2 * width :]
    sums = jnp.sum(wide_ref[:, :, 3 * width :], axis=0)
    pairs = [sums[i : i + 2] + sums[i + 2 : i + 4] for i in (0, 4)]
    picked = 1.0 + jnp.concatenate(
        [jnp.concatenate([pair[0:1], pair[1:2]], axis=1) for pair in pairs], axis=0
    )
    gain_ref[...] = picked
    gain_col_ref[...] = jnp.transpose(jnp.broadcast_to(picked[0:1], (128, width)))
    root = root_ref[...]
    unit = unit_ref[...]
    normed = (unit * picked[0:1]).astype(BF16)
    value_ref[...] = mm(normed, weight[:, 2 * width :]).astype(BF16)
    ones_head = same_head(width // 2, size // 2)
    cos, sine = cos_ref[...], sine_ref[...]
    for i, ref in enumerate((query_ref, key_ref)):
        first, second = halves(mm(normed, turned[i * width : (i + 1) * width]))
        short = lax.rsqrt(mm((first * first + second * second).astype(BF16), ones_head) + EPS)
        length = short * root
        ref[...] = jnp.concatenate(
            [(first * cos - second * sine) * length, (second * cos + first * sine) * length], axis=1
        ).astype(BF16)
        along = jnp.concatenate([first * short, second * short], axis=1)
        if i == 0:
            along_q_ref[...], length_q_ref[...] = own_rows(along, count), own_rows(length, count)
        else:
            along_k_ref[...], length_k_ref[...] = along, length
    ones_half = jnp.ones((2 * count, 128), BF16)
    for band in range(bands):
        start = 2 * band * count
        query = query_ref[start + edge : start + edge + count, :].astype(F32)
        scores = mm_rt(stack_heads(query, heads), key_ref[start : start + 2 * count, :])
        raised = jnp.exp(scores).astype(BF16) * jnp.concatenate([mask_ref[band]] * heads, axis=0)
        raised_ref[band] = raised
        value = value_ref[start : start + 2 * count, :]
        span = slice(band * count, (band + 1) * count)
        for pair in range(heads // 2):
            lanes = slice(128 * pair, 128 * pair + 128)
            both = mm(
                raised[2 * pair * count : 2 * (pair + 1) * count],
                jnp.concatenate([value[:, lanes], ones_half], axis=1),
            )
            inverse = 1.0 / merge_pair(both[:, 128:], size)
            mixed_ref[span, lanes] = merge_pair(both[:, :128], size) * inverse
            inverse_ref[span, lanes] = inverse


def feed_kernel(
    heads, place, inputs_ref, cot_ref, p0, p1, p2, p3, p4, p5, p6, p7, gain_ref, mixed_ref, inverse_ref,
    middle_ref, middle_grad_ref, shrunk_ref, gain_grad_ref,
    w_down_ref, mixed_low_ref, normed_ref, gated_ref, d_exp_ref, branch_ref,
    wide_ref,
):
    width = inputs_ref.shape[1]
    chunks = wide_ref.shape[0]
    hidden = w_down_ref.shape[0]
    own_down = hidden // chunks
    ups = 2 * hidden
    place_parts(place, (p0, p1, p2, p3, p4, p5, p6, p7), wide_ref, True)
    w_up = columns(wide_ref, 0, ups)
    w_out = columns(wide_ref, ups, width)
    w_down = (
        jnp.concatenate(
            [
                wide_ref[:, :, ups + width * (i + 1) : ups + width * (i + 2)]
                for i in range(own_down // 8)
            ],
            axis=1,
        )
        .reshape(hidden, width)
        .astype(BF16)
    )
    w_down_ref[...] = w_down
    gain_feed = gain_ref[1:2]
    mixed = mixed_ref[...]
    mixed_low = mixed.astype(BF16)
    mixed_low_ref[...] = mixed_low
    middle = inputs_ref[...] + mm(mixed_low, w_out)
    middle_ref[...] = middle
    scale = norm_scale(middle)
    unit = middle * scale
    normed = (unit * gain_feed).astype(BF16)
    normed_ref[...] = normed
    cot = cot_ref[...].astype(F32)
    half = math.sqrt(0.5)
    density = 1.0 / math.sqrt(2.0 * math.pi)
    pulled = None
    for start in range(0, hidden, width):
        here = slice(start, start + width)
        there = slice(hidden + start, hidden + start + width)
        left = mm(normed, w_up[:, here])
        gate = mm(normed, w_up[:, there])
        d_gated = mm_rt(cot_ref[...], w_down[here])
        phi = 0.5 + 0.5 * lax.erf(gate * half)
        shaped = gate * phi
        gated_ref[:, here] = (left * shaped).astype(BF16)
        slope = phi + gate * (jnp.exp(gate * gate * -0.5) * density)
        d_left = (d_gated * shaped).astype(BF16)
        d_gate = (d_gated * left * slope).astype(BF16)
        d_exp_ref[:, here] = d_left
        d_exp_ref[:, there] = d_gate
        part = mm_rt(d_left, w_up[:, here]) + mm_rt(d_gate, w_up[:, there])
        pulled = part if pulled is None else pulled + part
    gain_grad_ref[...] = jnp.sum(pulled * unit, axis=0, keepdims=True)
    inner = pulled * gain_feed
    d_middle = cot + scale * (inner - unit * jnp.mean(unit * inner, axis=-1, keepdims=True))
    middle_grad_ref[...] = d_middle
    branch = d_middle.astype(BF16)
    branch_ref[...] = branch
    shrunk_ref[...] = (mm_rt(branch, w_out) * inverse_ref[...]).astype(BF16)


def weights_kernel(
    place, cot_ref, mixed_low_ref, normed_ref, gated_ref, d_exp_ref, branch_ref, mine_ref, other_ref, wide_ref
):
    width = cot_ref.shape[1]
    chunks = wide_ref.shape[0]
    ups = d_exp_ref.shape[1]
    own_down = gated_ref.shape[1] // chunks
    wide_ref[:, :, :ups] = mm_lt(normed_ref[...], d_exp_ref[...]).reshape(chunks, 8, ups)
    wide_ref[:, :, ups : ups + width] = mm_lt(mixed_low_ref[...], branch_ref[...]).reshape(
        chunks, 8, width
    )
    grad = mm_lt(gated_ref[...], cot_ref[...]).reshape(chunks, own_down, width)
    for i in range(own_down // 8):
        start = ups + width * (i + 1)
        wide_ref[:, :, start : start + width] = grad[:, 8 * i : 8 * i + 8]
    split_parts(place, wide_ref, mine_ref, other_ref)


def output_kernel(middle_ref, gated_ref, w_down_ref, out_ref):
    rows, cols, width = out_ref.shape
    total = (middle_ref[...] + mm(gated_ref[...], w_down_ref[...])).astype(BF16)
    count = rows * BAND
    for band in range(cols // BAND):
        out_ref[:, band * BAND : (band + 1) * BAND, :] = total[band * count : (band + 1) * count].reshape(
            rows, BAND, width
        )


def back_kernel(
    heads, shrunk_ref, mixed_ref, raised_ref, query_ref, key_ref, value_ref, dq_ref, dk_ref, dv_ref
):
    bands, _, keys = raised_ref.shape
    count = keys // 2
    edge = REACH * BAND
    ones_half = jnp.ones((keys, 128), BF16)
    for band in range(bands):
        span = slice(band * count, (band + 1) * count)
        start = band * keys
        whole = slice(start, start + keys)
        shrunk = shrunk_ref[span].astype(F32)
        level_rows = -(shrunk * mixed_ref[span])
        value = value_ref[whole, :]
        raised = raised_ref[band]
        parts, stacks = [], []
        for pair in range(heads // 2):
            lanes = slice(128 * pair, 128 * pair + 128)
            stacks.append(pair_lanes(shrunk, heads, pair))
            parts.append(
                mm_rt(
                    jnp.concatenate([stacks[-1], pair_lanes(level_rows, heads, pair)], axis=1),
                    jnp.concatenate([value[:, lanes], ones_half], axis=1),
                )
            )
        d_scores = (raised.astype(F32) * jnp.concatenate(parts, axis=0)).astype(BF16)
        dq_ref[span] = fold_heads(mm(d_scores, key_ref[whole, :]), heads)
        query = query_ref[start + edge : start + edge + count, :].astype(F32)
        dk_ref[whole, :] = mm_lt(d_scores, stack_heads(query, heads))
        for pair in range(heads // 2):
            lanes = slice(128 * pair, 128 * pair + 128)
            dv_ref[whole, lanes] = mm_lt(raised[2 * pair * count : 2 * (pair + 1) * count], stacks[pair])


def pull_head(grad, along, length, cos, sine, heads):
    first, second = halves(grad)
    along_first, along_second = halves(along)
    first, second = first * cos + second * sine, second * cos - first * sine
    ones_head = same_head(first.shape[1], first.shape[1] // heads)
    part = mm((along_first * first + along_second * second).astype(BF16), ones_head)
    grad = jnp.concatenate(
        [length * (first - along_first * part), length * (second - along_second * part)], axis=1
    )
    return grad.astype(BF16), jnp.sum(part, axis=0, keepdims=True)


def lane_sums(product):
    total = product[:, :128]
    for start in range(128, product.shape[1], 128):
        total = total + product[:, start : start + 128]
    return jnp.sum(jnp.transpose(total), axis=0, keepdims=True)


def project_kernel(
    heads, rows, place, root_ref, cos_ref, sine_ref, w_ref, gain_col_ref, unit_turned_ref, own_turned_ref,
    along_q_ref, length_q_ref, along_k_ref, length_k_ref, dq_ref, dk_ref, dv_ref, gain_grad_ref,
    d_query_ref, d_rest_ref, mine_ref, other_ref, wide_ref,
):
    tokens, width = dq_ref.shape
    chunks = wide_ref.shape[0]
    cos, sine = cos_ref[...], sine_ref[...]
    count = rows * BAND
    d_key, along_k = pull_head(dk_ref[...], along_k_ref[...], length_k_ref[...], cos, sine, heads)
    d_value = dv_ref[...].astype(BF16)
    d_query, along_q = pull_head(
        dq_ref[...], along_q_ref[...], length_q_ref[...], own_rows(cos, count), own_rows(sine, count), heads
    )
    d_query_ref[...] = d_query
    d_rest = jnp.concatenate([d_key, d_value], axis=1)
    d_rest_ref[...] = d_rest
    plain = jnp.concatenate(
        [
            mm(own_turned_ref[...], d_query),
            mm(unit_turned_ref[...], d_rest),
        ],
        axis=1,
    )
    scaled = plain * jnp.concatenate([gain_col_ref[...]] * (3 * width // 128), axis=1)
    turned = jnp.concatenate([scaled[:, :width], scaled[:, width : 2 * width]], axis=0).astype(BF16)
    plain_order = mm_rt(turned, turned_order(width, heads))
    wide_ref[:, :, :width] = plain_order[:width].reshape(chunks, 8, width)
    wide_ref[:, :, width : 2 * width] = plain_order[width:].reshape(chunks, 8, width)
    wide_ref[:, :, 2 * width : 3 * width] = scaled[:, 2 * width :].reshape(chunks, 8, width)
    gain_total = lane_sums(plain * w_ref[...].astype(F32))
    lines = []
    for total in (gain_total, gain_grad_ref[...]):
        lines += [total[:, :128], total[:, 128:]]
    total = (along_q + along_k) * 0.5 / root_ref[...]
    high = total.astype(BF16).astype(F32)
    lines += [high, total - high, jnp.zeros((2, 128), F32)]
    wide_ref[:, :, 3 * width :] = jnp.broadcast_to(
        jnp.concatenate(lines, axis=0)[None], (chunks, 8, 128)
    )
    split_parts(place, wide_ref, mine_ref, other_ref)


def normed_back_kernel(
    rows, place, w_ref, d_query_ref, d_rest_ref, own_ref, rim_swap_ref, rim_beside_ref
):
    width = own_ref.shape[1]
    count, edge = rows * BAND, REACH * BAND
    odd = place[5] == 1
    whole = mm_rt(d_rest_ref[...], w_ref[:, width:])
    own_ref[...] = mm_rt(d_query_ref[...], w_ref[:, :width]) + own_rows(whole, count)
    for band in range(whole.shape[0] // (2 * count)):
        start = 2 * band * count
        upper, lower = whole[start : start + edge], whole[start + edge + count : start + 2 * edge + count]
        here = slice(band * edge, (band + 1) * edge)
        rim_swap_ref[here] = jnp.where(odd, upper, lower).astype(BF16)
        rim_beside_ref[here] = jnp.where(odd, lower, upper).astype(BF16)


def features_kernel(place, inputs_ref, gain_ref, own_ref, rim_swap_ref, rim_beside_ref, middle_grad_ref, grad_ref):
    rows, cols, width = grad_ref.shape
    bands = cols // BAND
    count, edge = rows * BAND, REACH * BAND
    odd = place[5] == 1
    zeros = jnp.zeros((count - 2 * edge, width), F32)
    rims = []
    for band in range(bands):
        here = slice(band * edge, (band + 1) * edge)
        swapped, beside = rim_swap_ref[here].astype(F32), rim_beside_ref[here].astype(F32)
        rims += [jnp.where(odd, swapped, beside), zeros, jnp.where(odd, beside, swapped)]
    inner = (own_ref[...] + jnp.concatenate(rims, axis=0)) * gain_ref[0:1]
    inputs = inputs_ref[...]
    scale = norm_scale(inputs)
    unit = inputs * scale
    grad = middle_grad_ref[...] + scale * (inner - unit * jnp.mean(unit * inner, axis=-1, keepdims=True))
    for band in range(bands):
        grad_ref[:, band * BAND : (band + 1) * BAND, :] = grad[band * count : (band + 1) * count].reshape(
            rows, BAND, width
        )


def forward_kernel(
    heads, place, root_ref, unit_ref, cos_ref, sine_ref, mask_ref, inputs_ref, cot_ref,
    p0, p1, p2, p3, p4, p5, p6, p7,
    query_ref, key_ref, value_ref, raised_ref, mixed_ref, along_q_ref, length_q_ref, along_k_ref, length_k_ref,
    gain_ref, gain_col_ref, w_ref, middle_ref, middle_grad_ref, shrunk_ref, gain_grad_ref,
    w_down_ref, gated_ref, mine_ref, other_ref,
    inverse_ref, first_wide_ref, second_wide_ref, mixed_low_ref, normed_ref, d_exp_ref, branch_ref,
):
    parts = (p0, p1, p2, p3, p4, p5, p6, p7)
    attend_kernel(
        heads, place, root_ref, unit_ref, cos_ref, sine_ref, mask_ref, *parts,
        query_ref, key_ref, value_ref, raised_ref, mixed_ref, inverse_ref,
        along_q_ref, length_q_ref, along_k_ref, length_k_ref, gain_ref, gain_col_ref, w_ref, first_wide_ref,
    )
    feed_kernel(
        heads, place, inputs_ref, cot_ref, *parts, gain_ref, mixed_ref, inverse_ref,
        middle_ref, middle_grad_ref, shrunk_ref, gain_grad_ref,
        w_down_ref, mixed_low_ref, normed_ref, gated_ref, d_exp_ref, branch_ref, second_wide_ref,
    )
    weights_kernel(
        place, cot_ref, mixed_low_ref, normed_ref, gated_ref, d_exp_ref, branch_ref, mine_ref, other_ref,
        second_wide_ref,
    )


def backward_kernel(
    heads, rows, place, root_ref, shrunk_ref, mixed_ref, raised_ref, query_ref, key_ref, value_ref,
    cos_ref, sine_ref, w_ref, gain_col_ref, unit_turned_ref, own_turned_ref, along_q_ref, length_q_ref, along_k_ref, length_k_ref,
    gain_grad_ref,
    d_query_ref, d_rest_ref, mine_ref, other_ref, dq_ref, dk_ref, dv_ref, wide_ref,
):
    back_kernel(
        heads, shrunk_ref, mixed_ref, raised_ref, query_ref, key_ref, value_ref, dq_ref, dk_ref, dv_ref
    )
    project_kernel(
        heads, rows, place, root_ref, cos_ref, sine_ref, w_ref, gain_col_ref, unit_turned_ref, own_turned_ref,
        along_q_ref, length_q_ref, along_k_ref, length_k_ref, dq_ref, dk_ref, dv_ref, gain_grad_ref,
        d_query_ref, d_rest_ref, mine_ref, other_ref, wide_ref,
    )


def call(kernel, outs, scratch=(), place=None, smem=0, smem_out=0, flops=10**9, pin=True, aliases=None):
    if place is not None:
        kernel = functools.partial(kernel, place)

    def run(*args):
        args = [
            arg if i < smem else pltpu.with_memory_space_constraint(arg, pltpu.VMEM if pin else pltpu.HBM)
            for i, arg in enumerate(args)
        ]
        return pl.pallas_call(
            kernel,
            out_shape=outs,
            in_specs=[
                pl.BlockSpec(memory_space=pltpu.SMEM if i < smem else pltpu.VMEM)
                for i in range(len(args))
            ],
            out_specs=[
                pl.BlockSpec(memory_space=pltpu.SMEM if i >= len(outs) - smem_out else pltpu.VMEM)
                for i in range(len(outs))
            ],
            scratch_shapes=list(scratch),
            input_output_aliases=aliases or {},
            compiler_params=pltpu.CompilerParams(vmem_limit_bytes=VMEM_LIMIT),
            cost_estimate=pl.CostEstimate(flops=flops, bytes_accessed=4 * 10**6 if flops > 1 else 1, transcendentals=0),
        )(*args)

    return run


def rotation_tables(row_place, col_place, heads, size):
    part = size // 8
    lane = jnp.arange(heads * size // 2) % (size // 2)
    index = (lane % part).astype(F32)
    frequency = math.pi / 8.0 * jnp.exp(index * (-math.log(10.0) / part))
    group = lane // part

    def table(place, kind):
        angle = place.astype(F32)[:, None] * frequency
        cos = jnp.where(group == kind, jnp.cos(angle), 0.0)
        if kind:
            cos = jnp.where(group >= 2, 1.0, cos)
        return jnp.stack([cos, jnp.where(group == kind, jnp.sin(angle), 0.0)])

    return table(row_place, 0), table(col_place, 1)


def window_ids(crop_ids, row_start, rows):
    ids = jnp.pad(crop_ids[:, ::BAND], ((REACH, 2 * rows), (0, 0)), constant_values=-1)
    ids = lax.dynamic_slice_in_dim(ids, row_start, 2 * rows, 0)
    return jnp.repeat(ids, BAND, axis=0), jnp.repeat(ids.T, BAND, axis=1)


def on_device(
    features, crop_ids, conditioning, qkv_weight, out_weight, up_weight, down_weight,
    attn_cond_weight, feed_cond_weight, attention_scale, cotangent,
):
    rows, cols, width = features.shape
    heads = attention_scale.shape[0]
    size = width // heads
    bands = cols // BAND
    count = rows * BAND
    tokens = rows * cols
    edge = REACH * BAND
    n_rows, n_cols = lax.axis_size("rows"), lax.axis_size("cols")
    devices = n_rows * n_cols
    hidden = down_weight.shape[0] * devices
    own_cond = attn_cond_weight.shape[0]
    canvases = conditioning.shape[0]
    row, col = lax.axis_index("rows"), lax.axis_index("cols")
    row_start, col_start = row * rows, col * cols
    canvas = col_start // CANVAS
    group, chips = 4, 4
    chunks = 2 * chips * group
    direct = (n_rows, n_cols) == (2 * chips, group) and chunks * 8 == width
    first_lanes = 3 * width + 128
    second_lanes = 2 * hidden + width + hidden * width // (8 * chunks)
    per_canvas = max(n_cols // canvases, 1)
    place = Place(direct, cols, n_cols)

    def result(*dims, dtype=F32):
        return jax.ShapeDtypeStruct(dims, dtype)

    def shape(*dims, dtype=F32):
        return pltpu.VMEM(dims, dtype)

    def low(*dims):
        return shape(*dims, dtype=BF16)

    def over(axis, by):
        size_of = lax.axis_size(axis)
        return lambda value: lax.ppermute(value, axis, [(i, i ^ by) for i in range(size_of)])

    z_moves = [over("cols", k) for k in range(1, group)]
    xy_moves = [over("rows", 2 * m) for m in range(1, chips)]

    def chip_pairs(step):
        return [(i, i ^ (4 if i % 2 == step else 2)) for i in range(n_rows)]

    def first_chip(value):
        return lax.ppermute(value, "rows", chip_pairs(0))

    def second_chip(value):
        return lax.ppermute(value, "rows", chip_pairs(1))

    core_move = over("rows", 1)

    if direct:
        near, far, cond_own = call(
            functools.partial(pack_kernel, per_canvas),
            [
                low(8, first_lanes + second_lanes),
                low(8, first_lanes + second_lanes),
                shape(own_cond, canvases),
            ],
            place=place,
            pin=False,
        )(conditioning, qkv_weight, up_weight, out_weight, down_weight, attn_cond_weight, feed_cond_weight)
        line = call(line_kernel, [low(group, 8, first_lanes + second_lanes)], place=place)(
            near,
            *[move(near if k // per_canvas == 0 else far) for k, move in enumerate(z_moves, 1)],
        )[0]
        mine = [line] + [move(line) for move in xy_moves]
    else:
        def parts_of(full):
            full = full.reshape(chips, 2, group, 8, full.shape[-1])
            return [full[m, core] for core in range(2) for m in range(chips)]

        def whole(weight):
            return lax.all_gather(weight, AXES, axis=0, tiled=True)

        cond = lax.dynamic_slice_in_dim(conditioning, place[4] * own_cond, own_cond, 1)
        cond_own = cond.T.astype(F32)
        sums = [
            lax.psum(jnp.dot(cond, weight, preferred_element_type=F32), AXES)
            for weight in (attn_cond_weight, feed_cond_weight)
        ]
        lines = []
        for part in sums:
            part = lax.dynamic_slice_in_dim(part, canvas, 1, 0).reshape(-1, 128)
            high = lax.reduce_precision(part, 8, 7)
            lines += [high, part - high]
        lines = jnp.pad(jnp.concatenate(lines).astype(BF16), ((0, width - 8), (0, 0)))
        down = whole(down_weight).reshape(chunks, -1, 8, width).transpose(0, 2, 1, 3).reshape(width, -1)
        parts = parts_of(
            jnp.concatenate([whole(qkv_weight), lines, whole(up_weight), whole(out_weight), down], axis=1)
        )

    odd = row % 2 == 1
    beside_pairs = [(i, (i + 1 if i % 2 else i - 1) % n_rows) for i in range(n_rows)]

    def beside_move(value):
        return lax.ppermute(value, "rows", beside_pairs)

    first_rows, last_rows = features[:REACH], features[rows - REACH :]
    halo_swap = core_move(jnp.where(odd, first_rows, last_rows))
    halo_beside = beside_move(jnp.where(odd, last_rows, first_rows))

    row_place = row_start - REACH + jnp.arange(2 * rows, dtype=jnp.int32)
    col_place = (col_start + jnp.arange(cols, dtype=jnp.int32)) % CANVAS
    row_table, col_table = rotation_tables(row_place, col_place, heads, size)
    id_query, id_key = window_ids(crop_ids, row_start, rows)

    unit, unit_turned, own_turned, cos, sine, mask, inputs, cot, root = call(
        functools.partial(ready_kernel, heads),
        [
            shape(2 * tokens, width),
            low(width, 2 * tokens),
            low(width, tokens),
            shape(2 * tokens, width // 2),
            shape(2 * tokens, width // 2),
            low(bands, count, 2 * count),
            shape(tokens, width),
            low(tokens, width),
            shape(1, width // 2),
        ],
        place=place,
        smem=1,
    )(attention_scale, features, cotangent, halo_swap, halo_beside, row_table, col_table, id_query, id_key)
    if direct:
        mine = mine[:1] + [lax.optimization_barrier((part, unit))[0] for part in mine[1:]]
        far = core_move(mine[3])
        for i in (1, 2):
            mine[i], far = lax.optimization_barrier((mine[i], far))
        parts = mine + [core_move(part) for part in mine[:3]] + [far]

    (
        query, key, value, raised, mixed, along_q, length_q, along_k, length_k, gain, gain_col, w_qkv,
        middle, middle_grad, shrunk, gain_grad, w_down, gated, mine_second, other_second,
    ) = call(
        functools.partial(forward_kernel, heads),
        [
            low(2 * tokens, width),
            low(2 * tokens, width),
            low(2 * tokens, width),
            low(bands, heads * count, 2 * count),
            shape(tokens, width),
            shape(tokens, width),
            shape(tokens, width // 2),
            shape(2 * tokens, width),
            shape(2 * tokens, width // 2),
            shape(2, width),
            shape(width, 128),
            low(width, 3 * width),
            shape(tokens, width),
            shape(tokens, width),
            low(tokens, width),
            shape(1, width),
            low(hidden, width),
            low(tokens, hidden),
            low(chips, group, 8, second_lanes),
            low(chips, group, 8, second_lanes),
        ],
        scratch=[
            pltpu.VMEM((tokens, width), F32),
            pltpu.VMEM((chunks, 8, first_lanes), F32),
            pltpu.VMEM((chunks, 8, second_lanes), F32),
            pltpu.VMEM((tokens, width), BF16),
            pltpu.VMEM((tokens, width), BF16),
            pltpu.VMEM((tokens, 2 * hidden), BF16),
            pltpu.VMEM((tokens, width), BF16),
        ],
        place=place,
    )(root, unit, cos, sine, mask, inputs, cot, *parts)

    d_query, d_rest, mine_first, other_first = call(
        functools.partial(backward_kernel, heads, rows),
        [
            low(tokens, width),
            low(2 * tokens, 2 * width),
            low(chips, group, 8, first_lanes),
            low(chips, group, 8, first_lanes),
        ],
        scratch=[
            pltpu.VMEM((tokens, width), F32),
            pltpu.VMEM((2 * tokens, width), F32),
            pltpu.VMEM((2 * tokens, width), F32),
            pltpu.VMEM((chunks, 8, first_lanes), F32),
        ],
        place=place,
        flops=1,
    )(
        root, shrunk, mixed, raised, query, key, value, cos, sine, w_qkv, gain_col, unit_turned, own_turned,
        along_q, length_q, along_k, length_k, gain_grad,
    )

    def last_output(gated):
        return call(output_kernel, [result(rows, cols, width, dtype=BF16)])(middle, gated, w_down)[0]

    def normed_back(d_query, d_rest):
        return call(
            functools.partial(normed_back_kernel, rows),
            [shape(tokens, width), low(bands * edge, width), low(bands * edge, width)],
            place=place,
        )(w_qkv, d_query, d_rest)

    def last_features(own, rim_swap, rim_beside):
        return call(features_kernel, [result(rows, cols, width)], place=place)(
            inputs, gain, own, rim_swap, rim_beside, middle_grad
        )[0]

    if direct:
        all_lanes = second_lanes + first_lanes
        lines = [low(group, 8, all_lanes) for _ in range(chips)]
        second_got = core_move(other_second)
        sums = call(core_sum_kernel, lines, place=place)(mine_second, second_got)
        sums = call(core_sum_kernel, lines, place=place, aliases={2 + i: i for i in range(chips)})(
            mine_first, core_move(other_first), *sums
        )
        sums, d_rest = lax.optimization_barrier((sums, d_rest))
        own, first_part, second_part, far_part = sums
        far_got, second_got = second_chip(far_part), second_chip(second_part)
        first_part = call(pair_sum_kernel, [low(group, 8, all_lanes)], flops=1)(first_part, far_got)[0]
        sums = [own, first_chip(first_part), second_got]
        own_grad, rim_swap, rim_beside = normed_back(d_query, d_rest)
        rim_swap, rim_beside = core_move(rim_swap), beside_move(rim_beside)
        blocks = call(
            chip_sum_kernel,
            [shape(8, all_lanes)] + [low(8, all_lanes) for _ in z_moves],
            scratch=[pltpu.VMEM((group, 8, all_lanes), F32)],
            place=place,
        )(*sums)
        blocks, gated, own_grad = lax.optimization_barrier((blocks, gated, own_grad))
        output = last_output(gated)
        grad_features = last_features(own_grad, rim_swap, rim_beside)
        grad_qkv, grad_out, grad_up, grad_down, grad_attn_cond, grad_feed_cond, grad_scale = call(
            functools.partial(last_kernel, per_canvas, size // 2),
            [
                result(8, 3 * width),
                result(8, width),
                result(8, 2 * hidden),
                result(hidden // chunks, width),
                result(own_cond, width),
                result(own_cond, width),
                result(heads),
            ],
            place=place,
            smem_out=1,
        )(cond_own, blocks[0], *[move(block) for move, block in zip(z_moves, blocks[1:])])
    else:
        own_grad, rim_swap, rim_beside = normed_back(d_query, d_rest)
        grad_features = last_features(own_grad, core_move(rim_swap), beside_move(rim_beside))
        output = last_output(gated)

        def joined(mine, other):
            return jnp.stack([mine, other], axis=1).astype(F32).reshape(chunks, 8, mine.shape[-1])

        def scattered(grad):
            return lax.psum_scatter(grad.reshape(-1, grad.shape[-1]), AXES, scatter_dimension=0, tiled=True)

        last = joined(mine_first, other_first)
        second = joined(mine_second, other_second)
        ups = 2 * hidden
        grad_qkv = scattered(last[:, :, : 3 * width])
        grad_up = scattered(second[:, :, :ups])
        grad_out = scattered(second[:, :, ups : ups + width])
        grad_down = scattered(
            second[:, :, ups + width :].reshape(chunks, 8, -1, width).transpose(0, 2, 1, 3)
        )
        spot = (jnp.arange(canvases) == canvas).astype(F32)[:, None, None]
        tail = lax.psum(spot * last[0, :, 3 * width :][None], AXES)

        def cond_grad(sums):
            return jnp.sum(cond_own[:, :, None] * sums.reshape(canvases, width)[None], axis=1)

        grad_attn_cond = cond_grad(tail[:, 0:2])
        grad_feed_cond = cond_grad(tail[:, 2:4])
        grad_scale = jnp.sum(tail[:, 4] + tail[:, 5], axis=0)[:: size // 2]
    return (
        output, grad_features, grad_qkv, grad_out, grad_up, grad_down, grad_attn_cond, grad_feed_cond, grad_scale,
    )


def solution(mesh):
    tile, whole, split = P("rows", "cols", None), P(), P(AXES, None)
    return jax.shard_map(
        on_device,
        mesh=mesh,
        in_specs=(tile, P(None, "cols"), whole, split, split, split, split, split, split, whole, tile),
        out_specs=(tile, tile, split, split, split, split, split, split, whole),
        check_vma=False,
    )
```

```python
import functools
import math

import jax
import jax.numpy as jnp
from jax import lax
from jax.experimental import pallas as pl
from jax.experimental.pallas import tpu as pltpu
from jax.sharding import PartitionSpec as P

CANVAS = 128
BAND = 16
REACH = 3
AXES = ("rows", "cols")
F32 = jnp.float32
BF16 = jnp.bfloat16
EPS = 1e-06
VMEM_LIMIT = 32 * 1024 * 1024


class Place:
    def __init__(self, direct, cols, n_cols):
        self.direct, self.cols, self.n_cols = direct, cols, n_cols

    def __getitem__(self, item):
        row, col = lax.axis_index("rows"), lax.axis_index("cols")
        if item == 0:
            return col * self.cols // CANVAS
        if item == 4:
            return row * self.n_cols + col
        if item == 5:
            return lax.rem(row, 2)
        if not self.direct:
            return (0, 0, 0, 0, 0, 0, 1)[item]
        return (None, row // 2, lax.rem(row, 2), col, None, None, 2 - lax.rem(row, 2))[item]


def mm(left, right):
    return lax.dot_general(left, right, (((1,), (0,)), ((), ())), preferred_element_type=F32)


def mm_rt(left, right):
    return lax.dot_general(left, right, (((1,), (1,)), ((), ())), preferred_element_type=F32)


def mm_lt(left, right):
    return lax.dot_general(left, right, (((0,), (0,)), ((), ())), preferred_element_type=F32)


def same_head(width, size):
    first = lax.broadcasted_iota(jnp.int32, (width, width), 0) // size
    second = lax.broadcasted_iota(jnp.int32, (width, width), 1) // size
    return jnp.where(first == second, 1.0, 0.0).astype(BF16)


def stack_heads(values, heads):
    lane = head_of(values.shape, heads)
    return jnp.concatenate(
        [jnp.where(lane == h, values, 0.0).astype(BF16) for h in range(heads)], axis=0
    )


def fold_heads(values, heads):
    count = values.shape[0] // heads
    lane = head_of((count, values.shape[1]), heads)
    total = values[:count]
    for h in range(1, heads):
        total = jnp.where(lane == h, values[h * count : (h + 1) * count], total)
    return total


def turned_order(width, heads):
    size = width // heads
    part = size // 8
    row = lax.broadcasted_iota(jnp.int32, (width, width), 0)
    col = lax.broadcasted_iota(jnp.int32, (width, width), 1)
    half, lane = col // (width // 2), col % (width // 2)
    head, j = lane // (size // 2), lane % (size // 2)
    rotated = j // part * 2 * part + j % part + half * part
    kept = 4 * part + j - 2 * part + half * 2 * part
    return jnp.where(row == head * size + jnp.where(j < 2 * part, rotated, kept), 1.0, 0.0).astype(BF16)


def halves(values):
    half = values.shape[1] // 2
    return values[:, :half], values[:, half:]


def head_of(shape, heads):
    half = shape[1] // 2
    return lax.broadcasted_iota(jnp.int32, shape, 1) % half // (half // heads)


def own_rows(values, count):
    edge = REACH * BAND
    return jnp.concatenate(
        [values[start + edge : start + edge + count] for start in range(0, values.shape[0], 2 * count)], axis=0
    )


def bands_of(ref, bands):
    parts = [
        ref[:, band * BAND : (band + 1) * BAND, :].astype(F32).reshape(-1, ref.shape[-1])
        for band in range(bands)
    ]
    return jnp.concatenate(parts, axis=0)


def pair_lanes(values, heads, pair):
    size = values.shape[1] // heads
    part = values[:, 128 * pair : 128 * pair + 128]
    lane = lax.broadcasted_iota(jnp.int32, part.shape, 1)
    return jnp.concatenate(
        [jnp.where(lane < size, part, 0.0), jnp.where(lane < size, 0.0, part)], axis=0
    ).astype(BF16)


def merge_pair(values, size):
    count = values.shape[0] // 2
    lane = lax.broadcasted_iota(jnp.int32, (count, 128), 1)
    return jnp.where(lane < size, values[:count], values[count:])


def close(shape, query_row, key_row):
    token = lax.broadcasted_iota(jnp.int32, shape, 0)
    place = lax.broadcasted_iota(jnp.int32, shape, 1)
    return (jnp.abs(token // BAND + query_row - place // BAND - key_row) <= REACH) & (
        jnp.abs(token % BAND - place % BAND) <= REACH
    )


def norm_scale(values):
    return lax.rsqrt(jnp.mean(values * values, axis=-1, keepdims=True) + EPS)


def place_parts(place, part_refs):
    for index, part in enumerate(part_refs):
        chip = place[1] ^ (index % 4)
        core = place[2] ^ (index // 4)
        group = part.shape[0]
        yield (chip * 2 + core) * group, part[...].astype(F32)


def store_rows(ref, start, rows):
    group, count, lanes = rows.shape
    ref[pl.ds(pl.multiple_of(start * count, group * count), group * count), :] = rows.reshape(
        group * count, lanes
    ).astype(ref.dtype)


def split_parts(place, values, mine_ref, other_ref, start):
    chips, group = mine_ref.shape[:2]
    count = values.shape[0] // (2 * chips)
    first = place[2] == 0
    for chip in range(chips):
        zero, one = [values[(2 * chip + core) * count : (2 * chip + core + 1) * count] for core in range(2)]
        for ref, part in ((mine_ref, jnp.where(first, zero, one)), (other_ref, jnp.where(first, one, zero))):
            part = part.reshape(group, count // group, values.shape[1])
            for i in range(count // group // 8):
                at = start + i * values.shape[1]
                ref[chip, :, :, at : at + values.shape[1]] = part[:, 8 * i : 8 * i + 8].astype(BF16)


def pack_kernel(
    per_canvas, place, cond_ref, qkv_ref, up_ref, out_ref, down_ref, attn_ref, feed_ref,
    near_ref, far_ref, cond_own_ref,
):
    own = attn_ref.shape[0]
    canvases, total = cond_ref.shape
    width = out_ref.shape[1]
    row = lax.broadcasted_iota(jnp.int32, (own, total), 0) + place[4] * own
    pick = jnp.where(row == lax.broadcasted_iota(jnp.int32, (own, total), 1), 1.0, 0.0).astype(BF16)
    cond = mm_rt(pick, cond_ref[...])
    cond_own_ref[...] = cond
    tails = []
    for canvas in range(canvases):
        lines = []
        for weight_ref in (attn_ref, feed_ref):
            line = jnp.sum(
                cond[:, canvas : canvas + 1] * weight_ref[...].astype(F32), axis=0, keepdims=True
            )
            high = line.astype(BF16).astype(F32)
            for part in (high, line - high):
                lines += [part[:, :128], part[:, 128:]]
        tails.append(jnp.concatenate(lines, axis=0))
    down = down_ref[...].astype(F32)
    parts = [up_ref[...], out_ref[...]] + [down[8 * i : 8 * i + 8].astype(BF16) for i in range(down.shape[0] // 8)]
    qkv = qkv_ref.shape[1]
    mine = place[0] == 0
    for ref, tail in (
        (near_ref, jnp.where(mine, tails[0], tails[1])),
        (far_ref, jnp.where(mine, tails[1], tails[0])),
    ):
        ref[:, :qkv] = qkv_ref[...]
        ref[:, qkv : qkv + 128] = tail.astype(BF16)
        at = qkv + 128
        for part in parts:
            ref[:, at : at + part.shape[1]] = part
            at += part.shape[1]


def line_kernel(order, place, p0, p1, p2, p3, line_ref):
    for index, part in zip((0,) + order, (p0, p1, p2, p3)):
        line_ref[place[3] ^ index] = part[...]


def core_sum_kernel(place, mine_ref, got_ref, *outs):
    for index, out_ref in enumerate(outs):
        chip = place[1] ^ (0, place[6], place[6] ^ 3, 3)[index]
        out_ref[...] = (mine_ref[chip].astype(F32) + got_ref[chip].astype(F32)).astype(BF16)


def join_kernel(one_ref, two_ref, out_ref):
    split = one_ref.shape[-1]
    out_ref[:, :, :split] = one_ref[...]
    out_ref[:, :, split:] = two_ref[...]


def pair_sum_kernel(one_ref, two_ref, out_ref):
    out_ref[...] = (one_ref[...].astype(F32) + two_ref[...].astype(F32)).astype(BF16)


def chip_sum_kernel(place, p0, p1, q0, q1, both, o0, o1, o2, o3, keep_ref):
    split = p0.shape[-1]
    keep_ref[:, :, :split] = p0[...].astype(F32) + p1[...].astype(F32) + both[:, :, :split].astype(F32)
    keep_ref[:, :, split:] = q0[...].astype(F32) + q1[...].astype(F32) + both[:, :, split:].astype(F32)
    for index, out_ref in enumerate((o0, o1, o2, o3)):
        out_ref[...] = keep_ref[place[3] ^ index].astype(out_ref.dtype)


def last_kernel(
    per_canvas, size, place, cond_ref, own_ref, three_ref, two_ref, one_ref,
    qkv_ref, out_ref, up_ref, down_ref, attn_ref, feed_ref, scale_ref,
):
    parts = [own_ref[...]] + [ref[...].astype(F32) for ref in (one_ref, two_ref, three_ref)]
    total = parts[0] + parts[1] + parts[2] + parts[3]
    width = out_ref.shape[1]
    at = up_ref.shape[1]
    up_ref[...] = total[:, :at]
    out_ref[...] = total[:, at : at + width]
    for i in range(down_ref.shape[0] // 8):
        at += width
        down_ref[8 * i : 8 * i + 8, :] = total[:, at : at + width]
    at += width
    qkv_ref[...] = total[:, at : at + qkv_ref.shape[1]]
    at += qkv_ref.shape[1]
    cond = cond_ref[...]
    attn, feed = 0.0, 0.0
    for canvas in range(cond.shape[1]):
        tail = jnp.zeros((8, 128), F32)
        for index, part in enumerate(parts):
            same = (place[3] ^ index) // per_canvas == canvas
            tail = tail + jnp.where(same, part[:, at:], 0.0)
        weight = cond[:, canvas : canvas + 1]
        attn = attn + weight * jnp.concatenate([tail[0:1], tail[1:2]], axis=1)
        feed = feed + weight * jnp.concatenate([tail[2:3], tail[3:4]], axis=1)
    attn_ref[...] = attn
    feed_ref[...] = feed
    tail = total[:, at:]
    scale = tail[4:5] + tail[5:6]
    for h in range(scale_ref.shape[0]):
        scale_ref[h] = scale[0, h * size]


def ready_kernel(
    heads, place, scale_ref, feat_ref, cot_ref, swap_ref, beside_ref, row_ref, col_ref, id_query_ref, id_key_ref,
    unit_ref, unit_turned_ref, own_turned_ref, cos_ref, sine_ref, mask_ref, inputs_ref, cot_out_ref, root_ref,
):
    rows, cols, width = feat_ref.shape
    count = rows * BAND
    bands = cols // BAND
    odd = place[5] == 1
    near = close((count, 2 * count), REACH, 0)
    lane = lax.broadcasted_iota(jnp.int32, (1, width // 2), 1) // (width // 2 // heads)
    root = jnp.zeros((1, width // 2), F32)
    for h in range(heads):
        root = jnp.where(lane == h, scale_ref[h], root)
    root_ref[...] = jnp.sqrt(root)
    inputs_ref[...] = bands_of(feat_ref, bands)
    cot_out_ref[...] = bands_of(cot_ref, bands).astype(BF16)
    for band in range(bands):
        part = slice(band * BAND, (band + 1) * BAND)
        swapped = swap_ref[:, part, :].astype(F32)
        beside = beside_ref[:, part, :].astype(F32)
        full = jnp.concatenate(
            [
                jnp.where(odd, swapped, beside),
                feat_ref[:, part, :].astype(F32),
                jnp.where(odd, beside, swapped),
                jnp.zeros((2, BAND, width), F32),
            ],
            axis=0,
        ).reshape(2 * count, width)
        span = slice(2 * band * count, 2 * (band + 1) * count)
        unit = full * norm_scale(full)
        unit_ref[span] = unit
        turned = jnp.transpose(unit).astype(BF16)
        unit_turned_ref[:, span] = turned
        own = slice(REACH * BAND, REACH * BAND + count)
        own_turned_ref[:, band * count : (band + 1) * count] = jnp.transpose(unit[own]).astype(BF16)
        for i, ref in enumerate((cos_ref, sine_ref)):
            ref[span] = (row_ref[i][:, None, :] + col_ref[i, part, :][None]).reshape(2 * count, width // 2)
        alike = id_query_ref[REACH * BAND : REACH * BAND + count, band : band + 1] == id_key_ref[
            band : band + 1, :
        ]
        mask_ref[band] = jnp.where(near & alike, 1.0, 0.0).astype(BF16)


def attend_kernel(
    heads, root_ref, unit_ref, cos_ref, sine_ref, mask_ref, sums, raw_ref,
    query_ref, key_ref, value_ref, raised_ref, mixed_ref, inverse_ref, along_q_ref, length_q_ref, along_k_ref, length_k_ref,
    gain_ref, gain_col_ref, w_ref,
):
    bands, count = mask_ref.shape[:2]
    width = unit_ref.shape[1]
    size = width // heads
    edge = REACH * BAND
    weight = raw_ref[...]
    order = turned_order(width, heads)
    turned = mm(
        jnp.concatenate([weight[:, :width], weight[:, width : 2 * width]], axis=0), order
    ).astype(BF16)
    w_ref[:, :width], w_ref[:, width : 2 * width] = turned[:width], turned[width:]
    w_ref[:, 2 * width :] = weight[:, 2 * width :]
    pairs = [sums[i : i + 2] + sums[i + 2 : i + 4] for i in (0, 4)]
    picked = 1.0 + jnp.concatenate(
        [jnp.concatenate([pair[0:1], pair[1:2]], axis=1) for pair in pairs], axis=0
    )
    gain_ref[...] = picked
    gain_col_ref[...] = jnp.transpose(jnp.broadcast_to(picked[0:1], (128, width)))
    root = root_ref[...]
    unit = unit_ref[...]
    normed = (unit * picked[0:1]).astype(BF16)
    value_ref[...] = mm(normed, weight[:, 2 * width :]).astype(BF16)
    ones_head = same_head(width // 2, size // 2)
    cos, sine = cos_ref[...], sine_ref[...]
    for i, ref in enumerate((query_ref, key_ref)):
        first, second = halves(mm(normed, turned[i * width : (i + 1) * width]))
        short = lax.rsqrt(mm((first * first + second * second).astype(BF16), ones_head) + EPS)
        length = short * root
        ref[...] = jnp.concatenate(
            [(first * cos - second * sine) * length, (second * cos + first * sine) * length], axis=1
        ).astype(BF16)
        along = jnp.concatenate([first * short, second * short], axis=1)
        if i == 0:
            along_q_ref[...], length_q_ref[...] = own_rows(along, count), own_rows(length, count)
        else:
            along_k_ref[...], length_k_ref[...] = along, length
    ones_half = jnp.ones((2 * count, 128), BF16)
    for band in range(bands):
        start = 2 * band * count
        query = query_ref[start + edge : start + edge + count, :].astype(F32)
        scores = mm_rt(stack_heads(query, heads), key_ref[start : start + 2 * count, :])
        raised = jnp.exp(scores).astype(BF16) * jnp.concatenate([mask_ref[band]] * heads, axis=0)
        raised_ref[band] = raised
        value = value_ref[start : start + 2 * count, :]
        span = slice(band * count, (band + 1) * count)
        for pair in range(heads // 2):
            lanes = slice(128 * pair, 128 * pair + 128)
            both = mm(
                raised[2 * pair * count : 2 * (pair + 1) * count],
                jnp.concatenate([value[:, lanes], ones_half], axis=1),
            )
            inverse = 1.0 / merge_pair(both[:, 128:], size)
            mixed_ref[span, lanes] = merge_pair(both[:, :128], size) * inverse
            inverse_ref[span, lanes] = inverse


def feed_kernel(
    heads, inputs_ref, cot_ref, w_up_ref, w_out_ref, gain_ref, mixed_ref, inverse_ref,
    middle_ref, middle_grad_ref, shrunk_ref, gain_grad_ref,
    w_down_ref, mixed_low_ref, normed_ref, gated_ref, d_exp_ref, branch_ref,
):
    width = inputs_ref.shape[1]
    hidden = w_down_ref.shape[0]
    w_up, w_out, w_down = w_up_ref[...], w_out_ref[...], w_down_ref[...]
    gain_feed = gain_ref[1:2]
    mixed = mixed_ref[...]
    mixed_low = mixed.astype(BF16)
    mixed_low_ref[...] = mixed_low
    middle = inputs_ref[...] + mm(mixed_low, w_out)
    middle_ref[...] = middle
    scale = norm_scale(middle)
    unit = middle * scale
    normed = (unit * gain_feed).astype(BF16)
    normed_ref[...] = normed
    cot = cot_ref[...].astype(F32)
    half = math.sqrt(0.5)
    density = 1.0 / math.sqrt(2.0 * math.pi)
    pulled = None
    for start in range(0, hidden, width):
        here = slice(start, start + width)
        there = slice(hidden + start, hidden + start + width)
        left = mm(normed, w_up[:, here])
        gate = mm(normed, w_up[:, there])
        d_gated = mm_rt(cot_ref[...], w_down[here])
        phi = 0.5 + 0.5 * lax.erf(gate * half)
        shaped = gate * phi
        gated_ref[:, here] = (left * shaped).astype(BF16)
        slope = phi + gate * (jnp.exp(gate * gate * -0.5) * density)
        d_left = (d_gated * shaped).astype(BF16)
        d_gate = (d_gated * left * slope).astype(BF16)
        d_exp_ref[:, here] = d_left
        d_exp_ref[:, there] = d_gate
        part = mm_rt(d_left, w_up[:, here]) + mm_rt(d_gate, w_up[:, there])
        pulled = part if pulled is None else pulled + part
    gain_grad_ref[...] = jnp.sum(pulled * unit, axis=0, keepdims=True)
    inner = pulled * gain_feed
    d_middle = cot + scale * (inner - unit * jnp.mean(unit * inner, axis=-1, keepdims=True))
    middle_grad_ref[...] = d_middle
    branch = d_middle.astype(BF16)
    branch_ref[...] = branch
    shrunk_ref[...] = (mm_rt(branch, w_out) * inverse_ref[...]).astype(BF16)


def weights_kernel(place, cot_ref, mixed_low_ref, normed_ref, gated_ref, d_exp_ref, branch_ref, mine_ref, other_ref):
    width, ups = cot_ref.shape[1], d_exp_ref.shape[1]
    split_parts(place, mm_lt(normed_ref[...], d_exp_ref[...]), mine_ref, other_ref, 0)
    split_parts(place, mm_lt(mixed_low_ref[...], branch_ref[...]), mine_ref, other_ref, ups)
    split_parts(place, mm_lt(gated_ref[...], cot_ref[...]), mine_ref, other_ref, ups + width)


def output_kernel(middle_ref, gated_ref, w_down_ref, out_ref):
    rows, cols, width = out_ref.shape
    total = (middle_ref[...] + mm(gated_ref[...], w_down_ref[...])).astype(BF16)
    count = rows * BAND
    for band in range(cols // BAND):
        out_ref[:, band * BAND : (band + 1) * BAND, :] = total[band * count : (band + 1) * count].reshape(
            rows, BAND, width
        )


def pull_head(grad, along, length, cos, sine, heads):
    first, second = halves(grad)
    along_first, along_second = halves(along)
    first, second = first * cos + second * sine, second * cos - first * sine
    ones_head = same_head(first.shape[1], first.shape[1] // heads)
    part = mm((along_first * first + along_second * second).astype(BF16), ones_head)
    grad = jnp.concatenate(
        [length * (first - along_first * part), length * (second - along_second * part)], axis=1
    )
    return grad.astype(BF16), jnp.sum(part, axis=0, keepdims=True)


def lane_sums(product):
    total = product[:, :128]
    for start in range(128, product.shape[1], 128):
        total = total + product[:, start : start + 128]
    return jnp.sum(jnp.transpose(total), axis=0, keepdims=True)


def normed_back_kernel(
    rows, place, w_ref, d_query_ref, d_rest_ref, own_ref, rim_swap_ref, rim_beside_ref
):
    width = own_ref.shape[1]
    count, edge = rows * BAND, REACH * BAND
    odd = place[5] == 1
    whole = mm_rt(d_rest_ref[...], w_ref[:, width:])
    own_ref[...] = mm_rt(d_query_ref[...], w_ref[:, :width]) + own_rows(whole, count)
    for band in range(whole.shape[0] // (2 * count)):
        start = 2 * band * count
        upper, lower = whole[start : start + edge], whole[start + edge + count : start + 2 * edge + count]
        here = slice(band * edge, (band + 1) * edge)
        rim_swap_ref[here] = jnp.where(odd, upper, lower).astype(BF16)
        rim_beside_ref[here] = jnp.where(odd, lower, upper).astype(BF16)


def features_kernel(place, inputs_ref, gain_ref, own_ref, rim_swap_ref, rim_beside_ref, middle_grad_ref, grad_ref):
    rows, cols, width = grad_ref.shape
    bands = cols // BAND
    count, edge = rows * BAND, REACH * BAND
    odd = place[5] == 1
    zeros = jnp.zeros((count - 2 * edge, width), F32)
    rims = []
    for band in range(bands):
        here = slice(band * edge, (band + 1) * edge)
        swapped, beside = rim_swap_ref[here].astype(F32), rim_beside_ref[here].astype(F32)
        rims += [jnp.where(odd, swapped, beside), zeros, jnp.where(odd, beside, swapped)]
    inner = (own_ref[...] + jnp.concatenate(rims, axis=0)) * gain_ref[0:1]
    inputs = inputs_ref[...]
    scale = norm_scale(inputs)
    unit = inputs * scale
    grad = middle_grad_ref[...] + scale * (inner - unit * jnp.mean(unit * inner, axis=-1, keepdims=True))
    for band in range(bands):
        grad_ref[:, band * BAND : (band + 1) * BAND, :] = grad[band * count : (band + 1) * count].reshape(
            rows, BAND, width
        )


def forward_kernel(
    heads, place, root_ref, unit_ref, cos_ref, sine_ref, mask_ref, inputs_ref, cot_ref,
    p0, p1, p2, p3, p4, p5, p6, p7,
    query_ref, key_ref, value_ref, raised_ref, mixed_ref, along_q_ref, length_q_ref, along_k_ref, length_k_ref,
    gain_ref, gain_col_ref, w_ref, middle_ref, middle_grad_ref, shrunk_ref, gain_grad_ref,
    w_down_ref, gated_ref, mine_ref, other_ref,
    inverse_ref, raw_ref, w_up_ref, w_out_ref, mixed_low_ref, normed_ref, d_exp_ref, branch_ref,
):
    width = inputs_ref.shape[1]
    first, ups = 3 * width + 128, w_up_ref.shape[1]
    sums = jnp.zeros((8, 128), F32)
    for start, rows in place_parts(place, (p0, p1, p2, p3, p4, p5, p6, p7)):
        store_rows(raw_ref, start, rows[:, :, : 3 * width])
        sums = sums + jnp.sum(rows[:, :, 3 * width : first], axis=0)
        store_rows(w_up_ref, start, rows[:, :, first : first + ups])
        store_rows(w_out_ref, start, rows[:, :, first + ups : first + ups + width])
        down = [rows[:, :, at : at + width] for at in range(first + ups + width, rows.shape[2], width)]
        store_rows(w_down_ref, start, jnp.concatenate(down, axis=1))
    attend_kernel(
        heads, root_ref, unit_ref, cos_ref, sine_ref, mask_ref, sums, raw_ref,
        query_ref, key_ref, value_ref, raised_ref, mixed_ref, inverse_ref,
        along_q_ref, length_q_ref, along_k_ref, length_k_ref, gain_ref, gain_col_ref, w_ref,
    )
    feed_kernel(
        heads, inputs_ref, cot_ref, w_up_ref, w_out_ref, gain_ref, mixed_ref, inverse_ref,
        middle_ref, middle_grad_ref, shrunk_ref, gain_grad_ref,
        w_down_ref, mixed_low_ref, normed_ref, gated_ref, d_exp_ref, branch_ref,
    )
    weights_kernel(
        place, cot_ref, mixed_low_ref, normed_ref, gated_ref, d_exp_ref, branch_ref, mine_ref, other_ref
    )


def backward_kernel(
    heads, rows, place, root_ref, shrunk_ref, mixed_ref, raised_ref, query_ref, key_ref, value_ref,
    cos_ref, sine_ref, w_ref, gain_col_ref, unit_turned_ref, own_turned_ref, along_q_ref, length_q_ref,
    along_k_ref, length_k_ref, gain_grad_ref,
    d_query_ref, d_rest_ref, mine_ref, other_ref,
):
    bands, _, keys = raised_ref.shape
    count, edge = keys // 2, REACH * BAND
    width = shrunk_ref.shape[1]
    ones_half = jnp.ones((keys, 128), BF16)
    along_total = jnp.zeros((1, width // 2), F32)
    for band in range(bands):
        span = slice(band * count, (band + 1) * count)
        start = band * keys
        whole = slice(start, start + keys)
        own = slice(start + edge, start + edge + count)
        shrunk = shrunk_ref[span].astype(F32)
        level_rows = -(shrunk * mixed_ref[span])
        value = value_ref[whole, :]
        raised = raised_ref[band]
        parts, stacks = [], []
        for pair in range(heads // 2):
            lanes = slice(128 * pair, 128 * pair + 128)
            stacks.append(pair_lanes(shrunk, heads, pair))
            parts.append(
                mm_rt(
                    jnp.concatenate([stacks[-1], pair_lanes(level_rows, heads, pair)], axis=1),
                    jnp.concatenate([value[:, lanes], ones_half], axis=1),
                )
            )
        d_scores = (raised.astype(F32) * jnp.concatenate(parts, axis=0)).astype(BF16)
        query = query_ref[own, :].astype(F32)
        d_key = mm_lt(d_scores, stack_heads(query, heads))
        d_query = fold_heads(mm(d_scores, key_ref[whole, :]), heads)
        for pair in range(heads // 2):
            lanes = slice(width + 128 * pair, width + 128 * pair + 128)
            d_value = mm_lt(raised[2 * pair * count : 2 * (pair + 1) * count], stacks[pair])
            d_rest_ref[whole, lanes] = d_value.astype(BF16)
        d_rest_ref[whole, :width], along_k = pull_head(
            d_key, along_k_ref[whole, :], length_k_ref[whole, :], cos_ref[whole, :], sine_ref[whole, :], heads
        )
        d_query_ref[span, :], along_q = pull_head(
            d_query, along_q_ref[span, :], length_q_ref[span, :], cos_ref[own, :], sine_ref[own, :], heads
        )
        along_total = along_total + along_k + along_q
    plain = jnp.concatenate(
        [mm(own_turned_ref[...], d_query_ref[...]), mm(unit_turned_ref[...], d_rest_ref[...])], axis=1
    )
    scaled = plain * jnp.concatenate([gain_col_ref[...]] * (3 * width // 128), axis=1)
    turned = jnp.concatenate([scaled[:, :width], scaled[:, width : 2 * width]], axis=0).astype(BF16)
    plain_order = mm_rt(turned, turned_order(width, heads))
    split_parts(place, plain_order[:width], mine_ref, other_ref, 0)
    split_parts(place, plain_order[width:], mine_ref, other_ref, width)
    split_parts(place, scaled[:, 2 * width :], mine_ref, other_ref, 2 * width)
    lines = []
    for total in (lane_sums(plain * w_ref[...].astype(F32)), gain_grad_ref[...]):
        lines += [total[:, :128], total[:, 128:]]
    total = along_total * 0.5 / root_ref[...]
    high = total.astype(BF16).astype(F32)
    lines += [high, total - high, jnp.zeros((2, 128), F32)]
    tail = jnp.concatenate(lines, axis=0).astype(BF16)
    for ref in (mine_ref, other_ref):
        ref[:, :, :, 3 * width :] = jnp.broadcast_to(tail[None, None], ref.shape[:2] + tail.shape)


def call(kernel, outs, scratch=(), place=None, smem=0, smem_out=0, flops=10**9, pin=True, aliases=None):
    if place is not None:
        kernel = functools.partial(kernel, place)

    def run(*args):
        args = [
            arg if i < smem else pltpu.with_memory_space_constraint(arg, pltpu.VMEM if pin else pltpu.HBM)
            for i, arg in enumerate(args)
        ]
        return pl.pallas_call(
            kernel,
            out_shape=outs,
            in_specs=[
                pl.BlockSpec(memory_space=pltpu.SMEM if i < smem else pltpu.VMEM)
                for i in range(len(args))
            ],
            out_specs=[
                pl.BlockSpec(memory_space=pltpu.SMEM if i >= len(outs) - smem_out else pltpu.VMEM)
                for i in range(len(outs))
            ],
            scratch_shapes=list(scratch),
            input_output_aliases=aliases or {},
            compiler_params=pltpu.CompilerParams(vmem_limit_bytes=VMEM_LIMIT),
            cost_estimate=pl.CostEstimate(flops=flops, bytes_accessed=4 * 10**6 if flops > 1 else 1, transcendentals=0),
        )(*args)

    return run


def rotation_tables(row_place, col_place, heads, size):
    part = size // 8
    lane = jnp.arange(heads * size // 2) % (size // 2)
    index = (lane % part).astype(F32)
    frequency = math.pi / 8.0 * jnp.exp(index * (-math.log(10.0) / part))
    group = lane // part

    def table(place, kind):
        angle = place.astype(F32)[:, None] * frequency
        cos = jnp.where(group == kind, jnp.cos(angle), 0.0)
        if kind:
            cos = jnp.where(group >= 2, 1.0, cos)
        return jnp.stack([cos, jnp.where(group == kind, jnp.sin(angle), 0.0)])

    return table(row_place, 0), table(col_place, 1)


def window_ids(crop_ids, row_start, rows):
    ids = jnp.pad(crop_ids[:, ::BAND], ((REACH, 2 * rows), (0, 0)), constant_values=-1)
    ids = lax.dynamic_slice_in_dim(ids, row_start, 2 * rows, 0)
    return jnp.repeat(ids, BAND, axis=0), jnp.repeat(ids.T, BAND, axis=1)


def on_device(
    features, crop_ids, conditioning, qkv_weight, out_weight, up_weight, down_weight,
    attn_cond_weight, feed_cond_weight, attention_scale, cotangent,
):
    rows, cols, width = features.shape
    heads = attention_scale.shape[0]
    size = width // heads
    bands = cols // BAND
    count = rows * BAND
    tokens = rows * cols
    edge = REACH * BAND
    n_rows, n_cols = lax.axis_size("rows"), lax.axis_size("cols")
    devices = n_rows * n_cols
    hidden = down_weight.shape[0] * devices
    own_cond = attn_cond_weight.shape[0]
    canvases = conditioning.shape[0]
    row, col = lax.axis_index("rows"), lax.axis_index("cols")
    row_start, col_start = row * rows, col * cols
    canvas = col_start // CANVAS
    group, chips = 4, 4
    chunks = 2 * chips * group
    direct = (n_rows, n_cols) == (2 * chips, group) and chunks * 8 == width
    first_lanes = 3 * width + 128
    second_lanes = 2 * hidden + width + hidden * width // (8 * chunks)
    per_canvas = max(n_cols // canvases, 1)
    place = Place(direct, cols, n_cols)

    def result(*dims, dtype=F32):
        return jax.ShapeDtypeStruct(dims, dtype)

    def shape(*dims, dtype=F32):
        return pltpu.VMEM(dims, dtype)

    def low(*dims):
        return shape(*dims, dtype=BF16)

    def over(axis, by):
        size_of = lax.axis_size(axis)
        return lambda value: lax.ppermute(value, axis, [(i, i ^ by) for i in range(size_of)])

    z_moves = [over("cols", k) for k in range(1, group)]
    xy_moves = [over("rows", 2 * m) for m in range(1, chips)]

    def chip_pairs(step):
        return [(i, i ^ (4 if i % 2 == step else 2)) for i in range(n_rows)]

    def first_chip(value):
        return lax.ppermute(value, "rows", chip_pairs(0))

    def second_chip(value):
        return lax.ppermute(value, "rows", chip_pairs(1))

    core_move = over("rows", 1)

    if direct:
        near, far, cond_own = call(
            functools.partial(pack_kernel, per_canvas),
            [
                low(8, first_lanes + second_lanes),
                low(8, first_lanes + second_lanes),
                shape(own_cond, canvases),
            ],
            place=place,
            pin=False,
        )(conditioning, qkv_weight, up_weight, out_weight, down_weight, attn_cond_weight, feed_cond_weight)
        z_order = (3, 1, 2)
        line = call(functools.partial(line_kernel, z_order), [low(group, 8, first_lanes + second_lanes)], place=place)(
            near,
            *[z_moves[k - 1](near if k // per_canvas == 0 else far) for k in z_order],
        )[0]
        mine = [line] + [move(line) for move in xy_moves]
    else:
        def parts_of(full):
            full = full.reshape(chips, 2, group, 8, full.shape[-1])
            return [full[m, core] for core in range(2) for m in range(chips)]

        def whole(weight):
            return lax.all_gather(weight, AXES, axis=0, tiled=True)

        cond = lax.dynamic_slice_in_dim(conditioning, place[4] * own_cond, own_cond, 1)
        cond_own = cond.T.astype(F32)
        sums = [
            lax.psum(jnp.dot(cond, weight, preferred_element_type=F32), AXES)
            for weight in (attn_cond_weight, feed_cond_weight)
        ]
        lines = []
        for part in sums:
            part = lax.dynamic_slice_in_dim(part, canvas, 1, 0).reshape(-1, 128)
            high = lax.reduce_precision(part, 8, 7)
            lines += [high, part - high]
        lines = jnp.pad(jnp.concatenate(lines).astype(BF16), ((0, width - 8), (0, 0)))
        down = whole(down_weight).reshape(chunks, -1, 8, width).transpose(0, 2, 1, 3).reshape(width, -1)
        parts = parts_of(
            jnp.concatenate([whole(qkv_weight), lines, whole(up_weight), whole(out_weight), down], axis=1)
        )

    odd = row % 2 == 1
    beside_pairs = [(i, (i + 1 if i % 2 else i - 1) % n_rows) for i in range(n_rows)]

    def beside_move(value):
        return lax.ppermute(value, "rows", beside_pairs)

    first_rows, last_rows = features[:REACH], features[rows - REACH :]
    halo_swap = core_move(jnp.where(odd, first_rows, last_rows))
    halo_beside = beside_move(jnp.where(odd, last_rows, first_rows))

    row_place = row_start - REACH + jnp.arange(2 * rows, dtype=jnp.int32)
    col_place = (col_start + jnp.arange(cols, dtype=jnp.int32)) % CANVAS
    row_table, col_table = rotation_tables(row_place, col_place, heads, size)
    id_query, id_key = window_ids(crop_ids, row_start, rows)

    unit, unit_turned, own_turned, cos, sine, mask, inputs, cot, root = call(
        functools.partial(ready_kernel, heads),
        [
            shape(2 * tokens, width),
            low(width, 2 * tokens),
            low(width, tokens),
            shape(2 * tokens, width // 2),
            shape(2 * tokens, width // 2),
            low(bands, count, 2 * count),
            shape(tokens, width),
            low(tokens, width),
            shape(1, width // 2),
        ],
        place=place,
        smem=1,
    )(attention_scale, features, cotangent, halo_swap, halo_beside, row_table, col_table, id_query, id_key)
    if direct:
        mine = mine[:1] + [lax.optimization_barrier((part, unit))[0] for part in mine[1:]]
        far = core_move(mine[3])
        for i in (1, 2):
            mine[i], far = lax.optimization_barrier((mine[i], far))
        parts = mine + [core_move(part) for part in mine[:3]] + [far]

    (
        query, key, value, raised, mixed, along_q, length_q, along_k, length_k, gain, gain_col, w_qkv,
        middle, middle_grad, shrunk, gain_grad, w_down, gated, mine_second, other_second,
    ) = call(
        functools.partial(forward_kernel, heads),
        [
            low(2 * tokens, width),
            low(2 * tokens, width),
            low(2 * tokens, width),
            low(bands, heads * count, 2 * count),
            shape(tokens, width),
            shape(tokens, width),
            shape(tokens, width // 2),
            shape(2 * tokens, width),
            shape(2 * tokens, width // 2),
            shape(2, width),
            shape(width, 128),
            low(width, 3 * width),
            shape(tokens, width),
            shape(tokens, width),
            low(tokens, width),
            shape(1, width),
            low(hidden, width),
            low(tokens, hidden),
            low(chips, group, 8, second_lanes),
            low(chips, group, 8, second_lanes),
        ],
        scratch=[
            pltpu.VMEM((tokens, width), F32),
            pltpu.VMEM((width, 3 * width), BF16),
            pltpu.VMEM((width, 2 * hidden), BF16),
            pltpu.VMEM((width, width), BF16),
            pltpu.VMEM((tokens, width), BF16),
            pltpu.VMEM((tokens, width), BF16),
            pltpu.VMEM((tokens, 2 * hidden), BF16),
            pltpu.VMEM((tokens, width), BF16),
        ],
        place=place,
    )(root, unit, cos, sine, mask, inputs, cot, *parts)

    d_query, d_rest, mine_first, other_first = call(
        functools.partial(backward_kernel, heads, rows),
        [
            low(tokens, width),
            low(2 * tokens, 2 * width),
            low(chips, group, 8, first_lanes),
            low(chips, group, 8, first_lanes),
        ],
        place=place,
        flops=1,
    )(
        root, shrunk, mixed, raised, query, key, value, cos, sine, w_qkv, gain_col, unit_turned, own_turned,
        along_q, length_q, along_k, length_k, gain_grad,
    )

    def last_output(gated):
        return call(output_kernel, [result(rows, cols, width, dtype=BF16)])(middle, gated, w_down)[0]

    def normed_back(d_query, d_rest):
        return call(
            functools.partial(normed_back_kernel, rows),
            [shape(tokens, width), low(bands * edge, width), low(bands * edge, width)],
            place=place,
        )(w_qkv, d_query, d_rest)

    def last_features(own, rim_swap, rim_beside):
        return call(features_kernel, [result(rows, cols, width)], place=place)(
            inputs, gain, own, rim_swap, rim_beside, middle_grad
        )[0]

    if direct:
        all_lanes = second_lanes + first_lanes
        def core_sum(mine, got):
            return call(core_sum_kernel, [low(group, 8, mine.shape[-1]) for _ in range(chips)], place=place)(mine, got)

        def pair_sum(one, two):
            return call(pair_sum_kernel, [low(*one.shape)], flops=1)(one, two)[0]

        first_got = core_move(other_first)
        second_own, second_near, second_beside, second_far = core_sum(mine_second, core_move(other_second))
        second_far = second_chip(second_far)
        first_own, first_near, first_beside, first_far = core_sum(mine_first, first_got)
        first_far = second_chip(first_far)
        second_far, first_far = lax.optimization_barrier((second_far, first_far))
        first_own, d_rest = lax.optimization_barrier((first_own, d_rest))
        beside = second_chip(call(join_kernel, [low(group, 8, all_lanes)], flops=1)(second_beside, first_beside)[0])
        sums = [
            second_own,
            first_chip(pair_sum(second_near, second_far)),
            first_own,
            first_chip(pair_sum(first_near, first_far)),
            beside,
        ]
        own_grad, rim_swap, rim_beside = normed_back(d_query, d_rest)
        rim_swap, rim_beside = core_move(rim_swap), beside_move(rim_beside)
        blocks = call(
            chip_sum_kernel,
            [shape(8, all_lanes)] + [low(8, all_lanes) for _ in z_moves],
            scratch=[pltpu.VMEM((group, 8, all_lanes), F32)],
            place=place,
        )(*sums)
        blocks, gated, own_grad = lax.optimization_barrier((blocks, gated, own_grad))
        output = last_output(gated)
        grad_features = last_features(own_grad, rim_swap, rim_beside)
        grad_qkv, grad_out, grad_up, grad_down, grad_attn_cond, grad_feed_cond, grad_scale = call(
            functools.partial(last_kernel, per_canvas, size // 2),
            [
                result(8, 3 * width),
                result(8, width),
                result(8, 2 * hidden),
                result(hidden // chunks, width),
                result(own_cond, width),
                result(own_cond, width),
                result(heads),
            ],
            place=place,
            smem_out=1,
        )(cond_own, blocks[0], *[move(block) for move, block in reversed(list(zip(z_moves, blocks[1:])))])
    else:
        own_grad, rim_swap, rim_beside = normed_back(d_query, d_rest)
        grad_features = last_features(own_grad, core_move(rim_swap), beside_move(rim_beside))
        output = last_output(gated)

        def joined(mine, other):
            return jnp.stack([mine, other], axis=1).astype(F32).reshape(chunks, 8, mine.shape[-1])

        def scattered(grad):
            return lax.psum_scatter(grad.reshape(-1, grad.shape[-1]), AXES, scatter_dimension=0, tiled=True)

        last = joined(mine_first, other_first)
        second = joined(mine_second, other_second)
        ups = 2 * hidden
        grad_qkv = scattered(last[:, :, : 3 * width])
        grad_up = scattered(second[:, :, :ups])
        grad_out = scattered(second[:, :, ups : ups + width])
        grad_down = scattered(
            second[:, :, ups + width :].reshape(chunks, 8, -1, width).transpose(0, 2, 1, 3)
        )
        spot = (jnp.arange(canvases) == canvas).astype(F32)[:, None, None]
        tail = lax.psum(spot * last[0, :, 3 * width :][None], AXES)

        def cond_grad(sums):
            return jnp.sum(cond_own[:, :, None] * sums.reshape(canvases, width)[None], axis=1)

        grad_attn_cond = cond_grad(tail[:, 0:2])
        grad_feed_cond = cond_grad(tail[:, 2:4])
        grad_scale = jnp.sum(tail[:, 4] + tail[:, 5], axis=0)[:: size // 2]
    return (
        output, grad_features, grad_qkv, grad_out, grad_up, grad_down, grad_attn_cond, grad_feed_cond, grad_scale,
    )


def solution(mesh):
    tile, whole, split = P("rows", "cols", None), P(), P(AXES, None)
    return jax.shard_map(
        on_device,
        mesh=mesh,
        in_specs=(tile, P(None, "cols"), whole, split, split, split, split, split, split, whole, tile),
        out_specs=(tile, tile, split, split, split, split, split, split, whole),
        check_vma=False,
    )
```

```python
import functools
import math

import jax
import jax.numpy as jnp
from jax import lax
from jax.experimental import pallas as pl
from jax.experimental.pallas import tpu as pltpu
from jax.sharding import PartitionSpec as P

CANVAS = 128
BAND = 16
REACH = 3
AXES = ("rows", "cols")
F32 = jnp.float32
BF16 = jnp.bfloat16
EPS = 1e-06
VMEM_LIMIT = 32 * 1024 * 1024


class Place:
    def __init__(self, direct, cols, n_cols):
        self.direct, self.cols, self.n_cols = direct, cols, n_cols

    def __getitem__(self, item):
        row, col = lax.axis_index("rows"), lax.axis_index("cols")
        if item == 0:
            return col * self.cols // CANVAS
        if item == 4:
            return row * self.n_cols + col
        if item == 5:
            return lax.rem(row, 2)
        if not self.direct:
            return (0, 0, 0, 0, 0, 0, 1)[item]
        return (None, row // 2, lax.rem(row, 2), col, None, None, 2 - lax.rem(row, 2))[item]


def mm(left, right):
    return lax.dot_general(left, right, (((1,), (0,)), ((), ())), preferred_element_type=F32)


def mm_rt(left, right):
    return lax.dot_general(left, right, (((1,), (1,)), ((), ())), preferred_element_type=F32)


def mm_lt(left, right):
    return lax.dot_general(left, right, (((0,), (0,)), ((), ())), preferred_element_type=F32)


def same_head(width, size):
    first = lax.broadcasted_iota(jnp.int32, (width, width), 0) // size
    second = lax.broadcasted_iota(jnp.int32, (width, width), 1) // size
    return jnp.where(first == second, 1.0, 0.0).astype(BF16)


def stack_heads(values, heads):
    lane = head_of(values.shape, heads)
    return jnp.concatenate(
        [jnp.where(lane == h, values, 0.0).astype(BF16) for h in range(heads)], axis=0
    )


def fold_heads(values, heads):
    count = values.shape[0] // heads
    lane = head_of((count, values.shape[1]), heads)
    total = values[:count]
    for h in range(1, heads):
        total = jnp.where(lane == h, values[h * count : (h + 1) * count], total)
    return total


def turned_order(width, heads):
    size = width // heads
    part = size // 8
    row = lax.broadcasted_iota(jnp.int32, (width, width), 0)
    col = lax.broadcasted_iota(jnp.int32, (width, width), 1)
    half, lane = col // (width // 2), col % (width // 2)
    head, j = lane // (size // 2), lane % (size // 2)
    rotated = j // part * 2 * part + j % part + half * part
    kept = 4 * part + j - 2 * part + half * 2 * part
    return jnp.where(row == head * size + jnp.where(j < 2 * part, rotated, kept), 1.0, 0.0).astype(BF16)


def halves(values):
    half = values.shape[1] // 2
    return values[:, :half], values[:, half:]


def head_of(shape, heads):
    half = shape[1] // 2
    return lax.broadcasted_iota(jnp.int32, shape, 1) % half // (half // heads)


def own_rows(values, count):
    edge = REACH * BAND
    return jnp.concatenate(
        [values[start + edge : start + edge + count] for start in range(0, values.shape[0], 2 * count)], axis=0
    )


def bands_of(ref, bands):
    parts = [
        ref[:, band * BAND : (band + 1) * BAND, :].astype(F32).reshape(-1, ref.shape[-1])
        for band in range(bands)
    ]
    return jnp.concatenate(parts, axis=0)


def pair_lanes(values, heads, pair):
    size = values.shape[1] // heads
    part = values[:, 128 * pair : 128 * pair + 128]
    lane = lax.broadcasted_iota(jnp.int32, part.shape, 1)
    return jnp.concatenate(
        [jnp.where(lane < size, part, 0.0), jnp.where(lane < size, 0.0, part)], axis=0
    ).astype(BF16)


def merge_pair(values, size):
    count = values.shape[0] // 2
    lane = lax.broadcasted_iota(jnp.int32, (count, 128), 1)
    return jnp.where(lane < size, values[:count], values[count:])


def close(shape, query_row, key_row):
    token = lax.broadcasted_iota(jnp.int32, shape, 0)
    place = lax.broadcasted_iota(jnp.int32, shape, 1)
    return (jnp.abs(token // BAND + query_row - place // BAND - key_row) <= REACH) & (
        jnp.abs(token % BAND - place % BAND) <= REACH
    )


def norm_scale(values):
    return lax.rsqrt(jnp.mean(values * values, axis=-1, keepdims=True) + EPS)


def place_parts(place, part_refs):
    for index, part in enumerate(part_refs):
        chip = place[1] ^ (index % 4)
        core = place[2] ^ (index // 4)
        group = part.shape[0]
        yield (chip * 2 + core) * group, part[...].astype(F32)


def store_rows(ref, start, rows):
    group, count, lanes = rows.shape
    ref[pl.ds(pl.multiple_of(start * count, group * count), group * count), :] = rows.reshape(
        group * count, lanes
    ).astype(ref.dtype)


def split_parts(place, values, mine_ref, other_ref, start):
    chips, group = mine_ref.shape[:2]
    count = values.shape[0] // (2 * chips)
    first = place[2] == 0
    for chip in range(chips):
        zero, one = [values[(2 * chip + core) * count : (2 * chip + core + 1) * count] for core in range(2)]
        for ref, part in ((mine_ref, jnp.where(first, zero, one)), (other_ref, jnp.where(first, one, zero))):
            part = part.reshape(group, count // group, values.shape[1])
            for i in range(count // group // 8):
                at = start + i * values.shape[1]
                ref[chip, :, :, at : at + values.shape[1]] = part[:, 8 * i : 8 * i + 8].astype(BF16)


def pack_kernel(
    heads, per_canvas, place, cond_ref, qkv_ref, up_ref, out_ref, down_ref, attn_ref, feed_ref,
    near_ref, far_ref, cond_own_ref,
):
    own = attn_ref.shape[0]
    canvases, total = cond_ref.shape
    width = out_ref.shape[1]
    row = lax.broadcasted_iota(jnp.int32, (own, total), 0) + place[4] * own
    pick = jnp.where(row == lax.broadcasted_iota(jnp.int32, (own, total), 1), 1.0, 0.0).astype(BF16)
    cond = mm_rt(pick, cond_ref[...])
    cond_own_ref[...] = cond
    tails = []
    for canvas in range(canvases):
        lines = []
        for weight_ref in (attn_ref, feed_ref):
            line = jnp.sum(
                cond[:, canvas : canvas + 1] * weight_ref[...].astype(F32), axis=0, keepdims=True
            )
            high = line.astype(BF16).astype(F32)
            for part in (high, line - high):
                lines += [part[:, :128], part[:, 128:]]
        tails.append(jnp.concatenate(lines, axis=0))
    down = down_ref[...].astype(F32)
    parts = [up_ref[...], out_ref[...]] + [down[8 * i : 8 * i + 8].astype(BF16) for i in range(down.shape[0] // 8)]
    qkv = qkv_ref.shape[1]
    turned = mm(
        jnp.concatenate([qkv_ref[:, :width], qkv_ref[:, width : 2 * width]], axis=0).astype(F32).astype(BF16),
        turned_order(width, heads),
    ).astype(BF16)
    mine = place[0] == 0
    for ref, tail in (
        (near_ref, jnp.where(mine, tails[0], tails[1])),
        (far_ref, jnp.where(mine, tails[1], tails[0])),
    ):
        ref[:, :width], ref[:, width : 2 * width] = turned[:8], turned[8:]
        ref[:, 2 * width : qkv] = qkv_ref[:, 2 * width :]
        ref[:, qkv : qkv + 128] = tail.astype(BF16)
        at = qkv + 128
        for part in parts:
            ref[:, at : at + part.shape[1]] = part
            at += part.shape[1]


def line_kernel(order, place, p0, p1, p2, p3, line_ref):
    for index, part in zip((0,) + order, (p0, p1, p2, p3)):
        line_ref[place[3] ^ index] = part[...]


def core_sum_kernel(place, mine_ref, got_ref, *outs):
    for index, out_ref in enumerate(outs):
        chip = place[1] ^ (0, place[6], place[6] ^ 3, 3)[index]
        out_ref[...] = (mine_ref[chip].astype(F32) + got_ref[chip].astype(F32)).astype(BF16)


def join_kernel(one_ref, two_ref, out_ref):
    split = one_ref.shape[-1]
    out_ref[:, :, :split] = one_ref[...]
    out_ref[:, :, split:] = two_ref[...]


def pair_sum_kernel(one_ref, two_ref, out_ref):
    out_ref[...] = (one_ref[...].astype(F32) + two_ref[...].astype(F32)).astype(BF16)


def chip_sum_kernel(place, p0, p1, q0, q1, both, o0, o1, o2, o3, keep_ref):
    split = p0.shape[-1]
    keep_ref[:, :, :split] = p0[...].astype(F32) + p1[...].astype(F32) + both[:, :, :split].astype(F32)
    keep_ref[:, :, split:] = q0[...].astype(F32) + q1[...].astype(F32) + both[:, :, split:].astype(F32)
    for index, out_ref in enumerate((o0, o1, o2, o3)):
        out_ref[...] = keep_ref[place[3] ^ index].astype(out_ref.dtype)


def last_kernel(
    per_canvas, size, place, cond_ref, own_ref, three_ref, two_ref, one_ref,
    qkv_ref, out_ref, up_ref, down_ref, attn_ref, feed_ref, scale_ref,
):
    parts = [own_ref[...]] + [ref[...].astype(F32) for ref in (one_ref, two_ref, three_ref)]
    total = parts[0] + parts[1] + parts[2] + parts[3]
    width = out_ref.shape[1]
    at = up_ref.shape[1]
    up_ref[...] = total[:, :at]
    out_ref[...] = total[:, at : at + width]
    for i in range(down_ref.shape[0] // 8):
        at += width
        down_ref[8 * i : 8 * i + 8, :] = total[:, at : at + width]
    at += width
    qkv_ref[...] = total[:, at : at + qkv_ref.shape[1]]
    at += qkv_ref.shape[1]
    cond = cond_ref[...]
    attn, feed = 0.0, 0.0
    for canvas in range(cond.shape[1]):
        tail = jnp.zeros((8, 128), F32)
        for index, part in enumerate(parts):
            same = (place[3] ^ index) // per_canvas == canvas
            tail = tail + jnp.where(same, part[:, at:], 0.0)
        weight = cond[:, canvas : canvas + 1]
        attn = attn + weight * jnp.concatenate([tail[0:1], tail[1:2]], axis=1)
        feed = feed + weight * jnp.concatenate([tail[2:3], tail[3:4]], axis=1)
    attn_ref[...] = attn
    feed_ref[...] = feed
    tail = total[:, at:]
    scale = tail[4:5] + tail[5:6]
    for h in range(scale_ref.shape[0]):
        scale_ref[h] = scale[0, h * size]


def ready_kernel(
    heads, place, scale_ref, feat_ref, cot_ref, swap_ref, beside_ref, row_ref, col_ref, id_query_ref, id_key_ref,
    unit_ref, unit_turned_ref, own_turned_ref, cos_ref, sine_ref, mask_ref, inputs_ref, cot_out_ref, root_ref,
):
    rows, cols, width = feat_ref.shape
    count = rows * BAND
    bands = cols // BAND
    odd = place[5] == 1
    near = close((count, 2 * count), REACH, 0)
    lane = lax.broadcasted_iota(jnp.int32, (1, width // 2), 1) // (width // 2 // heads)
    root = jnp.zeros((1, width // 2), F32)
    for h in range(heads):
        root = jnp.where(lane == h, scale_ref[h], root)
    root_ref[...] = jnp.sqrt(root)
    inputs_ref[...] = bands_of(feat_ref, bands)
    cot_out_ref[...] = bands_of(cot_ref, bands).astype(BF16)
    for band in range(bands):
        part = slice(band * BAND, (band + 1) * BAND)
        swapped = swap_ref[:, part, :].astype(F32)
        beside = beside_ref[:, part, :].astype(F32)
        full = jnp.concatenate(
            [
                jnp.where(odd, swapped, beside),
                feat_ref[:, part, :].astype(F32),
                jnp.where(odd, beside, swapped),
                jnp.zeros((2, BAND, width), F32),
            ],
            axis=0,
        ).reshape(2 * count, width)
        span = slice(2 * band * count, 2 * (band + 1) * count)
        unit = full * norm_scale(full)
        unit_ref[span] = unit
        turned = jnp.transpose(unit).astype(BF16)
        unit_turned_ref[:, span] = turned
        own = slice(REACH * BAND, REACH * BAND + count)
        own_turned_ref[:, band * count : (band + 1) * count] = jnp.transpose(unit[own]).astype(BF16)
        for i, ref in enumerate((cos_ref, sine_ref)):
            ref[span] = (row_ref[i][:, None, :] + col_ref[i, part, :][None]).reshape(2 * count, width // 2)
        alike = id_query_ref[REACH * BAND : REACH * BAND + count, band : band + 1] == id_key_ref[
            band : band + 1, :
        ]
        mask_ref[band] = jnp.where(near & alike, 1.0, 0.0).astype(BF16)


def attend_kernel(
    heads, root_ref, unit_ref, cos_ref, sine_ref, mask_ref, sums, w_ref,
    query_ref, key_ref, value_ref, raised_ref, mixed_ref, inverse_ref, along_q_ref, length_q_ref, along_k_ref, length_k_ref,
    gain_ref, gain_col_ref,
):
    bands, count = mask_ref.shape[:2]
    width = unit_ref.shape[1]
    size = width // heads
    weight = w_ref[...]
    pairs = [sums[i : i + 2] + sums[i + 2 : i + 4] for i in (0, 4)]
    picked = 1.0 + jnp.concatenate(
        [jnp.concatenate([pair[0:1], pair[1:2]], axis=1) for pair in pairs], axis=0
    )
    gain_ref[...] = picked
    gain_col_ref[...] = jnp.transpose(jnp.broadcast_to(picked[0:1], (128, width)))
    root = root_ref[...]
    unit = unit_ref[...]
    normed = (unit * picked[0:1]).astype(BF16)
    value_ref[...] = mm(normed, weight[:, 2 * width :]).astype(BF16)
    ones_head = same_head(width // 2, size // 2)
    cos, sine = cos_ref[...], sine_ref[...]
    own = [own_rows(part, count) for part in (normed, cos, sine)]
    for i, (ref, along_ref, length_ref, (rows, cos, sine)) in enumerate(
        (
            (query_ref, along_q_ref, length_q_ref, own),
            (key_ref, along_k_ref, length_k_ref, (normed, cos, sine)),
        )
    ):
        first, second = halves(mm(rows, weight[:, i * width : (i + 1) * width]))
        short = lax.rsqrt(mm((first * first + second * second).astype(BF16), ones_head) + EPS)
        length = short * root
        ref[...] = jnp.concatenate(
            [(first * cos - second * sine) * length, (second * cos + first * sine) * length], axis=1
        ).astype(BF16)
        along_ref[...] = jnp.concatenate([first * short, second * short], axis=1)
        length_ref[...] = length
    ones_half = jnp.ones((2 * count, 128), BF16)
    for band in range(bands):
        start = 2 * band * count
        span = slice(band * count, (band + 1) * count)
        query = query_ref[span, :].astype(F32)
        scores = mm_rt(stack_heads(query, heads), key_ref[start : start + 2 * count, :])
        raised = jnp.exp(scores).astype(BF16) * jnp.concatenate([mask_ref[band]] * heads, axis=0)
        raised_ref[band] = raised
        value = value_ref[start : start + 2 * count, :]
        for pair in range(heads // 2):
            lanes = slice(128 * pair, 128 * pair + 128)
            both = mm(
                raised[2 * pair * count : 2 * (pair + 1) * count],
                jnp.concatenate([value[:, lanes], ones_half], axis=1),
            )
            inverse = 1.0 / merge_pair(both[:, 128:], size)
            mixed_ref[span, lanes] = merge_pair(both[:, :128], size) * inverse
            inverse_ref[span, lanes] = inverse


def feed_kernel(
    heads, inputs_ref, cot_ref, w_up_ref, w_out_ref, gain_ref, mixed_ref, inverse_ref,
    middle_ref, middle_grad_ref, shrunk_ref, gain_grad_ref,
    w_down_ref, mixed_low_ref, normed_ref, gated_ref, d_exp_ref, branch_ref,
):
    width = inputs_ref.shape[1]
    hidden = w_down_ref.shape[0]
    w_up, w_out, w_down = w_up_ref[...], w_out_ref[...], w_down_ref[...]
    gain_feed = gain_ref[1:2]
    mixed = mixed_ref[...]
    mixed_low = mixed.astype(BF16)
    mixed_low_ref[...] = mixed_low
    middle = inputs_ref[...] + mm(mixed_low, w_out)
    middle_ref[...] = middle
    scale = norm_scale(middle)
    unit = middle * scale
    normed = (unit * gain_feed).astype(BF16)
    normed_ref[...] = normed
    cot = cot_ref[...].astype(F32)
    half = math.sqrt(0.5)
    density = 1.0 / math.sqrt(2.0 * math.pi)
    pulled = None
    for start in range(0, hidden, width):
        here = slice(start, start + width)
        there = slice(hidden + start, hidden + start + width)
        left = mm(normed, w_up[:, here])
        gate = mm(normed, w_up[:, there])
        d_gated = mm_rt(cot_ref[...], w_down[here])
        phi = 0.5 + 0.5 * lax.erf(gate * half)
        shaped = gate * phi
        gated_ref[:, here] = (left * shaped).astype(BF16)
        slope = phi + gate * (jnp.exp(gate * gate * -0.5) * density)
        d_left = (d_gated * shaped).astype(BF16)
        d_gate = (d_gated * left * slope).astype(BF16)
        d_exp_ref[:, here] = d_left
        d_exp_ref[:, there] = d_gate
        part = mm_rt(d_left, w_up[:, here]) + mm_rt(d_gate, w_up[:, there])
        pulled = part if pulled is None else pulled + part
    gain_grad_ref[...] = jnp.sum(pulled * unit, axis=0, keepdims=True)
    inner = pulled * gain_feed
    d_middle = cot + scale * (inner - unit * jnp.mean(unit * inner, axis=-1, keepdims=True))
    middle_grad_ref[...] = d_middle
    branch = d_middle.astype(BF16)
    branch_ref[...] = branch
    shrunk_ref[...] = (mm_rt(branch, w_out) * inverse_ref[...]).astype(BF16)


def weights_kernel(place, cot_ref, mixed_low_ref, normed_ref, gated_ref, d_exp_ref, branch_ref, mine_ref, other_ref):
    width, ups = cot_ref.shape[1], d_exp_ref.shape[1]
    split_parts(place, mm_lt(normed_ref[...], d_exp_ref[...]), mine_ref, other_ref, 0)
    split_parts(place, mm_lt(mixed_low_ref[...], branch_ref[...]), mine_ref, other_ref, ups)
    split_parts(place, mm_lt(gated_ref[...], cot_ref[...]), mine_ref, other_ref, ups + width)


def output_kernel(middle_ref, gated_ref, w_down_ref, out_ref):
    rows, cols, width = out_ref.shape
    total = (middle_ref[...] + mm(gated_ref[...], w_down_ref[...])).astype(BF16)
    count = rows * BAND
    for band in range(cols // BAND):
        out_ref[:, band * BAND : (band + 1) * BAND, :] = total[band * count : (band + 1) * count].reshape(
            rows, BAND, width
        )


def pull_head(grad, along, length, cos, sine, heads):
    first, second = halves(grad)
    along_first, along_second = halves(along)
    first, second = first * cos + second * sine, second * cos - first * sine
    ones_head = same_head(first.shape[1], first.shape[1] // heads)
    part = mm((along_first * first + along_second * second).astype(BF16), ones_head)
    grad = jnp.concatenate(
        [length * (first - along_first * part), length * (second - along_second * part)], axis=1
    )
    return grad.astype(BF16), jnp.sum(part, axis=0, keepdims=True)


def lane_sums(product):
    total = product[:, :128]
    for start in range(128, product.shape[1], 128):
        total = total + product[:, start : start + 128]
    return jnp.sum(jnp.transpose(total), axis=0, keepdims=True)


def normed_back_kernel(
    rows, place, w_ref, d_query_ref, d_rest_ref, own_ref, rim_swap_ref, rim_beside_ref
):
    width = own_ref.shape[1]
    count, edge = rows * BAND, REACH * BAND
    odd = place[5] == 1
    whole = mm_rt(d_rest_ref[...], w_ref[:, width:])
    own_ref[...] = mm_rt(d_query_ref[...], w_ref[:, :width]) + own_rows(whole, count)
    for band in range(whole.shape[0] // (2 * count)):
        start = 2 * band * count
        upper, lower = whole[start : start + edge], whole[start + edge + count : start + 2 * edge + count]
        here = slice(band * edge, (band + 1) * edge)
        rim_swap_ref[here] = jnp.where(odd, upper, lower).astype(BF16)
        rim_beside_ref[here] = jnp.where(odd, lower, upper).astype(BF16)


def features_kernel(place, inputs_ref, gain_ref, own_ref, rim_swap_ref, rim_beside_ref, middle_grad_ref, grad_ref):
    rows, cols, width = grad_ref.shape
    bands = cols // BAND
    count, edge = rows * BAND, REACH * BAND
    odd = place[5] == 1
    zeros = jnp.zeros((count - 2 * edge, width), F32)
    rims = []
    for band in range(bands):
        here = slice(band * edge, (band + 1) * edge)
        swapped, beside = rim_swap_ref[here].astype(F32), rim_beside_ref[here].astype(F32)
        rims += [jnp.where(odd, swapped, beside), zeros, jnp.where(odd, beside, swapped)]
    inner = (own_ref[...] + jnp.concatenate(rims, axis=0)) * gain_ref[0:1]
    inputs = inputs_ref[...]
    scale = norm_scale(inputs)
    unit = inputs * scale
    grad = middle_grad_ref[...] + scale * (inner - unit * jnp.mean(unit * inner, axis=-1, keepdims=True))
    for band in range(bands):
        grad_ref[:, band * BAND : (band + 1) * BAND, :] = grad[band * count : (band + 1) * count].reshape(
            rows, BAND, width
        )


def forward_kernel(
    heads, place, root_ref, unit_ref, cos_ref, sine_ref, mask_ref, inputs_ref, cot_ref,
    p0, p1, p2, p3, p4, p5, p6, p7,
    query_ref, key_ref, value_ref, raised_ref, mixed_ref, along_q_ref, length_q_ref, along_k_ref, length_k_ref,
    gain_ref, gain_col_ref, w_ref, middle_ref, middle_grad_ref, shrunk_ref, gain_grad_ref,
    w_down_ref, gated_ref, mine_ref, other_ref,
    inverse_ref, w_up_ref, w_out_ref, mixed_low_ref, normed_ref, d_exp_ref, branch_ref,
):
    width = inputs_ref.shape[1]
    first, ups = 3 * width + 128, w_up_ref.shape[1]
    sums = jnp.zeros((8, 128), F32)
    for start, rows in place_parts(place, (p0, p1, p2, p3, p4, p5, p6, p7)):
        store_rows(w_ref, start, rows[:, :, : 3 * width])
        sums = sums + jnp.sum(rows[:, :, 3 * width : first], axis=0)
        store_rows(w_up_ref, start, rows[:, :, first : first + ups])
        store_rows(w_out_ref, start, rows[:, :, first + ups : first + ups + width])
        down = [rows[:, :, at : at + width] for at in range(first + ups + width, rows.shape[2], width)]
        store_rows(w_down_ref, start, jnp.concatenate(down, axis=1))
    attend_kernel(
        heads, root_ref, unit_ref, cos_ref, sine_ref, mask_ref, sums, w_ref,
        query_ref, key_ref, value_ref, raised_ref, mixed_ref, inverse_ref,
        along_q_ref, length_q_ref, along_k_ref, length_k_ref, gain_ref, gain_col_ref,
    )
    feed_kernel(
        heads, inputs_ref, cot_ref, w_up_ref, w_out_ref, gain_ref, mixed_ref, inverse_ref,
        middle_ref, middle_grad_ref, shrunk_ref, gain_grad_ref,
        w_down_ref, mixed_low_ref, normed_ref, gated_ref, d_exp_ref, branch_ref,
    )
    weights_kernel(
        place, cot_ref, mixed_low_ref, normed_ref, gated_ref, d_exp_ref, branch_ref, mine_ref, other_ref
    )


def backward_kernel(
    heads, rows, place, root_ref, shrunk_ref, mixed_ref, raised_ref, query_ref, key_ref, value_ref,
    cos_ref, sine_ref, w_ref, gain_col_ref, unit_turned_ref, own_turned_ref, along_q_ref, length_q_ref,
    along_k_ref, length_k_ref, gain_grad_ref,
    d_query_ref, d_rest_ref, mine_ref, other_ref,
):
    bands, _, keys = raised_ref.shape
    count, edge = keys // 2, REACH * BAND
    width = shrunk_ref.shape[1]
    ones_half = jnp.ones((keys, 128), BF16)
    along_total = jnp.zeros((1, width // 2), F32)
    for band in range(bands):
        span = slice(band * count, (band + 1) * count)
        start = band * keys
        whole = slice(start, start + keys)
        own = slice(start + edge, start + edge + count)
        shrunk = shrunk_ref[span].astype(F32)
        level_rows = -(shrunk * mixed_ref[span])
        value = value_ref[whole, :]
        raised = raised_ref[band]
        parts, stacks = [], []
        for pair in range(heads // 2):
            lanes = slice(128 * pair, 128 * pair + 128)
            stacks.append(pair_lanes(shrunk, heads, pair))
            parts.append(
                mm_rt(
                    jnp.concatenate([stacks[-1], pair_lanes(level_rows, heads, pair)], axis=1),
                    jnp.concatenate([value[:, lanes], ones_half], axis=1),
                )
            )
        d_scores = (raised.astype(F32) * jnp.concatenate(parts, axis=0)).astype(BF16)
        query = query_ref[span, :].astype(F32)
        d_key = mm_lt(d_scores, stack_heads(query, heads))
        d_query = fold_heads(mm(d_scores, key_ref[whole, :]), heads)
        for pair in range(heads // 2):
            lanes = slice(width + 128 * pair, width + 128 * pair + 128)
            d_value = mm_lt(raised[2 * pair * count : 2 * (pair + 1) * count], stacks[pair])
            d_rest_ref[whole, lanes] = d_value.astype(BF16)
        d_rest_ref[whole, :width], along_k = pull_head(
            d_key, along_k_ref[whole, :], length_k_ref[whole, :], cos_ref[whole, :], sine_ref[whole, :], heads
        )
        d_query_ref[span, :], along_q = pull_head(
            d_query, along_q_ref[span, :], length_q_ref[span, :], cos_ref[own, :], sine_ref[own, :], heads
        )
        along_total = along_total + along_k + along_q
    plain = jnp.concatenate(
        [mm(own_turned_ref[...], d_query_ref[...]), mm(unit_turned_ref[...], d_rest_ref[...])], axis=1
    )
    scaled = plain * jnp.concatenate([gain_col_ref[...]] * (3 * width // 128), axis=1)
    turned = jnp.concatenate([scaled[:, :width], scaled[:, width : 2 * width]], axis=0).astype(BF16)
    plain_order = mm_rt(turned, turned_order(width, heads))
    split_parts(place, plain_order[:width], mine_ref, other_ref, 0)
    split_parts(place, plain_order[width:], mine_ref, other_ref, width)
    split_parts(place, scaled[:, 2 * width :], mine_ref, other_ref, 2 * width)
    lines = []
    for total in (lane_sums(plain * w_ref[...].astype(F32)), gain_grad_ref[...]):
        lines += [total[:, :128], total[:, 128:]]
    total = along_total * 0.5 / root_ref[...]
    high = total.astype(BF16).astype(F32)
    lines += [high, total - high, jnp.zeros((2, 128), F32)]
    tail = jnp.concatenate(lines, axis=0).astype(BF16)
    for ref in (mine_ref, other_ref):
        ref[:, :, :, 3 * width :] = jnp.broadcast_to(tail[None, None], ref.shape[:2] + tail.shape)


def call(kernel, outs, scratch=(), place=None, smem=0, smem_out=0, flops=10**9, pin=True, aliases=None):
    if place is not None:
        kernel = functools.partial(kernel, place)

    def run(*args):
        args = [
            arg if i < smem else pltpu.with_memory_space_constraint(arg, pltpu.VMEM if pin else pltpu.HBM)
            for i, arg in enumerate(args)
        ]
        return pl.pallas_call(
            kernel,
            out_shape=outs,
            in_specs=[
                pl.BlockSpec(memory_space=pltpu.SMEM if i < smem else pltpu.VMEM)
                for i in range(len(args))
            ],
            out_specs=[
                pl.BlockSpec(memory_space=pltpu.SMEM if i >= len(outs) - smem_out else pltpu.VMEM)
                for i in range(len(outs))
            ],
            scratch_shapes=list(scratch),
            input_output_aliases=aliases or {},
            compiler_params=pltpu.CompilerParams(vmem_limit_bytes=VMEM_LIMIT),
            cost_estimate=pl.CostEstimate(flops=flops, bytes_accessed=4 * 10**6 if flops > 1 else 1, transcendentals=0),
        )(*args)

    return run


def rotation_tables(row_place, col_place, heads, size):
    part = size // 8
    lane = jnp.arange(heads * size // 2) % (size // 2)
    index = (lane % part).astype(F32)
    frequency = math.pi / 8.0 * jnp.exp(index * (-math.log(10.0) / part))
    group = lane // part

    def table(place, kind):
        angle = place.astype(F32)[:, None] * frequency
        cos = jnp.where(group == kind, jnp.cos(angle), 0.0)
        if kind:
            cos = jnp.where(group >= 2, 1.0, cos)
        return jnp.stack([cos, jnp.where(group == kind, jnp.sin(angle), 0.0)])

    return table(row_place, 0), table(col_place, 1)


def window_ids(crop_ids, row_start, rows):
    ids = jnp.pad(crop_ids[:, ::BAND], ((REACH, 2 * rows), (0, 0)), constant_values=-1)
    ids = lax.dynamic_slice_in_dim(ids, row_start, 2 * rows, 0)
    return jnp.repeat(ids, BAND, axis=0), jnp.repeat(ids.T, BAND, axis=1)


def on_device(
    features, crop_ids, conditioning, qkv_weight, out_weight, up_weight, down_weight,
    attn_cond_weight, feed_cond_weight, attention_scale, cotangent,
):
    rows, cols, width = features.shape
    heads = attention_scale.shape[0]
    size = width // heads
    bands = cols // BAND
    count = rows * BAND
    tokens = rows * cols
    edge = REACH * BAND
    n_rows, n_cols = lax.axis_size("rows"), lax.axis_size("cols")
    devices = n_rows * n_cols
    hidden = down_weight.shape[0] * devices
    own_cond = attn_cond_weight.shape[0]
    canvases = conditioning.shape[0]
    row, col = lax.axis_index("rows"), lax.axis_index("cols")
    row_start, col_start = row * rows, col * cols
    canvas = col_start // CANVAS
    group, chips = 4, 4
    chunks = 2 * chips * group
    direct = (n_rows, n_cols) == (2 * chips, group) and chunks * 8 == width
    first_lanes = 3 * width + 128
    second_lanes = 2 * hidden + width + hidden * width // (8 * chunks)
    per_canvas = max(n_cols // canvases, 1)
    place = Place(direct, cols, n_cols)

    def result(*dims, dtype=F32):
        return jax.ShapeDtypeStruct(dims, dtype)

    def shape(*dims, dtype=F32):
        return pltpu.VMEM(dims, dtype)

    def low(*dims):
        return shape(*dims, dtype=BF16)

    def over(axis, by):
        size_of = lax.axis_size(axis)
        return lambda value: lax.ppermute(value, axis, [(i, i ^ by) for i in range(size_of)])

    z_moves = [over("cols", k) for k in range(1, group)]
    xy_moves = [over("rows", 2 * m) for m in range(1, chips)]

    def chip_pairs(step):
        return [(i, i ^ (4 if i % 2 == step else 2)) for i in range(n_rows)]

    def first_chip(value):
        return lax.ppermute(value, "rows", chip_pairs(0))

    def second_chip(value):
        return lax.ppermute(value, "rows", chip_pairs(1))

    core_move = over("rows", 1)

    if direct:
        near, far, cond_own = call(
            functools.partial(pack_kernel, heads, per_canvas),
            [
                low(8, first_lanes + second_lanes),
                low(8, first_lanes + second_lanes),
                shape(own_cond, canvases),
            ],
            place=place,
            pin=False,
        )(conditioning, qkv_weight, up_weight, out_weight, down_weight, attn_cond_weight, feed_cond_weight)
        z_order = (3, 1, 2)
        line = call(functools.partial(line_kernel, z_order), [low(group, 8, first_lanes + second_lanes)], place=place)(
            near,
            *[z_moves[k - 1](near if k // per_canvas == 0 else far) for k in z_order],
        )[0]
        mine = [line] + [move(line) for move in xy_moves]
    else:
        def parts_of(full):
            full = full.reshape(chips, 2, group, 8, full.shape[-1])
            return [full[m, core] for core in range(2) for m in range(chips)]

        def whole(weight):
            return lax.all_gather(weight, AXES, axis=0, tiled=True)

        cond = lax.dynamic_slice_in_dim(conditioning, place[4] * own_cond, own_cond, 1)
        cond_own = cond.T.astype(F32)
        sums = [
            lax.psum(jnp.dot(cond, weight, preferred_element_type=F32), AXES)
            for weight in (attn_cond_weight, feed_cond_weight)
        ]
        lines = []
        for part in sums:
            part = lax.dynamic_slice_in_dim(part, canvas, 1, 0).reshape(-1, 128)
            high = lax.reduce_precision(part, 8, 7)
            lines += [high, part - high]
        lines = jnp.pad(jnp.concatenate(lines).astype(BF16), ((0, width - 8), (0, 0)))
        qkv = whole(qkv_weight)
        turned = jnp.argmax(turned_order(width, heads), axis=0)
        qkv = jnp.concatenate([qkv[:, :width][:, turned], qkv[:, width : 2 * width][:, turned], qkv[:, 2 * width :]], axis=1)
        down = whole(down_weight).reshape(chunks, -1, 8, width).transpose(0, 2, 1, 3).reshape(width, -1)
        parts = parts_of(
            jnp.concatenate([qkv, lines, whole(up_weight), whole(out_weight), down], axis=1)
        )

    odd = row % 2 == 1
    beside_pairs = [(i, (i + 1 if i % 2 else i - 1) % n_rows) for i in range(n_rows)]

    def beside_move(value):
        return lax.ppermute(value, "rows", beside_pairs)

    first_rows, last_rows = features[:REACH], features[rows - REACH :]
    halo_swap = core_move(jnp.where(odd, first_rows, last_rows))
    halo_beside = beside_move(jnp.where(odd, last_rows, first_rows))

    row_place = row_start - REACH + jnp.arange(2 * rows, dtype=jnp.int32)
    col_place = (col_start + jnp.arange(cols, dtype=jnp.int32)) % CANVAS
    row_table, col_table = rotation_tables(row_place, col_place, heads, size)
    id_query, id_key = window_ids(crop_ids, row_start, rows)

    unit, unit_turned, own_turned, cos, sine, mask, inputs, cot, root = call(
        functools.partial(ready_kernel, heads),
        [
            shape(2 * tokens, width),
            low(width, 2 * tokens),
            low(width, tokens),
            shape(2 * tokens, width // 2),
            shape(2 * tokens, width // 2),
            low(bands, count, 2 * count),
            shape(tokens, width),
            low(tokens, width),
            shape(1, width // 2),
        ],
        place=place,
        smem=1,
    )(attention_scale, features, cotangent, halo_swap, halo_beside, row_table, col_table, id_query, id_key)
    if direct:
        mine = mine[:1] + [lax.optimization_barrier((part, unit))[0] for part in mine[1:]]
        far = core_move(mine[3])
        for i in (1, 2):
            mine[i], far = lax.optimization_barrier((mine[i], far))
        parts = mine + [core_move(part) for part in mine[:3]] + [far]

    (
        query, key, value, raised, mixed, along_q, length_q, along_k, length_k, gain, gain_col, w_qkv,
        middle, middle_grad, shrunk, gain_grad, w_down, gated, mine_second, other_second,
    ) = call(
        functools.partial(forward_kernel, heads),
        [
            low(tokens, width),
            low(2 * tokens, width),
            low(2 * tokens, width),
            low(bands, heads * count, 2 * count),
            shape(tokens, width),
            shape(tokens, width),
            shape(tokens, width // 2),
            shape(2 * tokens, width),
            shape(2 * tokens, width // 2),
            shape(2, width),
            shape(width, 128),
            low(width, 3 * width),
            shape(tokens, width),
            shape(tokens, width),
            low(tokens, width),
            shape(1, width),
            low(hidden, width),
            low(tokens, hidden),
            low(chips, group, 8, second_lanes),
            low(chips, group, 8, second_lanes),
        ],
        scratch=[
            pltpu.VMEM((tokens, width), F32),
            pltpu.VMEM((width, 2 * hidden), BF16),
            pltpu.VMEM((width, width), BF16),
            pltpu.VMEM((tokens, width), BF16),
            pltpu.VMEM((tokens, width), BF16),
            pltpu.VMEM((tokens, 2 * hidden), BF16),
            pltpu.VMEM((tokens, width), BF16),
        ],
        place=place,
    )(root, unit, cos, sine, mask, inputs, cot, *parts)

    d_query, d_rest, mine_first, other_first = call(
        functools.partial(backward_kernel, heads, rows),
        [
            low(tokens, width),
            low(2 * tokens, 2 * width),
            low(chips, group, 8, first_lanes),
            low(chips, group, 8, first_lanes),
        ],
        place=place,
        flops=1,
    )(
        root, shrunk, mixed, raised, query, key, value, cos, sine, w_qkv, gain_col, unit_turned, own_turned,
        along_q, length_q, along_k, length_k, gain_grad,
    )

    def last_output(gated):
        return call(output_kernel, [result(rows, cols, width, dtype=BF16)])(middle, gated, w_down)[0]

    def normed_back(d_query, d_rest):
        return call(
            functools.partial(normed_back_kernel, rows),
            [shape(tokens, width), low(bands * edge, width), low(bands * edge, width)],
            place=place,
        )(w_qkv, d_query, d_rest)

    def last_features(own, rim_swap, rim_beside):
        return call(features_kernel, [result(rows, cols, width)], place=place)(
            inputs, gain, own, rim_swap, rim_beside, middle_grad
        )[0]

    if direct:
        all_lanes = second_lanes + first_lanes
        def core_sum(mine, got):
            return call(core_sum_kernel, [low(group, 8, mine.shape[-1]) for _ in range(chips)], place=place)(mine, got)

        def pair_sum(one, two):
            return call(pair_sum_kernel, [low(*one.shape)], flops=1)(one, two)[0]

        first_got = core_move(other_first)
        second_own, second_near, second_beside, second_far = core_sum(mine_second, core_move(other_second))
        second_far = second_chip(second_far)
        first_own, first_near, first_beside, first_far = core_sum(mine_first, first_got)
        first_far = second_chip(first_far)
        second_far, first_far = lax.optimization_barrier((second_far, first_far))
        first_own, d_rest = lax.optimization_barrier((first_own, d_rest))
        beside = second_chip(call(join_kernel, [low(group, 8, all_lanes)], flops=1)(second_beside, first_beside)[0])
        sums = [
            second_own,
            first_chip(pair_sum(second_near, second_far)),
            first_own,
            first_chip(pair_sum(first_near, first_far)),
            beside,
        ]
        own_grad, rim_swap, rim_beside = normed_back(d_query, d_rest)
        rim_swap, rim_beside = core_move(rim_swap), beside_move(rim_beside)
        blocks = call(
            chip_sum_kernel,
            [shape(8, all_lanes)] + [low(8, all_lanes) for _ in z_moves],
            scratch=[pltpu.VMEM((group, 8, all_lanes), F32)],
            place=place,
        )(*sums)
        blocks, gated, own_grad = lax.optimization_barrier((blocks, gated, own_grad))
        output = last_output(gated)
        grad_features = last_features(own_grad, rim_swap, rim_beside)
        grad_qkv, grad_out, grad_up, grad_down, grad_attn_cond, grad_feed_cond, grad_scale = call(
            functools.partial(last_kernel, per_canvas, size // 2),
            [
                result(8, 3 * width),
                result(8, width),
                result(8, 2 * hidden),
                result(hidden // chunks, width),
                result(own_cond, width),
                result(own_cond, width),
                result(heads),
            ],
            place=place,
            smem_out=1,
        )(cond_own, blocks[0], *[move(block) for move, block in reversed(list(zip(z_moves, blocks[1:])))])
    else:
        own_grad, rim_swap, rim_beside = normed_back(d_query, d_rest)
        grad_features = last_features(own_grad, core_move(rim_swap), beside_move(rim_beside))
        output = last_output(gated)

        def joined(mine, other):
            return jnp.stack([mine, other], axis=1).astype(F32).reshape(chunks, 8, mine.shape[-1])

        def scattered(grad):
            return lax.psum_scatter(grad.reshape(-1, grad.shape[-1]), AXES, scatter_dimension=0, tiled=True)

        last = joined(mine_first, other_first)
        second = joined(mine_second, other_second)
        ups = 2 * hidden
        grad_qkv = scattered(last[:, :, : 3 * width])
        grad_up = scattered(second[:, :, :ups])
        grad_out = scattered(second[:, :, ups : ups + width])
        grad_down = scattered(
            second[:, :, ups + width :].reshape(chunks, 8, -1, width).transpose(0, 2, 1, 3)
        )
        spot = (jnp.arange(canvases) == canvas).astype(F32)[:, None, None]
        tail = lax.psum(spot * last[0, :, 3 * width :][None], AXES)

        def cond_grad(sums):
            return jnp.sum(cond_own[:, :, None] * sums.reshape(canvases, width)[None], axis=1)

        grad_attn_cond = cond_grad(tail[:, 0:2])
        grad_feed_cond = cond_grad(tail[:, 2:4])
        grad_scale = jnp.sum(tail[:, 4] + tail[:, 5], axis=0)[:: size // 2]
    return (
        output, grad_features, grad_qkv, grad_out, grad_up, grad_down, grad_attn_cond, grad_feed_cond, grad_scale,
    )


def solution(mesh):
    tile, whole, split = P("rows", "cols", None), P(), P(AXES, None)
    return jax.shard_map(
        on_device,
        mesh=mesh,
        in_specs=(tile, P(None, "cols"), whole, split, split, split, split, split, split, whole, tile),
        out_specs=(tile, tile, split, split, split, split, split, split, whole),
        check_vma=False,
    )
```

```python
import functools
import math

import jax
import jax.numpy as jnp
from jax import lax
from jax.experimental import pallas as pl
from jax.experimental.pallas import tpu as pltpu
from jax.sharding import PartitionSpec as P

CANVAS = 128
BAND = 16
REACH = 3
AXES = ("rows", "cols")
F32 = jnp.float32
BF16 = jnp.bfloat16
EPS = 1e-06
VMEM_LIMIT = 32 * 1024 * 1024


class Place:
    def __init__(self, direct, cols, n_cols):
        self.direct, self.cols, self.n_cols = direct, cols, n_cols

    def __getitem__(self, item):
        row, col = lax.axis_index("rows"), lax.axis_index("cols")
        if item == 0:
            return col * self.cols // CANVAS
        if item == 4:
            return row * self.n_cols + col
        if item == 5:
            return lax.rem(row, 2)
        if not self.direct:
            return (0, 0, 0, 0, 0, 0, 1)[item]
        return (None, row // 2, lax.rem(row, 2), col, None, None, 2 - lax.rem(row, 2))[item]


def mm(left, right):
    return lax.dot_general(left, right, (((1,), (0,)), ((), ())), preferred_element_type=F32)


def mm_rt(left, right):
    return lax.dot_general(left, right, (((1,), (1,)), ((), ())), preferred_element_type=F32)


def mm_lt(left, right):
    return lax.dot_general(left, right, (((0,), (0,)), ((), ())), preferred_element_type=F32)


def same_head(width, size):
    first = lax.broadcasted_iota(jnp.int32, (width, width), 0) // size
    second = lax.broadcasted_iota(jnp.int32, (width, width), 1) // size
    return jnp.where(first == second, 1.0, 0.0).astype(BF16)


def stack_heads(values, heads):
    lane = head_of(values.shape, heads)
    return jnp.concatenate(
        [jnp.where(lane == h, values, 0.0).astype(BF16) for h in range(heads)], axis=0
    )


def fold_heads(values, heads):
    count = values.shape[0] // heads
    lane = head_of((count, values.shape[1]), heads)
    total = values[:count]
    for h in range(1, heads):
        total = jnp.where(lane == h, values[h * count : (h + 1) * count], total)
    return total


def turned_order(width, heads):
    size = width // heads
    part = size // 8
    row = lax.broadcasted_iota(jnp.int32, (width, width), 0)
    col = lax.broadcasted_iota(jnp.int32, (width, width), 1)
    half, lane = col // (width // 2), col % (width // 2)
    head, j = lane // (size // 2), lane % (size // 2)
    rotated = j // part * 2 * part + j % part + half * part
    kept = 4 * part + j - 2 * part + half * 2 * part
    return jnp.where(row == head * size + jnp.where(j < 2 * part, rotated, kept), 1.0, 0.0).astype(BF16)


def halves(values):
    half = values.shape[1] // 2
    return values[:, :half], values[:, half:]


def head_of(shape, heads):
    half = shape[1] // 2
    return lax.broadcasted_iota(jnp.int32, shape, 1) % half // (half // heads)


def own_rows(values, count):
    edge = REACH * BAND
    return jnp.concatenate(
        [values[start + edge : start + edge + count] for start in range(0, values.shape[0], 2 * count)], axis=0
    )


def bands_of(ref, bands):
    parts = [
        ref[:, band * BAND : (band + 1) * BAND, :].astype(F32).reshape(-1, ref.shape[-1])
        for band in range(bands)
    ]
    return jnp.concatenate(parts, axis=0)


def pair_lanes(values, heads, pair):
    size = values.shape[1] // heads
    part = values[:, 128 * pair : 128 * pair + 128]
    lane = lax.broadcasted_iota(jnp.int32, part.shape, 1)
    return jnp.concatenate(
        [jnp.where(lane < size, part, 0.0), jnp.where(lane < size, 0.0, part)], axis=0
    ).astype(BF16)


def merge_pair(values, size):
    count = values.shape[0] // 2
    lane = lax.broadcasted_iota(jnp.int32, (count, 128), 1)
    return jnp.where(lane < size, values[:count], values[count:])


def close(shape, query_row, key_row):
    token = lax.broadcasted_iota(jnp.int32, shape, 0)
    place = lax.broadcasted_iota(jnp.int32, shape, 1)
    return (jnp.abs(token // BAND + query_row - place // BAND - key_row) <= REACH) & (
        jnp.abs(token % BAND - place % BAND) <= REACH
    )


def norm_scale(values):
    return lax.rsqrt(jnp.mean(values * values, axis=-1, keepdims=True) + EPS)


def place_parts(place, part_refs):
    for index, part in enumerate(part_refs):
        chip = place[1] ^ (index % 4)
        core = place[2] ^ (index // 4)
        group = part.shape[0]
        yield (chip * 2 + core) * group, part[...].astype(F32)


def store_rows(ref, start, rows):
    group, count, lanes = rows.shape
    ref[pl.ds(pl.multiple_of(start * count, group * count), group * count), :] = rows.reshape(
        group * count, lanes
    ).astype(ref.dtype)


def split_parts(place, values, mine_ref, other_ref, start):
    chips, group = mine_ref.shape[:2]
    count = values.shape[0] // (2 * chips)
    first = place[2] == 0
    for chip in range(chips):
        zero, one = [values[(2 * chip + core) * count : (2 * chip + core + 1) * count] for core in range(2)]
        for ref, part in ((mine_ref, jnp.where(first, zero, one)), (other_ref, jnp.where(first, one, zero))):
            part = part.reshape(group, count // group, values.shape[1])
            for i in range(count // group // 8):
                at = start + i * values.shape[1]
                ref[chip, :, :, at : at + values.shape[1]] = part[:, 8 * i : 8 * i + 8].astype(BF16)


def pack_kernel(
    heads, per_canvas, place, cond_ref, qkv_ref, up_ref, out_ref, down_ref, attn_ref, feed_ref,
    near_ref, far_ref, cond_own_ref,
):
    own = attn_ref.shape[0]
    canvases, total = cond_ref.shape
    width = out_ref.shape[1]
    row = lax.broadcasted_iota(jnp.int32, (own, total), 0) + place[4] * own
    pick = jnp.where(row == lax.broadcasted_iota(jnp.int32, (own, total), 1), 1.0, 0.0).astype(BF16)
    cond = mm_rt(pick, cond_ref[...])
    cond_own_ref[...] = cond
    tails = []
    for canvas in range(canvases):
        lines = []
        for weight_ref in (attn_ref, feed_ref):
            line = jnp.sum(
                cond[:, canvas : canvas + 1] * weight_ref[...].astype(F32), axis=0, keepdims=True
            )
            high = line.astype(BF16).astype(F32)
            for part in (high, line - high):
                lines += [part[:, :128], part[:, 128:]]
        tails.append(jnp.concatenate(lines, axis=0))
    down = down_ref[...].astype(F32)
    parts = [up_ref[...], out_ref[...]] + [down[8 * i : 8 * i + 8].astype(BF16) for i in range(down.shape[0] // 8)]
    qkv = qkv_ref.shape[1]
    turned = mm(
        jnp.concatenate([qkv_ref[:, :width], qkv_ref[:, width : 2 * width]], axis=0).astype(F32).astype(BF16),
        turned_order(width, heads),
    ).astype(BF16)
    mine = place[0] == 0
    for ref, tail in (
        (near_ref, jnp.where(mine, tails[0], tails[1])),
        (far_ref, jnp.where(mine, tails[1], tails[0])),
    ):
        ref[:, :width], ref[:, width : 2 * width] = turned[:8], turned[8:]
        ref[:, 2 * width : qkv] = qkv_ref[:, 2 * width :]
        ref[:, qkv : qkv + 128] = tail.astype(BF16)
        at = qkv + 128
        for part in parts:
            ref[:, at : at + part.shape[1]] = part
            at += part.shape[1]


def line_kernel(order, place, p0, p1, p2, p3, line_ref):
    for index, part in zip((0,) + order, (p0, p1, p2, p3)):
        line_ref[place[3] ^ index] = part[...]


def carried(total):
    tail = total[..., total.shape[-1] - 128 :]
    value = tail[..., 4:5, :] + tail[..., 5:6, :]
    high = value.astype(BF16).astype(F32)
    row = lax.broadcasted_iota(jnp.int32, tail.shape, tail.ndim - 2)
    tail = jnp.where(row == 4, high, jnp.where(row == 5, value - high, tail))
    return jnp.concatenate([total[..., : total.shape[-1] - 128], tail], axis=-1)


def core_sum_kernel(carry, place, mine_ref, got_ref, *outs):
    for index, out_ref in enumerate(outs):
        chip = place[1] ^ (0, place[6], place[6] ^ 3, 3)[index]
        total = mine_ref[chip].astype(F32) + got_ref[chip].astype(F32)
        out_ref[...] = (carried(total) if carry else total).astype(BF16)


def join_kernel(one_ref, two_ref, out_ref):
    split = one_ref.shape[-1]
    out_ref[:, :, :split] = one_ref[...]
    out_ref[:, :, split:] = two_ref[...]


def pair_sum_kernel(carry, one_ref, two_ref, out_ref):
    total = one_ref[...].astype(F32) + two_ref[...].astype(F32)
    out_ref[...] = (carried(total) if carry else total).astype(BF16)


def chip_sum_kernel(place, p0, p1, q0, q1, both, o0, o1, o2, o3, keep_ref):
    split = p0.shape[-1]
    keep_ref[:, :, :split] = p0[...].astype(F32) + p1[...].astype(F32) + both[:, :, :split].astype(F32)
    keep_ref[:, :, split:] = carried(
        q0[...].astype(F32) + q1[...].astype(F32) + both[:, :, split:].astype(F32)
    )
    for index, out_ref in enumerate((o0, o1, o2, o3)):
        out_ref[...] = keep_ref[place[3] ^ index].astype(out_ref.dtype)


def last_kernel(
    per_canvas, size, place, cond_ref, own_ref, three_ref, two_ref, one_ref,
    qkv_ref, out_ref, up_ref, down_ref, attn_ref, feed_ref, scale_ref,
):
    parts = [own_ref[...]] + [ref[...].astype(F32) for ref in (one_ref, two_ref, three_ref)]
    total = parts[0] + parts[1] + parts[2] + parts[3]
    width = out_ref.shape[1]
    at = up_ref.shape[1]
    up_ref[...] = total[:, :at]
    out_ref[...] = total[:, at : at + width]
    for i in range(down_ref.shape[0] // 8):
        at += width
        down_ref[8 * i : 8 * i + 8, :] = total[:, at : at + width]
    at += width
    qkv_ref[...] = total[:, at : at + qkv_ref.shape[1]]
    at += qkv_ref.shape[1]
    cond = cond_ref[...]
    attn, feed = 0.0, 0.0
    for canvas in range(cond.shape[1]):
        tail = jnp.zeros((8, 128), F32)
        for index, part in enumerate(parts):
            same = (place[3] ^ index) // per_canvas == canvas
            tail = tail + jnp.where(same, part[:, at:], 0.0)
        weight = cond[:, canvas : canvas + 1]
        attn = attn + weight * jnp.concatenate([tail[0:1], tail[1:2]], axis=1)
        feed = feed + weight * jnp.concatenate([tail[2:3], tail[3:4]], axis=1)
    attn_ref[...] = attn
    feed_ref[...] = feed
    tail = total[:, at:]
    scale = tail[4:5] + tail[5:6]
    for h in range(scale_ref.shape[0]):
        scale_ref[h] = scale[0, h * size]


def ready_kernel(
    heads, place, scale_ref, feat_ref, cot_ref, swap_ref, beside_ref, row_ref, col_ref, id_query_ref, id_key_ref,
    unit_ref, unit_turned_ref, own_turned_ref, cos_ref, sine_ref, mask_ref, inputs_ref, cot_out_ref, root_ref,
):
    rows, cols, width = feat_ref.shape
    count = rows * BAND
    bands = cols // BAND
    odd = place[5] == 1
    near = close((count, 2 * count), REACH, 0)
    lane = lax.broadcasted_iota(jnp.int32, (1, width // 2), 1) // (width // 2 // heads)
    root = jnp.zeros((1, width // 2), F32)
    for h in range(heads):
        root = jnp.where(lane == h, scale_ref[h], root)
    root_ref[...] = jnp.sqrt(root)
    inputs_ref[...] = bands_of(feat_ref, bands)
    cot_out_ref[...] = bands_of(cot_ref, bands).astype(BF16)
    for band in range(bands):
        part = slice(band * BAND, (band + 1) * BAND)
        swapped = swap_ref[:, part, :].astype(F32)
        beside = beside_ref[:, part, :].astype(F32)
        full = jnp.concatenate(
            [
                jnp.where(odd, swapped, beside),
                feat_ref[:, part, :].astype(F32),
                jnp.where(odd, beside, swapped),
                jnp.zeros((2, BAND, width), F32),
            ],
            axis=0,
        ).reshape(2 * count, width)
        span = slice(2 * band * count, 2 * (band + 1) * count)
        unit = full * norm_scale(full)
        unit_ref[span] = unit
        turned = jnp.transpose(unit).astype(BF16)
        unit_turned_ref[:, span] = turned
        own = slice(REACH * BAND, REACH * BAND + count)
        own_turned_ref[:, band * count : (band + 1) * count] = jnp.transpose(unit[own]).astype(BF16)
        for i, ref in enumerate((cos_ref, sine_ref)):
            ref[span] = (row_ref[i][:, None, :] + col_ref[i, part, :][None]).reshape(2 * count, width // 2)
        alike = id_query_ref[REACH * BAND : REACH * BAND + count, band : band + 1] == id_key_ref[
            band : band + 1, :
        ]
        mask_ref[band] = jnp.where(near & alike, 1.0, 0.0).astype(BF16)


def attend_kernel(
    heads, root_ref, unit_ref, cos_ref, sine_ref, mask_ref, sums, w_ref,
    query_ref, key_ref, value_ref, raised_ref, mixed_ref, inverse_ref, inverse_rows_ref, along_q_ref, length_q_ref, along_k_ref, length_k_ref,
    gain_ref, gain_col_ref,
):
    bands, count = mask_ref.shape[:2]
    width = unit_ref.shape[1]
    size = width // heads
    weight = w_ref[...]
    pairs = [sums[i : i + 2] + sums[i + 2 : i + 4] for i in (0, 4)]
    picked = 1.0 + jnp.concatenate(
        [jnp.concatenate([pair[0:1], pair[1:2]], axis=1) for pair in pairs], axis=0
    )
    gain_ref[...] = picked
    gain_col_ref[...] = jnp.transpose(jnp.broadcast_to(picked[0:1], (128, width)))
    root = root_ref[...]
    unit = unit_ref[...]
    normed = (unit * picked[0:1]).astype(BF16)
    value_ref[...] = mm(normed, weight[:, 2 * width :]).astype(BF16)
    ones_head = same_head(width // 2, size // 2)
    cos, sine = cos_ref[...], sine_ref[...]
    own = [own_rows(part, count) for part in (normed, cos, sine)]
    for i, (ref, along_ref, length_ref, (rows, cos, sine)) in enumerate(
        (
            (query_ref, along_q_ref, length_q_ref, own),
            (key_ref, along_k_ref, length_k_ref, (normed, cos, sine)),
        )
    ):
        first, second = halves(mm(rows, weight[:, i * width : (i + 1) * width]))
        short = lax.rsqrt(mm((first * first + second * second).astype(BF16), ones_head) + EPS)
        length = short * root
        ref[...] = jnp.concatenate(
            [(first * cos - second * sine) * length, (second * cos + first * sine) * length], axis=1
        ).astype(BF16)
        along_ref[...] = jnp.concatenate([first * short, second * short], axis=1)
        length_ref[...] = length
    ones_half = jnp.ones((2 * count, 128), BF16)
    for band in range(bands):
        start = 2 * band * count
        span = slice(band * count, (band + 1) * count)
        query = query_ref[span, :].astype(F32)
        scores = mm_rt(stack_heads(query, heads), key_ref[start : start + 2 * count, :])
        raised = jnp.exp(scores).astype(BF16) * jnp.concatenate([mask_ref[band]] * heads, axis=0)
        raised_ref[band] = raised
        value = value_ref[start : start + 2 * count, :]
        for pair in range(heads // 2):
            lanes = slice(128 * pair, 128 * pair + 128)
            both = mm(
                raised[2 * pair * count : 2 * (pair + 1) * count],
                jnp.concatenate([value[:, lanes], ones_half], axis=1),
            )
            rows_inverse = 1.0 / both[:, 128:]
            inverse_rows_ref[band, 2 * pair * count : 2 * (pair + 1) * count, :] = rows_inverse
            inverse = merge_pair(rows_inverse, size)
            mixed_ref[span, lanes] = merge_pair(both[:, :128], size) * inverse
            inverse_ref[span, lanes] = inverse


def feed_kernel(
    heads, inputs_ref, cot_ref, w_up_ref, w_out_ref, gain_ref, mixed_ref, inverse_ref,
    middle_ref, middle_grad_ref, shrunk_ref, d_mixed_ref, levels_ref, gain_grad_ref,
    w_down_ref, mixed_low_ref, normed_ref, gated_ref, d_exp_ref, branch_ref,
):
    width = inputs_ref.shape[1]
    hidden = w_down_ref.shape[0]
    w_up, w_out, w_down = w_up_ref[...], w_out_ref[...], w_down_ref[...]
    gain_feed = gain_ref[1:2]
    mixed = mixed_ref[...]
    mixed_low = mixed.astype(BF16)
    mixed_low_ref[...] = mixed_low
    middle = inputs_ref[...] + mm(mixed_low, w_out)
    middle_ref[...] = middle
    scale = norm_scale(middle)
    unit = middle * scale
    normed = (unit * gain_feed).astype(BF16)
    normed_ref[...] = normed
    cot = cot_ref[...].astype(F32)
    half = math.sqrt(0.5)
    density = 1.0 / math.sqrt(2.0 * math.pi)
    pulled = None
    for start in range(0, hidden, width):
        here = slice(start, start + width)
        there = slice(hidden + start, hidden + start + width)
        left = mm(normed, w_up[:, here])
        gate = mm(normed, w_up[:, there])
        d_gated = mm_rt(cot_ref[...], w_down[here])
        phi = 0.5 + 0.5 * lax.erf(gate * half)
        shaped = gate * phi
        gated_ref[:, here] = (left * shaped).astype(BF16)
        slope = phi + gate * (jnp.exp(gate * gate * -0.5) * density)
        d_left = (d_gated * shaped).astype(BF16)
        d_gate = (d_gated * left * slope).astype(BF16)
        d_exp_ref[:, here] = d_left
        d_exp_ref[:, there] = d_gate
        part = mm_rt(d_left, w_up[:, here]) + mm_rt(d_gate, w_up[:, there])
        pulled = part if pulled is None else pulled + part
    gain_grad_ref[...] = jnp.sum(pulled * unit, axis=0, keepdims=True)
    inner = pulled * gain_feed
    d_middle = cot + scale * (inner - unit * jnp.mean(unit * inner, axis=-1, keepdims=True))
    middle_grad_ref[...] = d_middle
    branch = d_middle.astype(BF16)
    branch_ref[...] = branch
    d_mixed = mm_rt(branch, w_out)
    shrunk_ref[...] = (d_mixed * inverse_ref[...]).astype(BF16)
    d_mixed = d_mixed.astype(BF16)
    d_mixed_ref[...] = d_mixed
    level_rows = d_mixed.astype(F32) * mixed
    lane = lax.broadcasted_iota(jnp.int32, (width, 128), 1)
    head = lax.broadcasted_iota(jnp.int32, (width, 128), 0) // (width // heads)
    pick = jnp.where((lane % heads == head) & (lane < 2 * heads), 1.0, 0.0).astype(BF16)
    high = level_rows.astype(BF16)
    levels = mm(high, pick) + mm((level_rows - high.astype(F32)).astype(BF16), pick)
    high = levels.astype(BF16).astype(F32)
    lane = lax.broadcasted_iota(jnp.int32, levels.shape, 1)
    levels_ref[...] = jnp.where(lane < heads, high, levels - high).astype(BF16)


def weights_kernel(place, cot_ref, mixed_low_ref, normed_ref, gated_ref, d_exp_ref, branch_ref, mine_ref, other_ref):
    width, ups = cot_ref.shape[1], d_exp_ref.shape[1]
    split_parts(place, mm_lt(normed_ref[...], d_exp_ref[...]), mine_ref, other_ref, 0)
    split_parts(place, mm_lt(mixed_low_ref[...], branch_ref[...]), mine_ref, other_ref, ups)
    split_parts(place, mm_lt(gated_ref[...], cot_ref[...]), mine_ref, other_ref, ups + width)


def output_kernel(middle_ref, gated_ref, w_down_ref, out_ref):
    rows, cols, width = out_ref.shape
    total = (middle_ref[...] + mm(gated_ref[...], w_down_ref[...])).astype(BF16)
    count = rows * BAND
    for band in range(cols // BAND):
        out_ref[:, band * BAND : (band + 1) * BAND, :] = total[band * count : (band + 1) * count].reshape(
            rows, BAND, width
        )


def pull_head(grad, along, length, cos, sine, heads):
    first, second = halves(grad)
    along_first, along_second = halves(along)
    first, second = first * cos + second * sine, second * cos - first * sine
    ones_head = same_head(first.shape[1], first.shape[1] // heads)
    part = mm((along_first * first + along_second * second).astype(BF16), ones_head)
    grad = jnp.concatenate(
        [length * (first - along_first * part), length * (second - along_second * part)], axis=1
    )
    return grad.astype(BF16), jnp.sum(part, axis=0, keepdims=True)


def lane_sums(product):
    total = product[:, :128]
    for start in range(128, product.shape[1], 128):
        total = total + product[:, start : start + 128]
    return jnp.sum(jnp.transpose(total), axis=0, keepdims=True)


def normed_back_kernel(
    rows, place, w_ref, d_query_ref, d_rest_ref, own_ref, rim_swap_ref, rim_beside_ref
):
    width = own_ref.shape[1]
    count, edge = rows * BAND, REACH * BAND
    odd = place[5] == 1
    whole = mm_rt(d_rest_ref[...], w_ref[:, width:])
    own_ref[...] = mm_rt(d_query_ref[...], w_ref[:, :width]) + own_rows(whole, count)
    for band in range(whole.shape[0] // (2 * count)):
        start = 2 * band * count
        upper, lower = whole[start : start + edge], whole[start + edge + count : start + 2 * edge + count]
        here = slice(band * edge, (band + 1) * edge)
        rim_swap_ref[here] = jnp.where(odd, upper, lower).astype(BF16)
        rim_beside_ref[here] = jnp.where(odd, lower, upper).astype(BF16)


def features_kernel(place, inputs_ref, gain_ref, own_ref, rim_swap_ref, rim_beside_ref, middle_grad_ref, grad_ref):
    rows, cols, width = grad_ref.shape
    bands = cols // BAND
    count, edge = rows * BAND, REACH * BAND
    odd = place[5] == 1
    zeros = jnp.zeros((count - 2 * edge, width), F32)
    rims = []
    for band in range(bands):
        here = slice(band * edge, (band + 1) * edge)
        swapped, beside = rim_swap_ref[here].astype(F32), rim_beside_ref[here].astype(F32)
        rims += [jnp.where(odd, swapped, beside), zeros, jnp.where(odd, beside, swapped)]
    inner = (own_ref[...] + jnp.concatenate(rims, axis=0)) * gain_ref[0:1]
    inputs = inputs_ref[...]
    scale = norm_scale(inputs)
    unit = inputs * scale
    grad = middle_grad_ref[...] + scale * (inner - unit * jnp.mean(unit * inner, axis=-1, keepdims=True))
    for band in range(bands):
        grad_ref[:, band * BAND : (band + 1) * BAND, :] = grad[band * count : (band + 1) * count].reshape(
            rows, BAND, width
        )


def forward_kernel(
    heads, place, root_ref, unit_ref, cos_ref, sine_ref, mask_ref, inputs_ref, cot_ref,
    p0, p1, p2, p3, p4, p5, p6, p7,
    query_ref, key_ref, value_ref, raised_ref, inverse_rows_ref, mixed_ref, along_q_ref, length_q_ref, along_k_ref, length_k_ref,
    gain_ref, gain_col_ref, w_ref, middle_ref, middle_grad_ref, shrunk_ref, d_mixed_ref, levels_ref, gain_grad_ref,
    w_down_ref, gated_ref, mine_ref, other_ref,
    inverse_ref, w_up_ref, w_out_ref, mixed_low_ref, normed_ref, d_exp_ref, branch_ref,
):
    width = inputs_ref.shape[1]
    first, ups = 3 * width + 128, w_up_ref.shape[1]
    sums = jnp.zeros((8, 128), F32)
    for start, rows in place_parts(place, (p0, p1, p2, p3, p4, p5, p6, p7)):
        store_rows(w_ref, start, rows[:, :, : 3 * width])
        sums = sums + jnp.sum(rows[:, :, 3 * width : first], axis=0)
        store_rows(w_up_ref, start, rows[:, :, first : first + ups])
        store_rows(w_out_ref, start, rows[:, :, first + ups : first + ups + width])
        down = [rows[:, :, at : at + width] for at in range(first + ups + width, rows.shape[2], width)]
        store_rows(w_down_ref, start, jnp.concatenate(down, axis=1))
    attend_kernel(
        heads, root_ref, unit_ref, cos_ref, sine_ref, mask_ref, sums, w_ref,
        query_ref, key_ref, value_ref, raised_ref, mixed_ref, inverse_ref, inverse_rows_ref,
        along_q_ref, length_q_ref, along_k_ref, length_k_ref, gain_ref, gain_col_ref,
    )
    feed_kernel(
        heads, inputs_ref, cot_ref, w_up_ref, w_out_ref, gain_ref, mixed_ref, inverse_ref,
        middle_ref, middle_grad_ref, shrunk_ref, d_mixed_ref, levels_ref, gain_grad_ref,
        w_down_ref, mixed_low_ref, normed_ref, gated_ref, d_exp_ref, branch_ref,
    )
    weights_kernel(
        place, cot_ref, mixed_low_ref, normed_ref, gated_ref, d_exp_ref, branch_ref, mine_ref, other_ref
    )


def backward_kernel(
    heads, rows, place, root_ref, shrunk_ref, d_mixed_ref, levels_ref, raised_ref, inverse_rows_ref, query_ref, key_ref, value_ref,
    cos_ref, sine_ref, w_ref, gain_col_ref, unit_turned_ref, own_turned_ref, along_q_ref, length_q_ref,
    along_k_ref, length_k_ref, gain_grad_ref,
    d_query_ref, d_rest_ref, mine_ref, other_ref,
):
    bands, _, keys = raised_ref.shape
    count, edge = keys // 2, REACH * BAND
    width = shrunk_ref.shape[1]
    ones_half = jnp.ones((keys, 128), BF16)
    along_total = jnp.zeros((1, width // 2), F32)
    for band in range(bands):
        span = slice(band * count, (band + 1) * count)
        start = band * keys
        whole = slice(start, start + keys)
        own = slice(start + edge, start + edge + count)
        shrunk = shrunk_ref[span].astype(F32)
        d_mixed = d_mixed_ref[span].astype(F32)
        levels = levels_ref[span].astype(F32)
        lane = lax.broadcasted_iota(jnp.int32, levels.shape, 1)
        value = value_ref[whole, :]
        raised = raised_ref[band]
        parts, stacks = [], []
        for pair in range(heads // 2):
            lanes = slice(128 * pair, 128 * pair + 128)
            stacks.append(pair_lanes(shrunk, heads, pair))
            terms = jnp.concatenate(
                [jnp.where(lane % heads == h, -levels, 0.0) for h in (2 * pair, 2 * pair + 1)], axis=0
            ).astype(BF16)
            parts.append(
                mm_rt(
                    jnp.concatenate([pair_lanes(d_mixed, heads, pair), terms], axis=1),
                    jnp.concatenate([value[:, lanes], ones_half], axis=1),
                )
            )
        query = stack_heads(query_ref[span, :].astype(F32), heads)
        inverse = jnp.concatenate([inverse_rows_ref[band]] * (keys // 128), axis=1)
        probs = jnp.where(raised > 0, jnp.exp(mm_rt(query, key_ref[whole, :])) * inverse, 0.0)
        d_scores = (probs * jnp.concatenate(parts, axis=0)).astype(BF16)
        d_key = mm_lt(d_scores, query)
        d_query = fold_heads(mm(d_scores, key_ref[whole, :]), heads)
        for pair in range(heads // 2):
            lanes = slice(width + 128 * pair, width + 128 * pair + 128)
            d_value = mm_lt(raised[2 * pair * count : 2 * (pair + 1) * count], stacks[pair])
            d_rest_ref[whole, lanes] = d_value.astype(BF16)
        d_rest_ref[whole, :width], along_k = pull_head(
            d_key, along_k_ref[whole, :], length_k_ref[whole, :], cos_ref[whole, :], sine_ref[whole, :], heads
        )
        d_query_ref[span, :], along_q = pull_head(
            d_query, along_q_ref[span, :], length_q_ref[span, :], cos_ref[own, :], sine_ref[own, :], heads
        )
        along_total = along_total + along_k + along_q
    plain = jnp.concatenate(
        [mm(own_turned_ref[...], d_query_ref[...]), mm(unit_turned_ref[...], d_rest_ref[...])], axis=1
    )
    scaled = plain * jnp.concatenate([gain_col_ref[...]] * (3 * width // 128), axis=1)
    turned = jnp.concatenate([scaled[:, :width], scaled[:, width : 2 * width]], axis=0).astype(BF16)
    plain_order = mm_rt(turned, turned_order(width, heads))
    split_parts(place, plain_order[:width], mine_ref, other_ref, 0)
    split_parts(place, plain_order[width:], mine_ref, other_ref, width)
    split_parts(place, scaled[:, 2 * width :], mine_ref, other_ref, 2 * width)
    lines = []
    for total in (lane_sums(plain * w_ref[...].astype(F32)), gain_grad_ref[...]):
        lines += [total[:, :128], total[:, 128:]]
    total = along_total * 0.5 / root_ref[...]
    high = total.astype(BF16).astype(F32)
    lines += [high, total - high, jnp.zeros((2, 128), F32)]
    tail = jnp.concatenate(lines, axis=0).astype(BF16)
    for ref in (mine_ref, other_ref):
        ref[:, :, :, 3 * width :] = jnp.broadcast_to(tail[None, None], ref.shape[:2] + tail.shape)


def call(kernel, outs, scratch=(), place=None, smem=0, smem_out=0, flops=10**9, pin=True, aliases=None):
    if place is not None:
        kernel = functools.partial(kernel, place)

    def run(*args):
        args = [
            arg if i < smem else pltpu.with_memory_space_constraint(arg, pltpu.VMEM if pin else pltpu.HBM)
            for i, arg in enumerate(args)
        ]
        return pl.pallas_call(
            kernel,
            out_shape=outs,
            in_specs=[
                pl.BlockSpec(memory_space=pltpu.SMEM if i < smem else pltpu.VMEM)
                for i in range(len(args))
            ],
            out_specs=[
                pl.BlockSpec(memory_space=pltpu.SMEM if i >= len(outs) - smem_out else pltpu.VMEM)
                for i in range(len(outs))
            ],
            scratch_shapes=list(scratch),
            input_output_aliases=aliases or {},
            compiler_params=pltpu.CompilerParams(vmem_limit_bytes=VMEM_LIMIT),
            cost_estimate=pl.CostEstimate(flops=flops, bytes_accessed=4 * 10**6 if flops > 1 else 1, transcendentals=0),
        )(*args)

    return run


def rotation_tables(row_place, col_place, heads, size):
    part = size // 8
    lane = jnp.arange(heads * size // 2) % (size // 2)
    index = (lane % part).astype(F32)
    frequency = math.pi / 8.0 * jnp.exp(index * (-math.log(10.0) / part))
    group = lane // part

    def table(place, kind):
        angle = place.astype(F32)[:, None] * frequency
        cos = jnp.where(group == kind, jnp.cos(angle), 0.0)
        if kind:
            cos = jnp.where(group >= 2, 1.0, cos)
        return jnp.stack([cos, jnp.where(group == kind, jnp.sin(angle), 0.0)])

    return table(row_place, 0), table(col_place, 1)


def window_ids(crop_ids, row_start, rows):
    ids = jnp.pad(crop_ids[:, ::BAND], ((REACH, 2 * rows), (0, 0)), constant_values=-1)
    ids = lax.dynamic_slice_in_dim(ids, row_start, 2 * rows, 0)
    return jnp.repeat(ids, BAND, axis=0), jnp.repeat(ids.T, BAND, axis=1)


def on_device(
    features, crop_ids, conditioning, qkv_weight, out_weight, up_weight, down_weight,
    attn_cond_weight, feed_cond_weight, attention_scale, cotangent,
):
    rows, cols, width = features.shape
    heads = attention_scale.shape[0]
    size = width // heads
    bands = cols // BAND
    count = rows * BAND
    tokens = rows * cols
    edge = REACH * BAND
    n_rows, n_cols = lax.axis_size("rows"), lax.axis_size("cols")
    devices = n_rows * n_cols
    hidden = down_weight.shape[0] * devices
    own_cond = attn_cond_weight.shape[0]
    canvases = conditioning.shape[0]
    row, col = lax.axis_index("rows"), lax.axis_index("cols")
    row_start, col_start = row * rows, col * cols
    canvas = col_start // CANVAS
    group, chips = 4, 4
    chunks = 2 * chips * group
    direct = (n_rows, n_cols) == (2 * chips, group) and chunks * 8 == width
    first_lanes = 3 * width + 128
    second_lanes = 2 * hidden + width + hidden * width // (8 * chunks)
    per_canvas = max(n_cols // canvases, 1)
    place = Place(direct, cols, n_cols)

    def result(*dims, dtype=F32):
        return jax.ShapeDtypeStruct(dims, dtype)

    def shape(*dims, dtype=F32):
        return pltpu.VMEM(dims, dtype)

    def low(*dims):
        return shape(*dims, dtype=BF16)

    def over(axis, by):
        size_of = lax.axis_size(axis)
        return lambda value: lax.ppermute(value, axis, [(i, i ^ by) for i in range(size_of)])

    z_moves = [over("cols", k) for k in range(1, group)]
    xy_moves = [over("rows", 2 * m) for m in range(1, chips)]

    def chip_pairs(step):
        return [(i, i ^ (4 if i % 2 == step else 2)) for i in range(n_rows)]

    def first_chip(value):
        return lax.ppermute(value, "rows", chip_pairs(0))

    def second_chip(value):
        return lax.ppermute(value, "rows", chip_pairs(1))

    core_move = over("rows", 1)

    if direct:
        near, far, cond_own = call(
            functools.partial(pack_kernel, heads, per_canvas),
            [
                low(8, first_lanes + second_lanes),
                low(8, first_lanes + second_lanes),
                shape(own_cond, canvases),
            ],
            place=place,
            pin=False,
        )(conditioning, qkv_weight, up_weight, out_weight, down_weight, attn_cond_weight, feed_cond_weight)
        z_order = (3, 1, 2)
        line = call(functools.partial(line_kernel, z_order), [low(group, 8, first_lanes + second_lanes)], place=place)(
            near,
            *[z_moves[k - 1](near if k // per_canvas == 0 else far) for k in z_order],
        )[0]
        mine = [line] + [move(line) for move in xy_moves]
    else:
        def parts_of(full):
            full = full.reshape(chips, 2, group, 8, full.shape[-1])
            return [full[m, core] for core in range(2) for m in range(chips)]

        def whole(weight):
            return lax.all_gather(weight, AXES, axis=0, tiled=True)

        cond = lax.dynamic_slice_in_dim(conditioning, place[4] * own_cond, own_cond, 1)
        cond_own = cond.T.astype(F32)
        sums = [
            lax.psum(jnp.dot(cond, weight, preferred_element_type=F32), AXES)
            for weight in (attn_cond_weight, feed_cond_weight)
        ]
        lines = []
        for part in sums:
            part = lax.dynamic_slice_in_dim(part, canvas, 1, 0).reshape(-1, 128)
            high = lax.reduce_precision(part, 8, 7)
            lines += [high, part - high]
        lines = jnp.pad(jnp.concatenate(lines).astype(BF16), ((0, width - 8), (0, 0)))
        qkv = whole(qkv_weight)
        turned = jnp.argmax(turned_order(width, heads), axis=0)
        qkv = jnp.concatenate([qkv[:, :width][:, turned], qkv[:, width : 2 * width][:, turned], qkv[:, 2 * width :]], axis=1)
        down = whole(down_weight).reshape(chunks, -1, 8, width).transpose(0, 2, 1, 3).reshape(width, -1)
        parts = parts_of(
            jnp.concatenate([qkv, lines, whole(up_weight), whole(out_weight), down], axis=1)
        )

    odd = row % 2 == 1
    beside_pairs = [(i, (i + 1 if i % 2 else i - 1) % n_rows) for i in range(n_rows)]

    def beside_move(value):
        return lax.ppermute(value, "rows", beside_pairs)

    first_rows, last_rows = features[:REACH], features[rows - REACH :]
    halo_swap = core_move(jnp.where(odd, first_rows, last_rows))
    halo_beside = beside_move(jnp.where(odd, last_rows, first_rows))

    row_place = row_start - REACH + jnp.arange(2 * rows, dtype=jnp.int32)
    col_place = (col_start + jnp.arange(cols, dtype=jnp.int32)) % CANVAS
    row_table, col_table = rotation_tables(row_place, col_place, heads, size)
    id_query, id_key = window_ids(crop_ids, row_start, rows)

    unit, unit_turned, own_turned, cos, sine, mask, inputs, cot, root = call(
        functools.partial(ready_kernel, heads),
        [
            shape(2 * tokens, width),
            low(width, 2 * tokens),
            low(width, tokens),
            shape(2 * tokens, width // 2),
            shape(2 * tokens, width // 2),
            low(bands, count, 2 * count),
            shape(tokens, width),
            low(tokens, width),
            shape(1, width // 2),
        ],
        place=place,
        smem=1,
    )(attention_scale, features, cotangent, halo_swap, halo_beside, row_table, col_table, id_query, id_key)
    if direct:
        mine = mine[:1] + [lax.optimization_barrier((part, unit))[0] for part in mine[1:]]
        far = core_move(mine[3])
        for i in (1, 2):
            mine[i], far = lax.optimization_barrier((mine[i], far))
        parts = mine + [core_move(part) for part in mine[:3]] + [far]

    (
        query, key, value, raised, inverse_rows, mixed, along_q, length_q, along_k, length_k, gain, gain_col, w_qkv,
        middle, middle_grad, shrunk, d_mixed, levels, gain_grad, w_down, gated, mine_second, other_second,
    ) = call(
        functools.partial(forward_kernel, heads),
        [
            low(tokens, width),
            low(2 * tokens, width),
            low(2 * tokens, width),
            low(bands, heads * count, 2 * count),
            shape(bands, heads * count, 128),
            shape(tokens, width),
            shape(tokens, width),
            shape(tokens, width // 2),
            shape(2 * tokens, width),
            shape(2 * tokens, width // 2),
            shape(2, width),
            shape(width, 128),
            low(width, 3 * width),
            shape(tokens, width),
            shape(tokens, width),
            low(tokens, width),
            low(tokens, width),
            low(tokens, 128),
            shape(1, width),
            low(hidden, width),
            low(tokens, hidden),
            low(chips, group, 8, second_lanes),
            low(chips, group, 8, second_lanes),
        ],
        scratch=[
            pltpu.VMEM((tokens, width), F32),
            pltpu.VMEM((width, 2 * hidden), BF16),
            pltpu.VMEM((width, width), BF16),
            pltpu.VMEM((tokens, width), BF16),
            pltpu.VMEM((tokens, width), BF16),
            pltpu.VMEM((tokens, 2 * hidden), BF16),
            pltpu.VMEM((tokens, width), BF16),
        ],
        place=place,
    )(root, unit, cos, sine, mask, inputs, cot, *parts)

    d_query, d_rest, mine_first, other_first = call(
        functools.partial(backward_kernel, heads, rows),
        [
            low(tokens, width),
            low(2 * tokens, 2 * width),
            low(chips, group, 8, first_lanes),
            low(chips, group, 8, first_lanes),
        ],
        place=place,
        flops=1,
    )(
        root, shrunk, d_mixed, levels, raised, inverse_rows, query, key, value, cos, sine, w_qkv, gain_col, unit_turned, own_turned,
        along_q, length_q, along_k, length_k, gain_grad,
    )

    def last_output(gated):
        return call(output_kernel, [result(rows, cols, width, dtype=BF16)])(middle, gated, w_down)[0]

    def normed_back(d_query, d_rest):
        return call(
            functools.partial(normed_back_kernel, rows),
            [shape(tokens, width), low(bands * edge, width), low(bands * edge, width)],
            place=place,
        )(w_qkv, d_query, d_rest)

    def last_features(own, rim_swap, rim_beside):
        return call(features_kernel, [result(rows, cols, width)], place=place)(
            inputs, gain, own, rim_swap, rim_beside, middle_grad
        )[0]

    if direct:
        all_lanes = second_lanes + first_lanes
        def core_sum(carry, mine, got):
            return call(functools.partial(core_sum_kernel, carry), [low(group, 8, mine.shape[-1]) for _ in range(chips)], place=place)(mine, got)

        def pair_sum(carry, one, two):
            return call(functools.partial(pair_sum_kernel, carry), [low(*one.shape)], flops=1)(one, two)[0]

        first_got = core_move(other_first)
        second_own, second_near, second_beside, second_far = core_sum(False, mine_second, core_move(other_second))
        second_far = second_chip(second_far)
        first_own, first_near, first_beside, first_far = core_sum(True, mine_first, first_got)
        first_far = second_chip(first_far)
        second_far, first_far = lax.optimization_barrier((second_far, first_far))
        first_own, d_rest = lax.optimization_barrier((first_own, d_rest))
        beside = second_chip(call(join_kernel, [low(group, 8, all_lanes)], flops=1)(second_beside, first_beside)[0])
        sums = [
            second_own,
            first_chip(pair_sum(False, second_near, second_far)),
            first_own,
            first_chip(pair_sum(True, first_near, first_far)),
            beside,
        ]
        own_grad, rim_swap, rim_beside = normed_back(d_query, d_rest)
        rim_swap, rim_beside = core_move(rim_swap), beside_move(rim_beside)
        blocks = call(
            chip_sum_kernel,
            [shape(8, all_lanes)] + [low(8, all_lanes) for _ in z_moves],
            scratch=[pltpu.VMEM((group, 8, all_lanes), F32)],
            place=place,
        )(*sums)
        blocks, gated, own_grad = lax.optimization_barrier((blocks, gated, own_grad))
        output = last_output(gated)
        grad_features = last_features(own_grad, rim_swap, rim_beside)
        grad_qkv, grad_out, grad_up, grad_down, grad_attn_cond, grad_feed_cond, grad_scale = call(
            functools.partial(last_kernel, per_canvas, size // 2),
            [
                result(8, 3 * width),
                result(8, width),
                result(8, 2 * hidden),
                result(hidden // chunks, width),
                result(own_cond, width),
                result(own_cond, width),
                result(heads),
            ],
            place=place,
            smem_out=1,
        )(cond_own, blocks[0], *[move(block) for move, block in reversed(list(zip(z_moves, blocks[1:])))])
    else:
        own_grad, rim_swap, rim_beside = normed_back(d_query, d_rest)
        grad_features = last_features(own_grad, core_move(rim_swap), beside_move(rim_beside))
        output = last_output(gated)

        def joined(mine, other):
            return jnp.stack([mine, other], axis=1).astype(F32).reshape(chunks, 8, mine.shape[-1])

        def scattered(grad):
            return lax.psum_scatter(grad.reshape(-1, grad.shape[-1]), AXES, scatter_dimension=0, tiled=True)

        last = joined(mine_first, other_first)
        second = joined(mine_second, other_second)
        ups = 2 * hidden
        grad_qkv = scattered(last[:, :, : 3 * width])
        grad_up = scattered(second[:, :, :ups])
        grad_out = scattered(second[:, :, ups : ups + width])
        grad_down = scattered(
            second[:, :, ups + width :].reshape(chunks, 8, -1, width).transpose(0, 2, 1, 3)
        )
        spot = (jnp.arange(canvases) == canvas).astype(F32)[:, None, None]
        tail = lax.psum(spot * last[0, :, 3 * width :][None], AXES)

        def cond_grad(sums):
            return jnp.sum(cond_own[:, :, None] * sums.reshape(canvases, width)[None], axis=1)

        grad_attn_cond = cond_grad(tail[:, 0:2])
        grad_feed_cond = cond_grad(tail[:, 2:4])
        grad_scale = jnp.sum(tail[:, 4] + tail[:, 5], axis=0)[:: size // 2]
    return (
        output, grad_features, grad_qkv, grad_out, grad_up, grad_down, grad_attn_cond, grad_feed_cond, grad_scale,
    )


def solution(mesh):
    tile, whole, split = P("rows", "cols", None), P(), P(AXES, None)
    return jax.shard_map(
        on_device,
        mesh=mesh,
        in_specs=(tile, P(None, "cols"), whole, split, split, split, split, split, split, whole, tile),
        out_specs=(tile, tile, split, split, split, split, split, split, whole),
        check_vma=False,
    )
```

```python
import functools
import math

import jax
import jax.numpy as jnp
from jax import lax
from jax.experimental import pallas as pl
from jax.experimental.pallas import tpu as pltpu
from jax.sharding import PartitionSpec as P

CANVAS = 128
BAND = 16
REACH = 3
AXES = ("rows", "cols")
F32 = jnp.float32
BF16 = jnp.bfloat16
EPS = 1e-06
VMEM_LIMIT = 32 * 1024 * 1024


class Place:
    def __init__(self, direct, cols, n_cols):
        self.direct, self.cols, self.n_cols = direct, cols, n_cols

    def __getitem__(self, item):
        row, col = lax.axis_index("rows"), lax.axis_index("cols")
        if item == 0:
            return col * self.cols // CANVAS
        if item == 4:
            return row * self.n_cols + col
        if item == 5:
            return lax.rem(row, 2)
        if not self.direct:
            return (0, 0, 0, 0, 0, 0, 1)[item]
        return (None, row // 2, lax.rem(row, 2), col, None, None, 2 - lax.rem(row, 2))[item]


def mm(left, right):
    return lax.dot_general(left, right, (((1,), (0,)), ((), ())), preferred_element_type=F32)


def mm_rt(left, right):
    return lax.dot_general(left, right, (((1,), (1,)), ((), ())), preferred_element_type=F32)


def mm_lt(left, right):
    return lax.dot_general(left, right, (((0,), (0,)), ((), ())), preferred_element_type=F32)


def same_head(width, size):
    first = lax.broadcasted_iota(jnp.int32, (width, width), 0) // size
    second = lax.broadcasted_iota(jnp.int32, (width, width), 1) // size
    return jnp.where(first == second, 1.0, 0.0).astype(BF16)


def stack_heads(values, heads):
    lane = head_of(values.shape, heads)
    return jnp.concatenate(
        [jnp.where(lane == h, values, 0.0).astype(BF16) for h in range(heads)], axis=0
    )


def fold_heads(values, heads):
    count = values.shape[0] // heads
    lane = head_of((count, values.shape[1]), heads)
    total = values[:count]
    for h in range(1, heads):
        total = jnp.where(lane == h, values[h * count : (h + 1) * count], total)
    return total


def turned_order(width, heads):
    size = width // heads
    part = size // 8
    row = lax.broadcasted_iota(jnp.int32, (width, width), 0)
    col = lax.broadcasted_iota(jnp.int32, (width, width), 1)
    half, lane = col // (width // 2), col % (width // 2)
    head, j = lane // (size // 2), lane % (size // 2)
    rotated = j // part * 2 * part + j % part + half * part
    kept = 4 * part + j - 2 * part + half * 2 * part
    return jnp.where(row == head * size + jnp.where(j < 2 * part, rotated, kept), 1.0, 0.0).astype(BF16)


def halves(values):
    half = values.shape[1] // 2
    return values[:, :half], values[:, half:]


def head_of(shape, heads):
    half = shape[1] // 2
    return lax.broadcasted_iota(jnp.int32, shape, 1) % half // (half // heads)


def own_rows(values, count):
    edge = REACH * BAND
    return jnp.concatenate(
        [values[start + edge : start + edge + count] for start in range(0, values.shape[0], 2 * count)], axis=0
    )


def bands_of(ref, bands):
    parts = [
        ref[:, band * BAND : (band + 1) * BAND, :].astype(F32).reshape(-1, ref.shape[-1])
        for band in range(bands)
    ]
    return jnp.concatenate(parts, axis=0)


def pair_lanes(values, heads, pair):
    size = values.shape[1] // heads
    part = values[:, 128 * pair : 128 * pair + 128]
    lane = lax.broadcasted_iota(jnp.int32, part.shape, 1)
    return jnp.concatenate(
        [jnp.where(lane < size, part, 0.0), jnp.where(lane < size, 0.0, part)], axis=0
    ).astype(BF16)


def merge_pair(values, size):
    count = values.shape[0] // 2
    lane = lax.broadcasted_iota(jnp.int32, (count, 128), 1)
    return jnp.where(lane < size, values[:count], values[count:])


def close(shape, query_row, key_row):
    token = lax.broadcasted_iota(jnp.int32, shape, 0)
    place = lax.broadcasted_iota(jnp.int32, shape, 1)
    return (jnp.abs(token // BAND + query_row - place // BAND - key_row) <= REACH) & (
        jnp.abs(token % BAND - place % BAND) <= REACH
    )


def norm_scale(values):
    return lax.rsqrt(jnp.mean(values * values, axis=-1, keepdims=True) + EPS)


def place_parts(place, part_refs):
    for index, part in enumerate(part_refs):
        chip = place[1] ^ (index % 4)
        core = place[2] ^ (index // 4)
        group = part.shape[0]
        yield (chip * 2 + core) * group, part[...].astype(F32)


def store_rows(ref, start, rows):
    group, count, lanes = rows.shape
    ref[pl.ds(pl.multiple_of(start * count, group * count), group * count), :] = rows.reshape(
        group * count, lanes
    ).astype(ref.dtype)


def split_parts(place, values, mine_ref, other_ref, start):
    chips, group = mine_ref.shape[:2]
    count = values.shape[0] // (2 * chips)
    first = place[2] == 0
    for chip in range(chips):
        zero, one = [values[(2 * chip + core) * count : (2 * chip + core + 1) * count] for core in range(2)]
        for ref, part in ((mine_ref, jnp.where(first, zero, one)), (other_ref, jnp.where(first, one, zero))):
            part = part.reshape(group, count // group, values.shape[1])
            for i in range(count // group // 8):
                at = start + i * values.shape[1]
                ref[chip, :, :, at : at + values.shape[1]] = part[:, 8 * i : 8 * i + 8].astype(BF16)


def pack_kernel(
    heads, per_canvas, place, cond_ref, qkv_ref, up_ref, out_ref, down_ref, attn_ref, feed_ref,
    near_ref, far_ref, both_ref, cond_own_ref,
):
    own = attn_ref.shape[0]
    canvases, total = cond_ref.shape
    width = out_ref.shape[1]
    row = lax.broadcasted_iota(jnp.int32, (own, total), 0) + place[4] * own
    pick = jnp.where(row == lax.broadcasted_iota(jnp.int32, (own, total), 1), 1.0, 0.0).astype(BF16)
    cond = mm_rt(pick, cond_ref[...])
    cond_own_ref[...] = cond
    tails = []
    for canvas in range(canvases):
        lines = []
        for weight_ref in (attn_ref, feed_ref):
            line = jnp.sum(
                cond[:, canvas : canvas + 1] * weight_ref[...].astype(F32), axis=0, keepdims=True
            )
            high = line.astype(BF16).astype(F32)
            for part in (high, line - high):
                lines += [part[:, :128], part[:, 128:]]
        tails.append(jnp.concatenate(lines, axis=0))
    down = down_ref[...].astype(F32)
    parts = [up_ref[...], out_ref[...]] + [down[8 * i : 8 * i + 8].astype(BF16) for i in range(down.shape[0] // 8)]
    qkv = qkv_ref.shape[1]
    turned = mm(
        jnp.concatenate([qkv_ref[:, :width], qkv_ref[:, width : 2 * width]], axis=0).astype(F32).astype(BF16),
        turned_order(width, heads),
    ).astype(BF16)
    mine = place[0] == 0
    near, far = jnp.where(mine, tails[0], tails[1]), jnp.where(mine, tails[1], tails[0])
    both_ref[:, both_ref.shape[1] - 128 :] = far.astype(BF16)
    for ref, tail in ((near_ref, near), (far_ref, far), (both_ref, near)):
        ref[:, :width], ref[:, width : 2 * width] = turned[:8], turned[8:]
        ref[:, 2 * width : qkv] = qkv_ref[:, 2 * width :]
        ref[:, qkv : qkv + 128] = tail.astype(BF16)
        at = qkv + 128
        for part in parts:
            ref[:, at : at + part.shape[1]] = part
            at += part.shape[1]


def again_kernel(at, both_ref, near_ref, far_ref):
    lanes = near_ref.shape[1]
    near_ref[...] = both_ref[:, :lanes]
    far_ref[...] = both_ref[:, :lanes]
    far_ref[:, at : at + 128] = both_ref[:, lanes:]


def line_kernel(order, place, p0, p1, p2, p3, line_ref):
    for index, part in zip((0,) + order, (p0, p1, p2, p3)):
        line_ref[place[3] ^ index] = part[...]


def carried(total):
    tail = total[..., total.shape[-1] - 128 :]
    value = tail[..., 4:5, :] + tail[..., 5:6, :]
    high = value.astype(BF16).astype(F32)
    row = lax.broadcasted_iota(jnp.int32, tail.shape, tail.ndim - 2)
    tail = jnp.where(row == 4, high, jnp.where(row == 5, value - high, tail))
    return jnp.concatenate([total[..., : total.shape[-1] - 128], tail], axis=-1)


def core_sum_kernel(carry, place, mine_ref, got_ref, *outs):
    for index, out_ref in enumerate(outs):
        chip = place[1] ^ (0, place[6], place[6] ^ 3, 3)[index]
        total = mine_ref[chip].astype(F32) + got_ref[chip].astype(F32)
        out_ref[...] = (carried(total) if carry else total).astype(BF16)


def join_kernel(one_ref, two_ref, out_ref):
    split = one_ref.shape[-1]
    out_ref[:, :, :split] = one_ref[...]
    out_ref[:, :, split:] = two_ref[...]


def pair_sum_kernel(carry, one_ref, two_ref, out_ref):
    total = one_ref[...].astype(F32) + two_ref[...].astype(F32)
    out_ref[...] = (carried(total) if carry else total).astype(BF16)


def chip_sum_kernel(place, p0, p1, q0, q1, both, o0, o1, o2, o3, keep_ref):
    split = p0.shape[-1]
    keep_ref[:, :, :split] = p0[...].astype(F32) + p1[...].astype(F32) + both[:, :, :split].astype(F32)
    keep_ref[:, :, split:] = carried(
        q0[...].astype(F32) + q1[...].astype(F32) + both[:, :, split:].astype(F32)
    )
    for index, out_ref in enumerate((o0, o1, o2, o3)):
        out_ref[...] = keep_ref[place[3] ^ index].astype(out_ref.dtype)


def last_kernel(
    per_canvas, size, place, cond_ref, own_ref, three_ref, two_ref, one_ref,
    qkv_ref, out_ref, up_ref, down_ref, attn_ref, feed_ref, scale_ref,
):
    parts = [own_ref[...]] + [ref[...].astype(F32) for ref in (one_ref, two_ref, three_ref)]
    total = parts[0] + parts[1] + parts[2] + parts[3]
    width = out_ref.shape[1]
    at = up_ref.shape[1]
    up_ref[...] = total[:, :at]
    out_ref[...] = total[:, at : at + width]
    for i in range(down_ref.shape[0] // 8):
        at += width
        down_ref[8 * i : 8 * i + 8, :] = total[:, at : at + width]
    at += width
    qkv_ref[...] = total[:, at : at + qkv_ref.shape[1]]
    at += qkv_ref.shape[1]
    cond = cond_ref[...]
    attn, feed = 0.0, 0.0
    for canvas in range(cond.shape[1]):
        tail = jnp.zeros((8, 128), F32)
        for index, part in enumerate(parts):
            same = (place[3] ^ index) // per_canvas == canvas
            tail = tail + jnp.where(same, part[:, at:], 0.0)
        weight = cond[:, canvas : canvas + 1]
        attn = attn + weight * jnp.concatenate([tail[0:1], tail[1:2]], axis=1)
        feed = feed + weight * jnp.concatenate([tail[2:3], tail[3:4]], axis=1)
    attn_ref[...] = attn
    feed_ref[...] = feed
    tail = total[:, at:]
    scale = tail[4:5] + tail[5:6]
    for h in range(scale_ref.shape[0]):
        scale_ref[h] = scale[0, h * size]


def ready_kernel(
    heads, place, scale_ref, feat_ref, cot_ref, swap_ref, beside_ref, row_ref, col_ref, id_query_ref, id_key_ref,
    unit_ref, unit_turned_ref, own_turned_ref, cos_ref, sine_ref, mask_ref, inputs_ref, cot_out_ref, root_ref,
):
    rows, cols, width = feat_ref.shape
    count = rows * BAND
    bands = cols // BAND
    odd = place[5] == 1
    near = close((count, 2 * count), REACH, 0)
    lane = lax.broadcasted_iota(jnp.int32, (1, width // 2), 1) // (width // 2 // heads)
    root = jnp.zeros((1, width // 2), F32)
    for h in range(heads):
        root = jnp.where(lane == h, scale_ref[h], root)
    root_ref[...] = jnp.sqrt(root)
    inputs_ref[...] = bands_of(feat_ref, bands)
    cot_out_ref[...] = bands_of(cot_ref, bands).astype(BF16)
    for band in range(bands):
        part = slice(band * BAND, (band + 1) * BAND)
        swapped = swap_ref[:, part, :].astype(F32)
        beside = beside_ref[:, part, :].astype(F32)
        full = jnp.concatenate(
            [
                jnp.where(odd, swapped, beside),
                feat_ref[:, part, :].astype(F32),
                jnp.where(odd, beside, swapped),
                jnp.zeros((2, BAND, width), F32),
            ],
            axis=0,
        ).reshape(2 * count, width)
        span = slice(2 * band * count, 2 * (band + 1) * count)
        unit = full * norm_scale(full)
        unit_ref[span] = unit
        turned = jnp.transpose(unit).astype(BF16)
        unit_turned_ref[:, span] = turned
        own = slice(REACH * BAND, REACH * BAND + count)
        own_turned_ref[:, band * count : (band + 1) * count] = jnp.transpose(unit[own]).astype(BF16)
        for i, ref in enumerate((cos_ref, sine_ref)):
            ref[span] = (row_ref[i][:, None, :] + col_ref[i, part, :][None]).reshape(2 * count, width // 2)
        alike = id_query_ref[REACH * BAND : REACH * BAND + count, band : band + 1] == id_key_ref[
            band : band + 1, :
        ]
        mask_ref[band] = jnp.where(near & alike, 1.0, 0.0).astype(BF16)


def attend_kernel(
    heads, root_ref, unit_ref, cos_ref, sine_ref, mask_ref, sums, w_ref,
    query_ref, key_ref, value_ref, raised_ref, exact_ref, mixed_ref, inverse_ref, inverse_rows_ref, along_q_ref, length_q_ref, along_k_ref, length_k_ref,
    gain_ref, gain_col_ref,
):
    bands, count = mask_ref.shape[:2]
    width = unit_ref.shape[1]
    size = width // heads
    weight = w_ref[...]
    pairs = [sums[i : i + 2] + sums[i + 2 : i + 4] for i in (0, 4)]
    picked = 1.0 + jnp.concatenate(
        [jnp.concatenate([pair[0:1], pair[1:2]], axis=1) for pair in pairs], axis=0
    )
    gain_ref[...] = picked
    gain_col_ref[...] = jnp.transpose(jnp.broadcast_to(picked[0:1], (128, width)))
    root = root_ref[...]
    unit = unit_ref[...]
    normed = (unit * picked[0:1]).astype(BF16)
    value_ref[...] = mm(normed, weight[:, 2 * width :]).astype(BF16)
    ones_head = same_head(width // 2, size // 2)
    cos, sine = cos_ref[...], sine_ref[...]
    own = [own_rows(part, count) for part in (normed, cos, sine)]
    for i, (ref, along_ref, length_ref, (rows, cos, sine)) in enumerate(
        (
            (query_ref, along_q_ref, length_q_ref, own),
            (key_ref, along_k_ref, length_k_ref, (normed, cos, sine)),
        )
    ):
        first, second = halves(mm(rows, weight[:, i * width : (i + 1) * width]))
        short = lax.rsqrt(mm((first * first + second * second).astype(BF16), ones_head) + EPS)
        length = short * root
        ref[...] = jnp.concatenate(
            [(first * cos - second * sine) * length, (second * cos + first * sine) * length], axis=1
        ).astype(BF16)
        along_ref[...] = jnp.concatenate([first * short, second * short], axis=1)
        length_ref[...] = length
    ones_half = jnp.ones((2 * count, 128), BF16)
    for band in range(bands):
        start = 2 * band * count
        span = slice(band * count, (band + 1) * count)
        query = query_ref[span, :].astype(F32)
        scores = mm_rt(stack_heads(query, heads), key_ref[start : start + 2 * count, :])
        exact = jnp.exp(scores)
        exact_ref[band] = exact
        raised = exact.astype(BF16) * jnp.concatenate([mask_ref[band]] * heads, axis=0)
        raised_ref[band] = raised
        value = value_ref[start : start + 2 * count, :]
        for pair in range(heads // 2):
            lanes = slice(128 * pair, 128 * pair + 128)
            both = mm(
                raised[2 * pair * count : 2 * (pair + 1) * count],
                jnp.concatenate([value[:, lanes], ones_half], axis=1),
            )
            rows_inverse = 1.0 / both[:, 128:]
            inverse_rows_ref[band, 2 * pair * count : 2 * (pair + 1) * count, :] = rows_inverse
            inverse = merge_pair(rows_inverse, size)
            mixed_ref[span, lanes] = merge_pair(both[:, :128], size) * inverse
            inverse_ref[span, lanes] = inverse


def feed_kernel(
    heads, inputs_ref, cot_ref, w_up_ref, w_out_ref, gain_ref, mixed_ref, inverse_ref,
    middle_ref, middle_grad_ref, shrunk_ref, d_mixed_ref, levels_ref, gain_grad_ref,
    w_down_ref, mixed_low_ref, normed_ref, gated_ref, d_exp_ref, branch_ref,
):
    width = inputs_ref.shape[1]
    hidden = w_down_ref.shape[0]
    w_up, w_out, w_down = w_up_ref[...], w_out_ref[...], w_down_ref[...]
    gain_feed = gain_ref[1:2]
    mixed = mixed_ref[...]
    mixed_low = mixed.astype(BF16)
    mixed_low_ref[...] = mixed_low
    middle = inputs_ref[...] + mm(mixed_low, w_out)
    middle_ref[...] = middle
    scale = norm_scale(middle)
    unit = middle * scale
    normed = (unit * gain_feed).astype(BF16)
    normed_ref[...] = normed
    cot = cot_ref[...].astype(F32)
    half = math.sqrt(0.5)
    density = 1.0 / math.sqrt(2.0 * math.pi)
    pulled = None
    for start in range(0, hidden, width):
        here = slice(start, start + width)
        there = slice(hidden + start, hidden + start + width)
        left = mm(normed, w_up[:, here])
        gate = mm(normed, w_up[:, there])
        d_gated = mm_rt(cot_ref[...], w_down[here])
        phi = 0.5 + 0.5 * lax.erf(gate * half)
        shaped = gate * phi
        gated_ref[:, here] = (left * shaped).astype(BF16)
        slope = phi + gate * (jnp.exp(gate * gate * -0.5) * density)
        d_left = (d_gated * shaped).astype(BF16)
        d_gate = (d_gated * left * slope).astype(BF16)
        d_exp_ref[:, here] = d_left
        d_exp_ref[:, there] = d_gate
        part = mm_rt(d_left, w_up[:, here]) + mm_rt(d_gate, w_up[:, there])
        pulled = part if pulled is None else pulled + part
    gain_grad_ref[...] = jnp.sum(pulled * unit, axis=0, keepdims=True)
    inner = pulled * gain_feed
    d_middle = cot + scale * (inner - unit * jnp.mean(unit * inner, axis=-1, keepdims=True))
    middle_grad_ref[...] = d_middle
    branch = d_middle.astype(BF16)
    branch_ref[...] = branch
    d_mixed = mm_rt(branch, w_out)
    shrunk_ref[...] = (d_mixed * inverse_ref[...]).astype(BF16)
    d_mixed = d_mixed.astype(BF16)
    d_mixed_ref[...] = d_mixed
    level_rows = d_mixed.astype(F32) * mixed
    lane = lax.broadcasted_iota(jnp.int32, (width, 128), 1)
    head = lax.broadcasted_iota(jnp.int32, (width, 128), 0) // (width // heads)
    pick = jnp.where((lane % heads == head) & (lane < 2 * heads), 1.0, 0.0).astype(BF16)
    high = level_rows.astype(BF16)
    levels = mm(high, pick) + mm((level_rows - high.astype(F32)).astype(BF16), pick)
    high = levels.astype(BF16).astype(F32)
    lane = lax.broadcasted_iota(jnp.int32, levels.shape, 1)
    levels_ref[...] = jnp.where(lane < heads, high, levels - high).astype(BF16)


def weights_kernel(place, cot_ref, mixed_low_ref, normed_ref, gated_ref, d_exp_ref, branch_ref, mine_ref, other_ref):
    width, ups = cot_ref.shape[1], d_exp_ref.shape[1]
    split_parts(place, mm_lt(normed_ref[...], d_exp_ref[...]), mine_ref, other_ref, 0)
    split_parts(place, mm_lt(mixed_low_ref[...], branch_ref[...]), mine_ref, other_ref, ups)
    split_parts(place, mm_lt(gated_ref[...], cot_ref[...]), mine_ref, other_ref, ups + width)


def output_kernel(middle_ref, gated_ref, w_down_ref, out_ref):
    rows, cols, width = out_ref.shape
    total = (middle_ref[...] + mm(gated_ref[...], w_down_ref[...])).astype(BF16)
    count = rows * BAND
    for band in range(cols // BAND):
        out_ref[:, band * BAND : (band + 1) * BAND, :] = total[band * count : (band + 1) * count].reshape(
            rows, BAND, width
        )


def pull_head(grad, along, length, cos, sine, heads):
    first, second = halves(grad)
    along_first, along_second = halves(along)
    first, second = first * cos + second * sine, second * cos - first * sine
    ones_head = same_head(first.shape[1], first.shape[1] // heads)
    part = mm((along_first * first + along_second * second).astype(BF16), ones_head)
    grad = jnp.concatenate(
        [length * (first - along_first * part), length * (second - along_second * part)], axis=1
    )
    return grad.astype(BF16), jnp.sum(part, axis=0, keepdims=True)


def lane_sums(product):
    total = product[:, :128]
    for start in range(128, product.shape[1], 128):
        total = total + product[:, start : start + 128]
    return jnp.sum(jnp.transpose(total), axis=0, keepdims=True)


def normed_back_kernel(
    rows, place, w_ref, d_query_ref, d_rest_ref, own_ref, rim_swap_ref, rim_beside_ref
):
    width = own_ref.shape[1]
    count, edge = rows * BAND, REACH * BAND
    odd = place[5] == 1
    whole = mm_rt(d_rest_ref[...], w_ref[:, width:])
    own_ref[...] = mm_rt(d_query_ref[...], w_ref[:, :width]) + own_rows(whole, count)
    for band in range(whole.shape[0] // (2 * count)):
        start = 2 * band * count
        upper, lower = whole[start : start + edge], whole[start + edge + count : start + 2 * edge + count]
        here = slice(band * edge, (band + 1) * edge)
        rim_swap_ref[here] = jnp.where(odd, upper, lower).astype(BF16)
        rim_beside_ref[here] = jnp.where(odd, lower, upper).astype(BF16)


def features_kernel(place, inputs_ref, gain_ref, own_ref, rim_swap_ref, rim_beside_ref, middle_grad_ref, grad_ref):
    rows, cols, width = grad_ref.shape
    bands = cols // BAND
    count, edge = rows * BAND, REACH * BAND
    odd = place[5] == 1
    zeros = jnp.zeros((count - 2 * edge, width), F32)
    rims = []
    for band in range(bands):
        here = slice(band * edge, (band + 1) * edge)
        swapped, beside = rim_swap_ref[here].astype(F32), rim_beside_ref[here].astype(F32)
        rims += [jnp.where(odd, swapped, beside), zeros, jnp.where(odd, beside, swapped)]
    inner = (own_ref[...] + jnp.concatenate(rims, axis=0)) * gain_ref[0:1]
    inputs = inputs_ref[...]
    scale = norm_scale(inputs)
    unit = inputs * scale
    grad = middle_grad_ref[...] + scale * (inner - unit * jnp.mean(unit * inner, axis=-1, keepdims=True))
    for band in range(bands):
        grad_ref[:, band * BAND : (band + 1) * BAND, :] = grad[band * count : (band + 1) * count].reshape(
            rows, BAND, width
        )


def forward_kernel(
    heads, place, root_ref, unit_ref, cos_ref, sine_ref, mask_ref, inputs_ref, cot_ref,
    p0, p1, p2, p3, p4, p5, p6, p7,
    query_ref, key_ref, value_ref, raised_ref, exact_ref, inverse_rows_ref, mixed_ref, along_q_ref, length_q_ref, along_k_ref, length_k_ref,
    gain_ref, gain_col_ref, w_ref, middle_ref, middle_grad_ref, shrunk_ref, d_mixed_ref, levels_ref, gain_grad_ref,
    w_down_ref, gated_ref, mine_ref, other_ref,
    inverse_ref, w_up_ref, w_out_ref, mixed_low_ref, normed_ref, d_exp_ref, branch_ref,
):
    width = inputs_ref.shape[1]
    first, ups = 3 * width + 128, w_up_ref.shape[1]
    sums = jnp.zeros((8, 128), F32)
    for start, rows in place_parts(place, (p0, p1, p2, p3, p4, p5, p6, p7)):
        store_rows(w_ref, start, rows[:, :, : 3 * width])
        sums = sums + jnp.sum(rows[:, :, 3 * width : first], axis=0)
        store_rows(w_up_ref, start, rows[:, :, first : first + ups])
        store_rows(w_out_ref, start, rows[:, :, first + ups : first + ups + width])
        down = [rows[:, :, at : at + width] for at in range(first + ups + width, rows.shape[2], width)]
        store_rows(w_down_ref, start, jnp.concatenate(down, axis=1))
    attend_kernel(
        heads, root_ref, unit_ref, cos_ref, sine_ref, mask_ref, sums, w_ref,
        query_ref, key_ref, value_ref, raised_ref, exact_ref, mixed_ref, inverse_ref, inverse_rows_ref,
        along_q_ref, length_q_ref, along_k_ref, length_k_ref, gain_ref, gain_col_ref,
    )
    feed_kernel(
        heads, inputs_ref, cot_ref, w_up_ref, w_out_ref, gain_ref, mixed_ref, inverse_ref,
        middle_ref, middle_grad_ref, shrunk_ref, d_mixed_ref, levels_ref, gain_grad_ref,
        w_down_ref, mixed_low_ref, normed_ref, gated_ref, d_exp_ref, branch_ref,
    )
    weights_kernel(
        place, cot_ref, mixed_low_ref, normed_ref, gated_ref, d_exp_ref, branch_ref, mine_ref, other_ref
    )


def backward_kernel(
    heads, rows, place, root_ref, shrunk_ref, d_mixed_ref, levels_ref, raised_ref, exact_ref, inverse_rows_ref, query_ref, key_ref, value_ref,
    cos_ref, sine_ref, w_ref, gain_col_ref, unit_turned_ref, own_turned_ref, along_q_ref, length_q_ref,
    along_k_ref, length_k_ref, gain_grad_ref,
    d_query_ref, d_rest_ref, mine_ref, other_ref,
):
    bands, _, keys = raised_ref.shape
    count, edge = keys // 2, REACH * BAND
    width = shrunk_ref.shape[1]
    ones_half = jnp.ones((keys, 128), BF16)
    along_total = jnp.zeros((1, width // 2), F32)
    for band in range(bands):
        span = slice(band * count, (band + 1) * count)
        start = band * keys
        whole = slice(start, start + keys)
        own = slice(start + edge, start + edge + count)
        shrunk = shrunk_ref[span].astype(F32)
        d_mixed = d_mixed_ref[span].astype(F32)
        levels = levels_ref[span].astype(F32)
        lane = lax.broadcasted_iota(jnp.int32, levels.shape, 1)
        value = value_ref[whole, :]
        raised = raised_ref[band]
        parts, stacks = [], []
        for pair in range(heads // 2):
            lanes = slice(128 * pair, 128 * pair + 128)
            stacks.append(pair_lanes(shrunk, heads, pair))
            terms = jnp.concatenate(
                [jnp.where(lane % heads == h, -levels, 0.0) for h in (2 * pair, 2 * pair + 1)], axis=0
            ).astype(BF16)
            parts.append(
                mm_rt(
                    jnp.concatenate([pair_lanes(d_mixed, heads, pair), terms], axis=1),
                    jnp.concatenate([value[:, lanes], ones_half], axis=1),
                )
            )
        query = stack_heads(query_ref[span, :].astype(F32), heads)
        inverse = jnp.concatenate([inverse_rows_ref[band]] * (keys // 128), axis=1)
        probs = jnp.where(raised > 0, exact_ref[band] * inverse, 0.0)
        d_scores = (probs * jnp.concatenate(parts, axis=0)).astype(BF16)
        d_key = mm_lt(d_scores, query)
        d_query = fold_heads(mm(d_scores, key_ref[whole, :]), heads)
        for pair in range(heads // 2):
            lanes = slice(width + 128 * pair, width + 128 * pair + 128)
            d_value = mm_lt(raised[2 * pair * count : 2 * (pair + 1) * count], stacks[pair])
            d_rest_ref[whole, lanes] = d_value.astype(BF16)
        d_rest_ref[whole, :width], along_k = pull_head(
            d_key, along_k_ref[whole, :], length_k_ref[whole, :], cos_ref[whole, :], sine_ref[whole, :], heads
        )
        d_query_ref[span, :], along_q = pull_head(
            d_query, along_q_ref[span, :], length_q_ref[span, :], cos_ref[own, :], sine_ref[own, :], heads
        )
        along_total = along_total + along_k + along_q
    plain = jnp.concatenate(
        [mm(own_turned_ref[...], d_query_ref[...]), mm(unit_turned_ref[...], d_rest_ref[...])], axis=1
    )
    scaled = plain * jnp.concatenate([gain_col_ref[...]] * (3 * width // 128), axis=1)
    turned = jnp.concatenate([scaled[:, :width], scaled[:, width : 2 * width]], axis=0).astype(BF16)
    plain_order = mm_rt(turned, turned_order(width, heads))
    split_parts(place, plain_order[:width], mine_ref, other_ref, 0)
    split_parts(place, plain_order[width:], mine_ref, other_ref, width)
    split_parts(place, scaled[:, 2 * width :], mine_ref, other_ref, 2 * width)
    lines = []
    for total in (lane_sums(plain * w_ref[...].astype(F32)), gain_grad_ref[...]):
        lines += [total[:, :128], total[:, 128:]]
    total = along_total * 0.5 / root_ref[...]
    high = total.astype(BF16).astype(F32)
    lines += [high, total - high, jnp.zeros((2, 128), F32)]
    tail = jnp.concatenate(lines, axis=0).astype(BF16)
    for ref in (mine_ref, other_ref):
        ref[:, :, :, 3 * width :] = jnp.broadcast_to(tail[None, None], ref.shape[:2] + tail.shape)


def call(kernel, outs, scratch=(), place=None, smem=0, smem_out=0, flops=10**9, pin=True, aliases=None):
    if place is not None:
        kernel = functools.partial(kernel, place)

    def run(*args):
        args = [
            arg if i < smem else pltpu.with_memory_space_constraint(arg, pltpu.VMEM if pin else pltpu.HBM)
            for i, arg in enumerate(args)
        ]
        return pl.pallas_call(
            kernel,
            out_shape=outs,
            in_specs=[
                pl.BlockSpec(memory_space=pltpu.SMEM if i < smem else pltpu.VMEM)
                for i in range(len(args))
            ],
            out_specs=[
                pl.BlockSpec(memory_space=pltpu.SMEM if i >= len(outs) - smem_out else pltpu.VMEM)
                for i in range(len(outs))
            ],
            scratch_shapes=list(scratch),
            input_output_aliases=aliases or {},
            compiler_params=pltpu.CompilerParams(vmem_limit_bytes=VMEM_LIMIT),
            cost_estimate=pl.CostEstimate(flops=flops, bytes_accessed=4 * 10**6 if flops > 1 else 1, transcendentals=0),
        )(*args)

    return run


def rotation_tables(row_place, col_place, heads, size):
    part = size // 8
    lane = jnp.arange(heads * size // 2) % (size // 2)
    index = (lane % part).astype(F32)
    frequency = math.pi / 8.0 * jnp.exp(index * (-math.log(10.0) / part))
    group = lane // part

    def table(place, kind):
        angle = place.astype(F32)[:, None] * frequency
        cos = jnp.where(group == kind, jnp.cos(angle), 0.0)
        if kind:
            cos = jnp.where(group >= 2, 1.0, cos)
        return jnp.stack([cos, jnp.where(group == kind, jnp.sin(angle), 0.0)])

    return table(row_place, 0), table(col_place, 1)


def window_ids(crop_ids, row_start, rows):
    ids = jnp.pad(crop_ids[:, ::BAND], ((REACH, 2 * rows), (0, 0)), constant_values=-1)
    ids = lax.dynamic_slice_in_dim(ids, row_start, 2 * rows, 0)
    return jnp.repeat(ids, BAND, axis=0), jnp.repeat(ids.T, BAND, axis=1)


def on_device(
    features, crop_ids, conditioning, qkv_weight, out_weight, up_weight, down_weight,
    attn_cond_weight, feed_cond_weight, attention_scale, cotangent,
):
    rows, cols, width = features.shape
    heads = attention_scale.shape[0]
    size = width // heads
    bands = cols // BAND
    count = rows * BAND
    tokens = rows * cols
    edge = REACH * BAND
    n_rows, n_cols = lax.axis_size("rows"), lax.axis_size("cols")
    devices = n_rows * n_cols
    hidden = down_weight.shape[0] * devices
    own_cond = attn_cond_weight.shape[0]
    canvases = conditioning.shape[0]
    row, col = lax.axis_index("rows"), lax.axis_index("cols")
    row_start, col_start = row * rows, col * cols
    canvas = col_start // CANVAS
    group, chips = 4, 4
    chunks = 2 * chips * group
    direct = (n_rows, n_cols) == (2 * chips, group) and chunks * 8 == width
    first_lanes = 3 * width + 128
    second_lanes = 2 * hidden + width + hidden * width // (8 * chunks)
    per_canvas = max(n_cols // canvases, 1)
    place = Place(direct, cols, n_cols)

    def result(*dims, dtype=F32):
        return jax.ShapeDtypeStruct(dims, dtype)

    def shape(*dims, dtype=F32):
        return pltpu.VMEM(dims, dtype)

    def low(*dims):
        return shape(*dims, dtype=BF16)

    def over(axis, by):
        size_of = lax.axis_size(axis)
        return lambda value: lax.ppermute(value, axis, [(i, i ^ by) for i in range(size_of)])

    z_moves = [over("cols", k) for k in range(1, group)]
    xy_moves = [over("rows", 2 * m) for m in range(1, chips)]

    def chip_pairs(step):
        return [(i, i ^ (4 if i % 2 == step else 2)) for i in range(n_rows)]

    def first_chip(value):
        return lax.ppermute(value, "rows", chip_pairs(0))

    def second_chip(value):
        return lax.ppermute(value, "rows", chip_pairs(1))

    core_move = over("rows", 1)

    if direct:
        near, far, both, cond_own = call(
            functools.partial(pack_kernel, heads, per_canvas),
            [
                low(8, first_lanes + second_lanes),
                low(8, first_lanes + second_lanes),
                low(8, first_lanes + second_lanes + 128),
                shape(own_cond, canvases),
            ],
            place=place,
            pin=False,
        )(conditioning, qkv_weight, up_weight, out_weight, down_weight, attn_cond_weight, feed_cond_weight)
        z_order = (3, 1, 2)

        def gather_line(near, far):
            return call(
                functools.partial(line_kernel, z_order), [low(group, 8, first_lanes + second_lanes)], place=place
            )(near, *[z_moves[k - 1](near if k // per_canvas == 0 else far) for k in z_order])[0]

        both = xy_moves[2](both)
        line = gather_line(near, far)
        across = gather_line(
            *call(
                functools.partial(again_kernel, 3 * width),
                [low(8, first_lanes + second_lanes), low(8, first_lanes + second_lanes)],
            )(both)
        )
        mine = [line, xy_moves[0](line), xy_moves[1](line), across]
    else:
        def parts_of(full):
            full = full.reshape(chips, 2, group, 8, full.shape[-1])
            return [full[m, core] for core in range(2) for m in range(chips)]

        def whole(weight):
            return lax.all_gather(weight, AXES, axis=0, tiled=True)

        cond = lax.dynamic_slice_in_dim(conditioning, place[4] * own_cond, own_cond, 1)
        cond_own = cond.T.astype(F32)
        sums = [
            lax.psum(jnp.dot(cond, weight, preferred_element_type=F32), AXES)
            for weight in (attn_cond_weight, feed_cond_weight)
        ]
        lines = []
        for part in sums:
            part = lax.dynamic_slice_in_dim(part, canvas, 1, 0).reshape(-1, 128)
            high = lax.reduce_precision(part, 8, 7)
            lines += [high, part - high]
        lines = jnp.pad(jnp.concatenate(lines).astype(BF16), ((0, width - 8), (0, 0)))
        qkv = whole(qkv_weight)
        turned = jnp.argmax(turned_order(width, heads), axis=0)
        qkv = jnp.concatenate([qkv[:, :width][:, turned], qkv[:, width : 2 * width][:, turned], qkv[:, 2 * width :]], axis=1)
        down = whole(down_weight).reshape(chunks, -1, 8, width).transpose(0, 2, 1, 3).reshape(width, -1)
        parts = parts_of(
            jnp.concatenate([qkv, lines, whole(up_weight), whole(out_weight), down], axis=1)
        )

    odd = row % 2 == 1
    beside_pairs = [(i, (i + 1 if i % 2 else i - 1) % n_rows) for i in range(n_rows)]

    def beside_move(value):
        return lax.ppermute(value, "rows", beside_pairs)

    first_rows, last_rows = features[:REACH], features[rows - REACH :]
    halo_swap = core_move(jnp.where(odd, first_rows, last_rows))
    halo_beside = beside_move(jnp.where(odd, last_rows, first_rows))

    row_place = row_start - REACH + jnp.arange(2 * rows, dtype=jnp.int32)
    col_place = (col_start + jnp.arange(cols, dtype=jnp.int32)) % CANVAS
    row_table, col_table = rotation_tables(row_place, col_place, heads, size)
    id_query, id_key = window_ids(crop_ids, row_start, rows)

    unit, unit_turned, own_turned, cos, sine, mask, inputs, cot, root = call(
        functools.partial(ready_kernel, heads),
        [
            shape(2 * tokens, width),
            low(width, 2 * tokens),
            low(width, tokens),
            shape(2 * tokens, width // 2),
            shape(2 * tokens, width // 2),
            low(bands, count, 2 * count),
            shape(tokens, width),
            low(tokens, width),
            shape(1, width // 2),
        ],
        place=place,
        smem=1,
    )(attention_scale, features, cotangent, halo_swap, halo_beside, row_table, col_table, id_query, id_key)
    if direct:
        mine = mine[:1] + [lax.optimization_barrier((part, unit))[0] for part in mine[1:]]
        parts = mine + [core_move(part) for part in mine]

    (
        query, key, value, raised, exact, inverse_rows, mixed, along_q, length_q, along_k, length_k, gain, gain_col, w_qkv,
        middle, middle_grad, shrunk, d_mixed, levels, gain_grad, w_down, gated, mine_second, other_second,
    ) = call(
        functools.partial(forward_kernel, heads),
        [
            low(tokens, width),
            low(2 * tokens, width),
            low(2 * tokens, width),
            low(bands, heads * count, 2 * count),
            shape(bands, heads * count, 2 * count),
            shape(bands, heads * count, 128),
            shape(tokens, width),
            shape(tokens, width),
            shape(tokens, width // 2),
            shape(2 * tokens, width),
            shape(2 * tokens, width // 2),
            shape(2, width),
            shape(width, 128),
            low(width, 3 * width),
            shape(tokens, width),
            shape(tokens, width),
            low(tokens, width),
            low(tokens, width),
            low(tokens, 128),
            shape(1, width),
            low(hidden, width),
            low(tokens, hidden),
            low(chips, group, 8, second_lanes),
            low(chips, group, 8, second_lanes),
        ],
        scratch=[
            pltpu.VMEM((tokens, width), F32),
            pltpu.VMEM((width, 2 * hidden), BF16),
            pltpu.VMEM((width, width), BF16),
            pltpu.VMEM((tokens, width), BF16),
            pltpu.VMEM((tokens, width), BF16),
            pltpu.VMEM((tokens, 2 * hidden), BF16),
            pltpu.VMEM((tokens, width), BF16),
        ],
        place=place,
    )(root, unit, cos, sine, mask, inputs, cot, *parts)

    d_query, d_rest, mine_first, other_first = call(
        functools.partial(backward_kernel, heads, rows),
        [
            low(tokens, width),
            low(2 * tokens, 2 * width),
            low(chips, group, 8, first_lanes),
            low(chips, group, 8, first_lanes),
        ],
        place=place,
        flops=1,
    )(
        root, shrunk, d_mixed, levels, raised, exact, inverse_rows, query, key, value, cos, sine, w_qkv, gain_col, unit_turned, own_turned,
        along_q, length_q, along_k, length_k, gain_grad,
    )

    def last_output(gated):
        return call(output_kernel, [result(rows, cols, width, dtype=BF16)])(middle, gated, w_down)[0]

    def normed_back(d_query, d_rest):
        return call(
            functools.partial(normed_back_kernel, rows),
            [shape(tokens, width), low(bands * edge, width), low(bands * edge, width)],
            place=place,
        )(w_qkv, d_query, d_rest)

    def last_features(own, rim_swap, rim_beside):
        return call(features_kernel, [result(rows, cols, width)], place=place)(
            inputs, gain, own, rim_swap, rim_beside, middle_grad
        )[0]

    if direct:
        all_lanes = second_lanes + first_lanes
        def core_sum(carry, mine, got):
            return call(functools.partial(core_sum_kernel, carry), [low(group, 8, mine.shape[-1]) for _ in range(chips)], place=place)(mine, got)

        def pair_sum(carry, one, two):
            return call(functools.partial(pair_sum_kernel, carry), [low(*one.shape)], flops=1)(one, two)[0]

        first_got = core_move(other_first)
        second_own, second_near, second_beside, second_far = core_sum(False, mine_second, core_move(other_second))
        second_far = second_chip(second_far)
        first_own, first_near, first_beside, first_far = core_sum(True, mine_first, first_got)
        first_far = second_chip(first_far)
        second_far, first_far = lax.optimization_barrier((second_far, first_far))
        first_own, d_rest = lax.optimization_barrier((first_own, d_rest))
        beside = second_chip(call(join_kernel, [low(group, 8, all_lanes)], flops=1)(second_beside, first_beside)[0])
        sums = [
            second_own,
            first_chip(pair_sum(False, second_near, second_far)),
            first_own,
            first_chip(pair_sum(True, first_near, first_far)),
            beside,
        ]
        own_grad, rim_swap, rim_beside = normed_back(d_query, d_rest)
        rim_swap, rim_beside = core_move(rim_swap), beside_move(rim_beside)
        blocks = call(
            chip_sum_kernel,
            [shape(8, all_lanes)] + [low(8, all_lanes) for _ in z_moves],
            scratch=[pltpu.VMEM((group, 8, all_lanes), F32)],
            place=place,
        )(*sums)
        blocks, gated, own_grad = lax.optimization_barrier((blocks, gated, own_grad))
        output = last_output(gated)
        grad_features = last_features(own_grad, rim_swap, rim_beside)
        grad_qkv, grad_out, grad_up, grad_down, grad_attn_cond, grad_feed_cond, grad_scale = call(
            functools.partial(last_kernel, per_canvas, size // 2),
            [
                result(8, 3 * width),
                result(8, width),
                result(8, 2 * hidden),
                result(hidden // chunks, width),
                result(own_cond, width),
                result(own_cond, width),
                result(heads),
            ],
            place=place,
            smem_out=1,
        )(cond_own, blocks[0], *[move(block) for move, block in reversed(list(zip(z_moves, blocks[1:])))])
    else:
        own_grad, rim_swap, rim_beside = normed_back(d_query, d_rest)
        grad_features = last_features(own_grad, core_move(rim_swap), beside_move(rim_beside))
        output = last_output(gated)

        def joined(mine, other):
            return jnp.stack([mine, other], axis=1).astype(F32).reshape(chunks, 8, mine.shape[-1])

        def scattered(grad):
            return lax.psum_scatter(grad.reshape(-1, grad.shape[-1]), AXES, scatter_dimension=0, tiled=True)

        last = joined(mine_first, other_first)
        second = joined(mine_second, other_second)
        ups = 2 * hidden
        grad_qkv = scattered(last[:, :, : 3 * width])
        grad_up = scattered(second[:, :, :ups])
        grad_out = scattered(second[:, :, ups : ups + width])
        grad_down = scattered(
            second[:, :, ups + width :].reshape(chunks, 8, -1, width).transpose(0, 2, 1, 3)
        )
        spot = (jnp.arange(canvases) == canvas).astype(F32)[:, None, None]
        tail = lax.psum(spot * last[0, :, 3 * width :][None], AXES)

        def cond_grad(sums):
            return jnp.sum(cond_own[:, :, None] * sums.reshape(canvases, width)[None], axis=1)

        grad_attn_cond = cond_grad(tail[:, 0:2])
        grad_feed_cond = cond_grad(tail[:, 2:4])
        grad_scale = jnp.sum(tail[:, 4] + tail[:, 5], axis=0)[:: size // 2]
    return (
        output, grad_features, grad_qkv, grad_out, grad_up, grad_down, grad_attn_cond, grad_feed_cond, grad_scale,
    )


def solution(mesh):
    tile, whole, split = P("rows", "cols", None), P(), P(AXES, None)
    return jax.shard_map(
        on_device,
        mesh=mesh,
        in_specs=(tile, P(None, "cols"), whole, split, split, split, split, split, split, whole, tile),
        out_specs=(tile, tile, split, split, split, split, split, split, whole),
        check_vma=False,
    )
```

```python
import functools
import math

import jax
import jax.numpy as jnp
from jax import lax
from jax.experimental import pallas as pl
from jax.experimental.pallas import tpu as pltpu
from jax.sharding import PartitionSpec as P

CANVAS = 128
BAND = 16
REACH = 3
AXES = ("rows", "cols")
F32 = jnp.float32
BF16 = jnp.bfloat16
EPS = 1e-06
VMEM_LIMIT = 32 * 1024 * 1024


class Place:
    def __init__(self, direct, cols, n_cols):
        self.direct, self.cols, self.n_cols = direct, cols, n_cols

    def __getitem__(self, item):
        row, col = lax.axis_index("rows"), lax.axis_index("cols")
        if item == 0:
            return col * self.cols // CANVAS
        if item == 4:
            return row * self.n_cols + col
        if item == 5:
            return lax.rem(row, 2)
        if not self.direct:
            return (0, 0, 0, 0, 0, 0, 1)[item]
        return (None, row // 2, lax.rem(row, 2), col, None, None, 2 - lax.rem(row, 2))[item]


def mm(left, right):
    return lax.dot_general(left, right, (((1,), (0,)), ((), ())), preferred_element_type=F32)


def mm_rt(left, right):
    return lax.dot_general(left, right, (((1,), (1,)), ((), ())), preferred_element_type=F32)


def mm_lt(left, right):
    return lax.dot_general(left, right, (((0,), (0,)), ((), ())), preferred_element_type=F32)


def same_head(width, size):
    first = lax.broadcasted_iota(jnp.int32, (width, width), 0) // size
    second = lax.broadcasted_iota(jnp.int32, (width, width), 1) // size
    return jnp.where(first == second, 1.0, 0.0).astype(BF16)


def stack_heads(values, heads):
    lane = head_of(values.shape, heads)
    return jnp.concatenate(
        [jnp.where(lane == h, values, 0.0).astype(BF16) for h in range(heads)], axis=0
    )


def fold_heads(values, heads):
    count = values.shape[0] // heads
    lane = head_of((count, values.shape[1]), heads)
    total = values[:count]
    for h in range(1, heads):
        total = jnp.where(lane == h, values[h * count : (h + 1) * count], total)
    return total


def turned_order(width, heads):
    size = width // heads
    part = size // 8
    row = lax.broadcasted_iota(jnp.int32, (width, width), 0)
    col = lax.broadcasted_iota(jnp.int32, (width, width), 1)
    half, lane = col // (width // 2), col % (width // 2)
    head, j = lane // (size // 2), lane % (size // 2)
    rotated = j // part * 2 * part + j % part + half * part
    kept = 4 * part + j - 2 * part + half * 2 * part
    return jnp.where(row == head * size + jnp.where(j < 2 * part, rotated, kept), 1.0, 0.0).astype(BF16)


def halves(values):
    half = values.shape[1] // 2
    return values[:, :half], values[:, half:]


def head_of(shape, heads):
    half = shape[1] // 2
    return lax.broadcasted_iota(jnp.int32, shape, 1) % half // (half // heads)


def own_rows(values, count):
    edge = REACH * BAND
    return jnp.concatenate(
        [values[start + edge : start + edge + count] for start in range(0, values.shape[0], 2 * count)], axis=0
    )


def bands_of(ref, bands):
    parts = [
        ref[:, band * BAND : (band + 1) * BAND, :].astype(F32).reshape(-1, ref.shape[-1])
        for band in range(bands)
    ]
    return jnp.concatenate(parts, axis=0)


def pair_lanes(values, heads, pair):
    size = values.shape[1] // heads
    part = values[:, 128 * pair : 128 * pair + 128]
    lane = lax.broadcasted_iota(jnp.int32, part.shape, 1)
    return jnp.concatenate(
        [jnp.where(lane < size, part, 0.0), jnp.where(lane < size, 0.0, part)], axis=0
    ).astype(BF16)


def merge_pair(values, size):
    count = values.shape[0] // 2
    lane = lax.broadcasted_iota(jnp.int32, (count, 128), 1)
    return jnp.where(lane < size, values[:count], values[count:])


def close(shape, query_row, key_row):
    token = lax.broadcasted_iota(jnp.int32, shape, 0)
    place = lax.broadcasted_iota(jnp.int32, shape, 1)
    return (jnp.abs(token // BAND + query_row - place // BAND - key_row) <= REACH) & (
        jnp.abs(token % BAND - place % BAND) <= REACH
    )


def norm_scale(values):
    return lax.rsqrt(jnp.mean(values * values, axis=-1, keepdims=True) + EPS)


def place_parts(place, part_refs):
    for index, part in enumerate(part_refs):
        chip = place[1] ^ (index % 4)
        core = place[2] ^ (index // 4)
        group = part.shape[0]
        yield (chip * 2 + core) * group, part[...].astype(F32)


def store_rows(ref, start, rows):
    group, count, lanes = rows.shape
    ref[pl.ds(pl.multiple_of(start * count, group * count), group * count), :] = rows.reshape(
        group * count, lanes
    ).astype(ref.dtype)


def split_parts(place, values, mine_ref, other_ref, start):
    chips, group = mine_ref.shape[:2]
    count = values.shape[0] // (2 * chips)
    first = place[2] == 0
    for chip in range(chips):
        zero, one = [values[(2 * chip + core) * count : (2 * chip + core + 1) * count] for core in range(2)]
        for ref, part in ((mine_ref, jnp.where(first, zero, one)), (other_ref, jnp.where(first, one, zero))):
            part = part.reshape(group, count // group, values.shape[1])
            for i in range(count // group // 8):
                at = start + i * values.shape[1]
                ref[chip, :, :, at : at + values.shape[1]] = part[:, 8 * i : 8 * i + 8].astype(BF16)


def pack_kernel(
    heads, per_canvas, place, cond_ref, qkv_ref, up_ref, out_ref, down_ref, attn_ref, feed_ref,
    near_ref, far_ref, both_ref, cond_own_ref,
):
    own = attn_ref.shape[0]
    canvases, total = cond_ref.shape
    width = out_ref.shape[1]
    row = lax.broadcasted_iota(jnp.int32, (own, total), 0) + place[4] * own
    pick = jnp.where(row == lax.broadcasted_iota(jnp.int32, (own, total), 1), 1.0, 0.0).astype(BF16)
    cond = mm_rt(pick, cond_ref[...])
    cond_own_ref[...] = cond
    tails = []
    for canvas in range(canvases):
        lines = []
        for weight_ref in (attn_ref, feed_ref):
            line = jnp.sum(
                cond[:, canvas : canvas + 1] * weight_ref[...].astype(F32), axis=0, keepdims=True
            )
            high = line.astype(BF16).astype(F32)
            for part in (high, line - high):
                lines += [part[:, :128], part[:, 128:]]
        tails.append(jnp.concatenate(lines, axis=0))
    down = down_ref[...].astype(F32)
    parts = [up_ref[...], out_ref[...]] + [down[8 * i : 8 * i + 8].astype(BF16) for i in range(down.shape[0] // 8)]
    qkv = qkv_ref.shape[1]
    turned = mm(
        jnp.concatenate([qkv_ref[:, :width], qkv_ref[:, width : 2 * width]], axis=0).astype(F32).astype(BF16),
        turned_order(width, heads),
    ).astype(BF16)
    mine = place[0] == 0
    near, far = jnp.where(mine, tails[0], tails[1]), jnp.where(mine, tails[1], tails[0])
    both_ref[:, both_ref.shape[1] - 128 :] = far.astype(BF16)
    for ref, tail in ((near_ref, near), (far_ref, far), (both_ref, near)):
        ref[:, :width], ref[:, width : 2 * width] = turned[:8], turned[8:]
        ref[:, 2 * width : qkv] = qkv_ref[:, 2 * width :]
        ref[:, qkv : qkv + 128] = tail.astype(BF16)
        at = qkv + 128
        for part in parts:
            ref[:, at : at + part.shape[1]] = part
            at += part.shape[1]


def again_kernel(at, both_ref, near_ref, far_ref):
    lanes = near_ref.shape[1]
    near_ref[...] = both_ref[:, :lanes]
    far_ref[...] = both_ref[:, :lanes]
    far_ref[:, at : at + 128] = both_ref[:, lanes:]


def line_kernel(order, place, p0, p1, p2, p3, line_ref):
    for index, part in zip((0,) + order, (p0, p1, p2, p3)):
        line_ref[place[3] ^ index] = part[...]


def carried(total):
    tail = total[..., total.shape[-1] - 128 :]
    value = tail[..., 4:5, :] + tail[..., 5:6, :]
    high = value.astype(BF16).astype(F32)
    row = lax.broadcasted_iota(jnp.int32, tail.shape, tail.ndim - 2)
    tail = jnp.where(row == 4, high, jnp.where(row == 5, value - high, tail))
    return jnp.concatenate([total[..., : total.shape[-1] - 128], tail], axis=-1)


def core_sum_kernel(carry, place, mine_ref, got_ref, *outs):
    for index, out_ref in enumerate(outs):
        chip = place[1] ^ (0, place[6], place[6] ^ 3, 3)[index]
        total = mine_ref[chip].astype(F32) + got_ref[chip].astype(F32)
        out_ref[...] = (carried(total) if carry else total).astype(BF16)


def join_kernel(one_ref, two_ref, out_ref):
    split = one_ref.shape[-1]
    out_ref[:, :, :split] = one_ref[...]
    out_ref[:, :, split:] = two_ref[...]


def pair_sum_kernel(carry, one_ref, two_ref, out_ref):
    total = one_ref[...].astype(F32) + two_ref[...].astype(F32)
    out_ref[...] = (carried(total) if carry else total).astype(BF16)


def chip_sum_kernel(place, p0, p1, q0, q1, both, o0, o1, o2, o3, keep_ref):
    split = p0.shape[-1]
    keep_ref[:, :, :split] = p0[...].astype(F32) + p1[...].astype(F32) + both[:, :, :split].astype(F32)
    keep_ref[:, :, split:] = carried(
        q0[...].astype(F32) + q1[...].astype(F32) + both[:, :, split:].astype(F32)
    )
    for index, out_ref in enumerate((o0, o1, o2, o3)):
        out_ref[...] = keep_ref[place[3] ^ index].astype(out_ref.dtype)


def last_kernel(
    per_canvas, size, place, cond_ref, own_ref, three_ref, two_ref, one_ref,
    qkv_ref, out_ref, up_ref, down_ref, attn_ref, feed_ref, scale_ref,
):
    parts = [own_ref[...]] + [ref[...].astype(F32) for ref in (one_ref, two_ref, three_ref)]
    total = parts[0] + parts[1] + parts[2] + parts[3]
    width = out_ref.shape[1]
    at = up_ref.shape[1]
    up_ref[...] = total[:, :at]
    out_ref[...] = total[:, at : at + width]
    for i in range(down_ref.shape[0] // 8):
        at += width
        down_ref[8 * i : 8 * i + 8, :] = total[:, at : at + width]
    at += width
    qkv_ref[...] = total[:, at : at + qkv_ref.shape[1]]
    at += qkv_ref.shape[1]
    cond = cond_ref[...]
    attn, feed = 0.0, 0.0
    for canvas in range(cond.shape[1]):
        tail = jnp.zeros((8, 128), F32)
        for index, part in enumerate(parts):
            same = (place[3] ^ index) // per_canvas == canvas
            tail = tail + jnp.where(same, part[:, at:], 0.0)
        weight = cond[:, canvas : canvas + 1]
        attn = attn + weight * jnp.concatenate([tail[0:1], tail[1:2]], axis=1)
        feed = feed + weight * jnp.concatenate([tail[2:3], tail[3:4]], axis=1)
    attn_ref[...] = attn
    feed_ref[...] = feed
    tail = total[:, at:]
    scale = tail[4:5] + tail[5:6]
    for h in range(scale_ref.shape[0]):
        scale_ref[h] = scale[0, h * size]


def ready_kernel(
    heads, place, scale_ref, feat_ref, cot_ref, swap_ref, beside_ref, row_ref, col_ref, id_query_ref, id_key_ref,
    unit_ref, unit_turned_ref, own_turned_ref, cos_ref, sine_ref, mask_ref, inputs_ref, cot_out_ref, root_ref,
):
    rows, cols, width = feat_ref.shape
    count = rows * BAND
    bands = cols // BAND
    odd = place[5] == 1
    near = close((count, 2 * count), REACH, 0)
    lane = lax.broadcasted_iota(jnp.int32, (1, width // 2), 1) // (width // 2 // heads)
    root = jnp.zeros((1, width // 2), F32)
    for h in range(heads):
        root = jnp.where(lane == h, scale_ref[h], root)
    root_ref[...] = jnp.sqrt(root)
    inputs_ref[...] = bands_of(feat_ref, bands)
    cot_out_ref[...] = bands_of(cot_ref, bands).astype(BF16)
    for band in range(bands):
        part = slice(band * BAND, (band + 1) * BAND)
        swapped = swap_ref[:, part, :].astype(F32)
        beside = beside_ref[:, part, :].astype(F32)
        full = jnp.concatenate(
            [
                jnp.where(odd, swapped, beside),
                feat_ref[:, part, :].astype(F32),
                jnp.where(odd, beside, swapped),
                jnp.zeros((2, BAND, width), F32),
            ],
            axis=0,
        ).reshape(2 * count, width)
        span = slice(2 * band * count, 2 * (band + 1) * count)
        unit = full * norm_scale(full)
        unit_ref[span] = unit
        turned = jnp.transpose(unit).astype(BF16)
        unit_turned_ref[:, span] = turned
        own = slice(REACH * BAND, REACH * BAND + count)
        own_turned_ref[:, band * count : (band + 1) * count] = jnp.transpose(unit[own]).astype(BF16)
        for i, ref in enumerate((cos_ref, sine_ref)):
            ref[span] = (row_ref[i][:, None, :] + col_ref[i, part, :][None]).reshape(2 * count, width // 2)
        alike = id_query_ref[REACH * BAND : REACH * BAND + count, band : band + 1] == id_key_ref[
            band : band + 1, :
        ]
        mask_ref[band] = jnp.where(near & alike, 1.0, 0.0).astype(BF16)


def attend_kernel(
    heads, root_ref, unit_ref, cos_ref, sine_ref, mask_ref, sums, w_ref,
    query_ref, key_ref, value_ref, raised_ref, exact_ref, mixed_ref, inverse_ref, inverse_rows_ref, along_q_ref, length_q_ref, along_k_ref, length_k_ref,
    gain_ref, gain_col_ref,
):
    bands, count = mask_ref.shape[:2]
    width = unit_ref.shape[1]
    size = width // heads
    weight = w_ref[...]
    pairs = [sums[i : i + 2] + sums[i + 2 : i + 4] for i in (0, 4)]
    picked = 1.0 + jnp.concatenate(
        [jnp.concatenate([pair[0:1], pair[1:2]], axis=1) for pair in pairs], axis=0
    )
    gain_ref[...] = picked
    gain_col_ref[...] = jnp.transpose(jnp.broadcast_to(picked[0:1], (128, width)))
    root = root_ref[...]
    unit = unit_ref[...]
    normed = (unit * picked[0:1]).astype(BF16)
    value_ref[...] = mm(normed, weight[:, 2 * width :]).astype(BF16)
    ones_head = same_head(width // 2, size // 2)
    cos, sine = cos_ref[...], sine_ref[...]
    own = [own_rows(part, count) for part in (normed, cos, sine)]
    for i, (ref, along_ref, length_ref, (rows, cos, sine)) in enumerate(
        (
            (query_ref, along_q_ref, length_q_ref, own),
            (key_ref, along_k_ref, length_k_ref, (normed, cos, sine)),
        )
    ):
        first, second = halves(mm(rows, weight[:, i * width : (i + 1) * width]))
        short = lax.rsqrt(mm((first * first + second * second).astype(BF16), ones_head) + EPS)
        length = short * root
        ref[...] = jnp.concatenate(
            [(first * cos - second * sine) * length, (second * cos + first * sine) * length], axis=1
        ).astype(BF16)
        along_ref[...] = jnp.concatenate([first * short, second * short], axis=1)
        length_ref[...] = length
    ones_half = jnp.ones((2 * count, 128), BF16)
    for band in range(bands):
        start = 2 * band * count
        span = slice(band * count, (band + 1) * count)
        query = query_ref[span, :].astype(F32)
        scores = mm_rt(stack_heads(query, heads), key_ref[start : start + 2 * count, :])
        exact = jnp.exp(scores) * jnp.concatenate([mask_ref[band].astype(F32)] * heads, axis=0)
        exact_ref[band] = exact
        raised = exact.astype(BF16)
        raised_ref[band] = raised
        value = value_ref[start : start + 2 * count, :]
        for pair in range(heads // 2):
            lanes = slice(128 * pair, 128 * pair + 128)
            both = mm(
                raised[2 * pair * count : 2 * (pair + 1) * count],
                jnp.concatenate([value[:, lanes], ones_half], axis=1),
            )
            rows_inverse = 1.0 / both[:, 128:]
            inverse_rows_ref[band, 2 * pair * count : 2 * (pair + 1) * count, :] = rows_inverse
            inverse = merge_pair(rows_inverse, size)
            mixed_ref[span, lanes] = merge_pair(both[:, :128], size) * inverse
            inverse_ref[span, lanes] = inverse


def feed_kernel(
    heads, inputs_ref, cot_ref, w_up_ref, w_out_ref, gain_ref, mixed_ref, inverse_ref,
    middle_ref, middle_grad_ref, shrunk_ref, d_mixed_ref, levels_ref, gain_grad_ref,
    w_down_ref, mixed_low_ref, normed_ref, gated_ref, d_exp_ref, branch_ref,
):
    width = inputs_ref.shape[1]
    hidden = w_down_ref.shape[0]
    w_up, w_out, w_down = w_up_ref[...], w_out_ref[...], w_down_ref[...]
    gain_feed = gain_ref[1:2]
    mixed = mixed_ref[...]
    mixed_low = mixed.astype(BF16)
    mixed_low_ref[...] = mixed_low
    middle = inputs_ref[...] + mm(mixed_low, w_out)
    middle_ref[...] = middle
    scale = norm_scale(middle)
    unit = middle * scale
    normed = (unit * gain_feed).astype(BF16)
    normed_ref[...] = normed
    cot = cot_ref[...].astype(F32)
    half = math.sqrt(0.5)
    density = 1.0 / math.sqrt(2.0 * math.pi)
    pulled = None
    for start in range(0, hidden, width):
        here = slice(start, start + width)
        there = slice(hidden + start, hidden + start + width)
        left = mm(normed, w_up[:, here])
        gate = mm(normed, w_up[:, there])
        d_gated = mm_rt(cot_ref[...], w_down[here])
        phi = 0.5 + 0.5 * lax.erf(gate * half)
        shaped = gate * phi
        gated_ref[:, here] = (left * shaped).astype(BF16)
        slope = phi + gate * (jnp.exp(gate * gate * -0.5) * density)
        d_left = (d_gated * shaped).astype(BF16)
        d_gate = (d_gated * left * slope).astype(BF16)
        d_exp_ref[:, here] = d_left
        d_exp_ref[:, there] = d_gate
        part = mm_rt(d_left, w_up[:, here]) + mm_rt(d_gate, w_up[:, there])
        pulled = part if pulled is None else pulled + part
    gain_grad_ref[...] = jnp.sum(pulled * unit, axis=0, keepdims=True)
    inner = pulled * gain_feed
    d_middle = cot + scale * (inner - unit * jnp.mean(unit * inner, axis=-1, keepdims=True))
    middle_grad_ref[...] = d_middle
    branch = d_middle.astype(BF16)
    branch_ref[...] = branch
    d_mixed = mm_rt(branch, w_out)
    shrunk_ref[...] = (d_mixed * inverse_ref[...]).astype(BF16)
    d_mixed = d_mixed.astype(BF16)
    d_mixed_ref[...] = d_mixed
    level_rows = d_mixed.astype(F32) * mixed
    lane = lax.broadcasted_iota(jnp.int32, (width, 128), 1)
    head = lax.broadcasted_iota(jnp.int32, (width, 128), 0) // (width // heads)
    pick = jnp.where((lane % heads == head) & (lane < 2 * heads), 1.0, 0.0).astype(BF16)
    high = level_rows.astype(BF16)
    levels = mm(high, pick) + mm((level_rows - high.astype(F32)).astype(BF16), pick)
    high = levels.astype(BF16).astype(F32)
    lane = lax.broadcasted_iota(jnp.int32, levels.shape, 1)
    levels_ref[...] = jnp.where(lane < heads, high, levels - high).astype(BF16)


def weights_kernel(place, cot_ref, mixed_low_ref, normed_ref, gated_ref, d_exp_ref, branch_ref, mine_ref, other_ref):
    width, ups = cot_ref.shape[1], d_exp_ref.shape[1]
    split_parts(place, mm_lt(normed_ref[...], d_exp_ref[...]), mine_ref, other_ref, 0)
    split_parts(place, mm_lt(mixed_low_ref[...], branch_ref[...]), mine_ref, other_ref, ups)
    split_parts(place, mm_lt(gated_ref[...], cot_ref[...]), mine_ref, other_ref, ups + width)


def output_kernel(middle_ref, gated_ref, w_down_ref, out_ref):
    rows, cols, width = out_ref.shape
    total = (middle_ref[...] + mm(gated_ref[...], w_down_ref[...])).astype(BF16)
    count = rows * BAND
    for band in range(cols // BAND):
        out_ref[:, band * BAND : (band + 1) * BAND, :] = total[band * count : (band + 1) * count].reshape(
            rows, BAND, width
        )


def pull_head(grad, along, length, cos, sine, heads):
    first, second = halves(grad)
    along_first, along_second = halves(along)
    first, second = first * cos + second * sine, second * cos - first * sine
    ones_head = same_head(first.shape[1], first.shape[1] // heads)
    part = mm((along_first * first + along_second * second).astype(BF16), ones_head)
    grad = jnp.concatenate(
        [length * (first - along_first * part), length * (second - along_second * part)], axis=1
    )
    return grad.astype(BF16), jnp.sum(part, axis=0, keepdims=True)


def lane_sums(product):
    total = product[:, :128]
    for start in range(128, product.shape[1], 128):
        total = total + product[:, start : start + 128]
    return jnp.sum(jnp.transpose(total), axis=0, keepdims=True)


def normed_back_kernel(
    rows, place, w_ref, d_query_ref, d_rest_ref, own_ref, rim_swap_ref, rim_beside_ref
):
    width = own_ref.shape[1]
    count, edge = rows * BAND, REACH * BAND
    odd = place[5] == 1
    whole = mm_rt(d_rest_ref[...], w_ref[:, width:])
    own_ref[...] = mm_rt(d_query_ref[...], w_ref[:, :width]) + own_rows(whole, count)
    for band in range(whole.shape[0] // (2 * count)):
        start = 2 * band * count
        upper, lower = whole[start : start + edge], whole[start + edge + count : start + 2 * edge + count]
        here = slice(band * edge, (band + 1) * edge)
        rim_swap_ref[here] = jnp.where(odd, upper, lower).astype(BF16)
        rim_beside_ref[here] = jnp.where(odd, lower, upper).astype(BF16)


def features_kernel(place, inputs_ref, gain_ref, own_ref, rim_swap_ref, rim_beside_ref, middle_grad_ref, grad_ref):
    rows, cols, width = grad_ref.shape
    bands = cols // BAND
    count, edge = rows * BAND, REACH * BAND
    odd = place[5] == 1
    zeros = jnp.zeros((count - 2 * edge, width), F32)
    rims = []
    for band in range(bands):
        here = slice(band * edge, (band + 1) * edge)
        swapped, beside = rim_swap_ref[here].astype(F32), rim_beside_ref[here].astype(F32)
        rims += [jnp.where(odd, swapped, beside), zeros, jnp.where(odd, beside, swapped)]
    inner = (own_ref[...] + jnp.concatenate(rims, axis=0)) * gain_ref[0:1]
    inputs = inputs_ref[...]
    scale = norm_scale(inputs)
    unit = inputs * scale
    grad = middle_grad_ref[...] + scale * (inner - unit * jnp.mean(unit * inner, axis=-1, keepdims=True))
    for band in range(bands):
        grad_ref[:, band * BAND : (band + 1) * BAND, :] = grad[band * count : (band + 1) * count].reshape(
            rows, BAND, width
        )


def forward_kernel(
    heads, place, root_ref, unit_ref, cos_ref, sine_ref, mask_ref, inputs_ref, cot_ref,
    p0, p1, p2, p3, p4, p5, p6, p7,
    query_ref, key_ref, value_ref, raised_ref, exact_ref, inverse_rows_ref, mixed_ref, along_q_ref, length_q_ref, along_k_ref, length_k_ref,
    gain_ref, gain_col_ref, w_ref, middle_ref, middle_grad_ref, shrunk_ref, d_mixed_ref, levels_ref, gain_grad_ref,
    w_down_ref, gated_ref, mine_ref, other_ref,
    inverse_ref, w_up_ref, w_out_ref, mixed_low_ref, normed_ref, d_exp_ref, branch_ref,
):
    width = inputs_ref.shape[1]
    first, ups = 3 * width + 128, w_up_ref.shape[1]
    sums = jnp.zeros((8, 128), F32)
    for start, rows in place_parts(place, (p0, p1, p2, p3, p4, p5, p6, p7)):
        store_rows(w_ref, start, rows[:, :, : 3 * width])
        sums = sums + jnp.sum(rows[:, :, 3 * width : first], axis=0)
        store_rows(w_up_ref, start, rows[:, :, first : first + ups])
        store_rows(w_out_ref, start, rows[:, :, first + ups : first + ups + width])
        down = [rows[:, :, at : at + width] for at in range(first + ups + width, rows.shape[2], width)]
        store_rows(w_down_ref, start, jnp.concatenate(down, axis=1))
    attend_kernel(
        heads, root_ref, unit_ref, cos_ref, sine_ref, mask_ref, sums, w_ref,
        query_ref, key_ref, value_ref, raised_ref, exact_ref, mixed_ref, inverse_ref, inverse_rows_ref,
        along_q_ref, length_q_ref, along_k_ref, length_k_ref, gain_ref, gain_col_ref,
    )
    feed_kernel(
        heads, inputs_ref, cot_ref, w_up_ref, w_out_ref, gain_ref, mixed_ref, inverse_ref,
        middle_ref, middle_grad_ref, shrunk_ref, d_mixed_ref, levels_ref, gain_grad_ref,
        w_down_ref, mixed_low_ref, normed_ref, gated_ref, d_exp_ref, branch_ref,
    )
    weights_kernel(
        place, cot_ref, mixed_low_ref, normed_ref, gated_ref, d_exp_ref, branch_ref, mine_ref, other_ref
    )


def backward_kernel(
    heads, rows, place, root_ref, shrunk_ref, d_mixed_ref, levels_ref, raised_ref, exact_ref, inverse_rows_ref, query_ref, key_ref, value_ref,
    cos_ref, sine_ref, w_ref, gain_col_ref, unit_turned_ref, own_turned_ref, along_q_ref, length_q_ref,
    along_k_ref, length_k_ref, gain_grad_ref,
    d_query_ref, d_rest_ref, mine_ref, other_ref,
):
    bands, _, keys = raised_ref.shape
    count, edge = keys // 2, REACH * BAND
    width = shrunk_ref.shape[1]
    ones_half = jnp.ones((keys, 128), BF16)
    along_total = jnp.zeros((1, width // 2), F32)
    for band in range(bands):
        span = slice(band * count, (band + 1) * count)
        start = band * keys
        whole = slice(start, start + keys)
        own = slice(start + edge, start + edge + count)
        shrunk = shrunk_ref[span].astype(F32)
        d_mixed = d_mixed_ref[span].astype(F32)
        levels = levels_ref[span].astype(F32)
        lane = lax.broadcasted_iota(jnp.int32, levels.shape, 1)
        value = value_ref[whole, :]
        raised = raised_ref[band]
        parts, stacks = [], []
        for pair in range(heads // 2):
            lanes = slice(128 * pair, 128 * pair + 128)
            stacks.append(pair_lanes(shrunk, heads, pair))
            terms = jnp.concatenate(
                [jnp.where(lane % heads == h, -levels, 0.0) for h in (2 * pair, 2 * pair + 1)], axis=0
            ).astype(BF16)
            parts.append(
                mm_rt(
                    jnp.concatenate([pair_lanes(d_mixed, heads, pair), terms], axis=1),
                    jnp.concatenate([value[:, lanes], ones_half], axis=1),
                )
            )
        query = stack_heads(query_ref[span, :].astype(F32), heads)
        inverse = jnp.concatenate([inverse_rows_ref[band]] * (keys // 128), axis=1)
        probs = exact_ref[band] * inverse
        d_scores = (probs * jnp.concatenate(parts, axis=0)).astype(BF16)
        d_key = mm_lt(d_scores, query)
        d_query = fold_heads(mm(d_scores, key_ref[whole, :]), heads)
        for pair in range(heads // 2):
            lanes = slice(width + 128 * pair, width + 128 * pair + 128)
            d_value = mm_lt(raised[2 * pair * count : 2 * (pair + 1) * count], stacks[pair])
            d_rest_ref[whole, lanes] = d_value.astype(BF16)
        d_rest_ref[whole, :width], along_k = pull_head(
            d_key, along_k_ref[whole, :], length_k_ref[whole, :], cos_ref[whole, :], sine_ref[whole, :], heads
        )
        d_query_ref[span, :], along_q = pull_head(
            d_query, along_q_ref[span, :], length_q_ref[span, :], cos_ref[own, :], sine_ref[own, :], heads
        )
        along_total = along_total + along_k + along_q
    plain = jnp.concatenate(
        [mm(own_turned_ref[...], d_query_ref[...]), mm(unit_turned_ref[...], d_rest_ref[...])], axis=1
    )
    scaled = plain * jnp.concatenate([gain_col_ref[...]] * (3 * width // 128), axis=1)
    turned = jnp.concatenate([scaled[:, :width], scaled[:, width : 2 * width]], axis=0).astype(BF16)
    plain_order = mm_rt(turned, turned_order(width, heads))
    split_parts(place, plain_order[:width], mine_ref, other_ref, 0)
    split_parts(place, plain_order[width:], mine_ref, other_ref, width)
    split_parts(place, scaled[:, 2 * width :], mine_ref, other_ref, 2 * width)
    lines = []
    for total in (lane_sums(plain * w_ref[...].astype(F32)), gain_grad_ref[...]):
        lines += [total[:, :128], total[:, 128:]]
    total = along_total * 0.5 / root_ref[...]
    high = total.astype(BF16).astype(F32)
    lines += [high, total - high, jnp.zeros((2, 128), F32)]
    tail = jnp.concatenate(lines, axis=0).astype(BF16)
    for ref in (mine_ref, other_ref):
        ref[:, :, :, 3 * width :] = jnp.broadcast_to(tail[None, None], ref.shape[:2] + tail.shape)


def call(kernel, outs, scratch=(), place=None, smem=0, smem_out=0, flops=10**9, pin=True, aliases=None):
    if place is not None:
        kernel = functools.partial(kernel, place)

    def run(*args):
        args = [
            arg if i < smem else pltpu.with_memory_space_constraint(arg, pltpu.VMEM if pin else pltpu.HBM)
            for i, arg in enumerate(args)
        ]
        return pl.pallas_call(
            kernel,
            out_shape=outs,
            in_specs=[
                pl.BlockSpec(memory_space=pltpu.SMEM if i < smem else pltpu.VMEM)
                for i in range(len(args))
            ],
            out_specs=[
                pl.BlockSpec(memory_space=pltpu.SMEM if i >= len(outs) - smem_out else pltpu.VMEM)
                for i in range(len(outs))
            ],
            scratch_shapes=list(scratch),
            input_output_aliases=aliases or {},
            compiler_params=pltpu.CompilerParams(vmem_limit_bytes=VMEM_LIMIT),
            cost_estimate=pl.CostEstimate(flops=flops, bytes_accessed=4 * 10**6 if flops > 1 else 1, transcendentals=0),
        )(*args)

    return run


def rotation_tables(row_place, col_place, heads, size):
    part = size // 8
    lane = jnp.arange(heads * size // 2) % (size // 2)
    index = (lane % part).astype(F32)
    frequency = math.pi / 8.0 * jnp.exp(index * (-math.log(10.0) / part))
    group = lane // part

    def table(place, kind):
        angle = place.astype(F32)[:, None] * frequency
        cos = jnp.where(group == kind, jnp.cos(angle), 0.0)
        if kind:
            cos = jnp.where(group >= 2, 1.0, cos)
        return jnp.stack([cos, jnp.where(group == kind, jnp.sin(angle), 0.0)])

    return table(row_place, 0), table(col_place, 1)


def window_ids(crop_ids, row_start, rows):
    ids = jnp.pad(crop_ids[:, ::BAND], ((REACH, 2 * rows), (0, 0)), constant_values=-1)
    ids = lax.dynamic_slice_in_dim(ids, row_start, 2 * rows, 0)
    return jnp.repeat(ids, BAND, axis=0), jnp.repeat(ids.T, BAND, axis=1)


def on_device(
    features, crop_ids, conditioning, qkv_weight, out_weight, up_weight, down_weight,
    attn_cond_weight, feed_cond_weight, attention_scale, cotangent,
):
    rows, cols, width = features.shape
    heads = attention_scale.shape[0]
    size = width // heads
    bands = cols // BAND
    count = rows * BAND
    tokens = rows * cols
    edge = REACH * BAND
    n_rows, n_cols = lax.axis_size("rows"), lax.axis_size("cols")
    devices = n_rows * n_cols
    hidden = down_weight.shape[0] * devices
    own_cond = attn_cond_weight.shape[0]
    canvases = conditioning.shape[0]
    row, col = lax.axis_index("rows"), lax.axis_index("cols")
    row_start, col_start = row * rows, col * cols
    canvas = col_start // CANVAS
    group, chips = 4, 4
    chunks = 2 * chips * group
    direct = (n_rows, n_cols) == (2 * chips, group) and chunks * 8 == width
    first_lanes = 3 * width + 128
    second_lanes = 2 * hidden + width + hidden * width // (8 * chunks)
    per_canvas = max(n_cols // canvases, 1)
    place = Place(direct, cols, n_cols)

    def result(*dims, dtype=F32):
        return jax.ShapeDtypeStruct(dims, dtype)

    def shape(*dims, dtype=F32):
        return pltpu.VMEM(dims, dtype)

    def low(*dims):
        return shape(*dims, dtype=BF16)

    def over(axis, by):
        size_of = lax.axis_size(axis)
        return lambda value: lax.ppermute(value, axis, [(i, i ^ by) for i in range(size_of)])

    z_moves = [over("cols", k) for k in range(1, group)]
    xy_moves = [over("rows", 2 * m) for m in range(1, chips)]

    def chip_pairs(step):
        return [(i, i ^ (4 if i % 2 == step else 2)) for i in range(n_rows)]

    def first_chip(value):
        return lax.ppermute(value, "rows", chip_pairs(0))

    def second_chip(value):
        return lax.ppermute(value, "rows", chip_pairs(1))

    core_move = over("rows", 1)

    if direct:
        near, far, both, cond_own = call(
            functools.partial(pack_kernel, heads, per_canvas),
            [
                low(8, first_lanes + second_lanes),
                low(8, first_lanes + second_lanes),
                low(8, first_lanes + second_lanes + 128),
                shape(own_cond, canvases),
            ],
            place=place,
            pin=False,
        )(conditioning, qkv_weight, up_weight, out_weight, down_weight, attn_cond_weight, feed_cond_weight)
        z_order = (3, 1, 2)

        def gather_line(near, far):
            return call(
                functools.partial(line_kernel, z_order), [low(group, 8, first_lanes + second_lanes)], place=place
            )(near, *[z_moves[k - 1](near if k // per_canvas == 0 else far) for k in z_order])[0]

        both = xy_moves[2](both)
        line = gather_line(near, far)
        across = gather_line(
            *call(
                functools.partial(again_kernel, 3 * width),
                [low(8, first_lanes + second_lanes), low(8, first_lanes + second_lanes)],
            )(both)
        )
        mine = [line, xy_moves[0](line), xy_moves[1](line), across]
    else:
        def parts_of(full):
            full = full.reshape(chips, 2, group, 8, full.shape[-1])
            return [full[m, core] for core in range(2) for m in range(chips)]

        def whole(weight):
            return lax.all_gather(weight, AXES, axis=0, tiled=True)

        cond = lax.dynamic_slice_in_dim(conditioning, place[4] * own_cond, own_cond, 1)
        cond_own = cond.T.astype(F32)
        sums = [
            lax.psum(jnp.dot(cond, weight, preferred_element_type=F32), AXES)
            for weight in (attn_cond_weight, feed_cond_weight)
        ]
        lines = []
        for part in sums:
            part = lax.dynamic_slice_in_dim(part, canvas, 1, 0).reshape(-1, 128)
            high = lax.reduce_precision(part, 8, 7)
            lines += [high, part - high]
        lines = jnp.pad(jnp.concatenate(lines).astype(BF16), ((0, width - 8), (0, 0)))
        qkv = whole(qkv_weight)
        turned = jnp.argmax(turned_order(width, heads), axis=0)
        qkv = jnp.concatenate([qkv[:, :width][:, turned], qkv[:, width : 2 * width][:, turned], qkv[:, 2 * width :]], axis=1)
        down = whole(down_weight).reshape(chunks, -1, 8, width).transpose(0, 2, 1, 3).reshape(width, -1)
        parts = parts_of(
            jnp.concatenate([qkv, lines, whole(up_weight), whole(out_weight), down], axis=1)
        )

    odd = row % 2 == 1
    beside_pairs = [(i, (i + 1 if i % 2 else i - 1) % n_rows) for i in range(n_rows)]

    def beside_move(value):
        return lax.ppermute(value, "rows", beside_pairs)

    first_rows, last_rows = features[:REACH], features[rows - REACH :]
    halo_swap = core_move(jnp.where(odd, first_rows, last_rows))
    halo_beside = beside_move(jnp.where(odd, last_rows, first_rows))

    row_place = row_start - REACH + jnp.arange(2 * rows, dtype=jnp.int32)
    col_place = (col_start + jnp.arange(cols, dtype=jnp.int32)) % CANVAS
    row_table, col_table = rotation_tables(row_place, col_place, heads, size)
    id_query, id_key = window_ids(crop_ids, row_start, rows)

    unit, unit_turned, own_turned, cos, sine, mask, inputs, cot, root = call(
        functools.partial(ready_kernel, heads),
        [
            shape(2 * tokens, width),
            low(width, 2 * tokens),
            low(width, tokens),
            shape(2 * tokens, width // 2),
            shape(2 * tokens, width // 2),
            low(bands, count, 2 * count),
            shape(tokens, width),
            low(tokens, width),
            shape(1, width // 2),
        ],
        place=place,
        smem=1,
    )(attention_scale, features, cotangent, halo_swap, halo_beside, row_table, col_table, id_query, id_key)
    if direct:
        mine = mine[:1] + [lax.optimization_barrier((part, unit))[0] for part in mine[1:]]
        parts = mine + [core_move(part) for part in mine]

    (
        query, key, value, raised, exact, inverse_rows, mixed, along_q, length_q, along_k, length_k, gain, gain_col, w_qkv,
        middle, middle_grad, shrunk, d_mixed, levels, gain_grad, w_down, gated, mine_second, other_second,
    ) = call(
        functools.partial(forward_kernel, heads),
        [
            low(tokens, width),
            low(2 * tokens, width),
            low(2 * tokens, width),
            low(bands, heads * count, 2 * count),
            shape(bands, heads * count, 2 * count),
            shape(bands, heads * count, 128),
            shape(tokens, width),
            shape(tokens, width),
            shape(tokens, width // 2),
            shape(2 * tokens, width),
            shape(2 * tokens, width // 2),
            shape(2, width),
            shape(width, 128),
            low(width, 3 * width),
            shape(tokens, width),
            shape(tokens, width),
            low(tokens, width),
            low(tokens, width),
            low(tokens, 128),
            shape(1, width),
            low(hidden, width),
            low(tokens, hidden),
            low(chips, group, 8, second_lanes),
            low(chips, group, 8, second_lanes),
        ],
        scratch=[
            pltpu.VMEM((tokens, width), F32),
            pltpu.VMEM((width, 2 * hidden), BF16),
            pltpu.VMEM((width, width), BF16),
            pltpu.VMEM((tokens, width), BF16),
            pltpu.VMEM((tokens, width), BF16),
            pltpu.VMEM((tokens, 2 * hidden), BF16),
            pltpu.VMEM((tokens, width), BF16),
        ],
        place=place,
    )(root, unit, cos, sine, mask, inputs, cot, *parts)

    d_query, d_rest, mine_first, other_first = call(
        functools.partial(backward_kernel, heads, rows),
        [
            low(tokens, width),
            low(2 * tokens, 2 * width),
            low(chips, group, 8, first_lanes),
            low(chips, group, 8, first_lanes),
        ],
        place=place,
        flops=1,
    )(
        root, shrunk, d_mixed, levels, raised, exact, inverse_rows, query, key, value, cos, sine, w_qkv, gain_col, unit_turned, own_turned,
        along_q, length_q, along_k, length_k, gain_grad,
    )

    def last_output(gated):
        return call(output_kernel, [result(rows, cols, width, dtype=BF16)])(middle, gated, w_down)[0]

    def normed_back(d_query, d_rest):
        return call(
            functools.partial(normed_back_kernel, rows),
            [shape(tokens, width), low(bands * edge, width), low(bands * edge, width)],
            place=place,
        )(w_qkv, d_query, d_rest)

    def last_features(own, rim_swap, rim_beside):
        return call(features_kernel, [result(rows, cols, width)], place=place)(
            inputs, gain, own, rim_swap, rim_beside, middle_grad
        )[0]

    if direct:
        all_lanes = second_lanes + first_lanes
        def core_sum(carry, mine, got):
            return call(functools.partial(core_sum_kernel, carry), [low(group, 8, mine.shape[-1]) for _ in range(chips)], place=place)(mine, got)

        def pair_sum(carry, one, two):
            return call(functools.partial(pair_sum_kernel, carry), [low(*one.shape)], flops=1)(one, two)[0]

        first_got = core_move(other_first)
        second_own, second_near, second_beside, second_far = core_sum(False, mine_second, core_move(other_second))
        second_far = second_chip(second_far)
        first_own, first_near, first_beside, first_far = core_sum(True, mine_first, first_got)
        first_far = second_chip(first_far)
        second_far, first_far = lax.optimization_barrier((second_far, first_far))
        first_own, d_rest = lax.optimization_barrier((first_own, d_rest))
        beside = second_chip(call(join_kernel, [low(group, 8, all_lanes)], flops=1)(second_beside, first_beside)[0])
        sums = [
            second_own,
            first_chip(pair_sum(False, second_near, second_far)),
            first_own,
            first_chip(pair_sum(True, first_near, first_far)),
            beside,
        ]
        own_grad, rim_swap, rim_beside = normed_back(d_query, d_rest)
        rim_swap, rim_beside = core_move(rim_swap), beside_move(rim_beside)
        blocks = call(
            chip_sum_kernel,
            [shape(8, all_lanes)] + [low(8, all_lanes) for _ in z_moves],
            scratch=[pltpu.VMEM((group, 8, all_lanes), F32)],
            place=place,
        )(*sums)
        blocks, gated, own_grad = lax.optimization_barrier((blocks, gated, own_grad))
        output = last_output(gated)
        grad_features = last_features(own_grad, rim_swap, rim_beside)
        grad_qkv, grad_out, grad_up, grad_down, grad_attn_cond, grad_feed_cond, grad_scale = call(
            functools.partial(last_kernel, per_canvas, size // 2),
            [
                result(8, 3 * width),
                result(8, width),
                result(8, 2 * hidden),
                result(hidden // chunks, width),
                result(own_cond, width),
                result(own_cond, width),
                result(heads),
            ],
            place=place,
            smem_out=1,
        )(cond_own, blocks[0], *[move(block) for move, block in reversed(list(zip(z_moves, blocks[1:])))])
    else:
        own_grad, rim_swap, rim_beside = normed_back(d_query, d_rest)
        grad_features = last_features(own_grad, core_move(rim_swap), beside_move(rim_beside))
        output = last_output(gated)

        def joined(mine, other):
            return jnp.stack([mine, other], axis=1).astype(F32).reshape(chunks, 8, mine.shape[-1])

        def scattered(grad):
            return lax.psum_scatter(grad.reshape(-1, grad.shape[-1]), AXES, scatter_dimension=0, tiled=True)

        last = joined(mine_first, other_first)
        second = joined(mine_second, other_second)
        ups = 2 * hidden
        grad_qkv = scattered(last[:, :, : 3 * width])
        grad_up = scattered(second[:, :, :ups])
        grad_out = scattered(second[:, :, ups : ups + width])
        grad_down = scattered(
            second[:, :, ups + width :].reshape(chunks, 8, -1, width).transpose(0, 2, 1, 3)
        )
        spot = (jnp.arange(canvases) == canvas).astype(F32)[:, None, None]
        tail = lax.psum(spot * last[0, :, 3 * width :][None], AXES)

        def cond_grad(sums):
            return jnp.sum(cond_own[:, :, None] * sums.reshape(canvases, width)[None], axis=1)

        grad_attn_cond = cond_grad(tail[:, 0:2])
        grad_feed_cond = cond_grad(tail[:, 2:4])
        grad_scale = jnp.sum(tail[:, 4] + tail[:, 5], axis=0)[:: size // 2]
    return (
        output, grad_features, grad_qkv, grad_out, grad_up, grad_down, grad_attn_cond, grad_feed_cond, grad_scale,
    )


def solution(mesh):
    tile, whole, split = P("rows", "cols", None), P(), P(AXES, None)
    return jax.shard_map(
        on_device,
        mesh=mesh,
        in_specs=(tile, P(None, "cols"), whole, split, split, split, split, split, split, whole, tile),
        out_specs=(tile, tile, split, split, split, split, split, split, whole),
        check_vma=False,
    )
```
